32 devices in a mesh: grp: 2 (over y), ctx: 8 (over z, x), head: 1, sub: 2 (over core).
Axes of the slice: x: 2, y: 2, z: 4, core: 2. Of those that a mesh axis runs over, the one named last changes fastest.
Arguments:
- queries: bfloat16 [32, 384, 2048], P(('grp', 'ctx', 'sub'), None, 'head'), parts along dimension 0, may hold values from -6 to 6
- keys: bfloat16 [32, 384, 2048], P(('grp', 'ctx', 'sub'), None, 'head'), parts along dimension 0, may hold values from -6 to 6
- values: bfloat16 [32, 384, 2048], P(('grp', 'ctx', 'sub'), None, 'head'), parts along dimension 0, may hold values from -6 to 6
- grad_out: bfloat16 [32, 384, 2048], P(('grp', 'ctx', 'sub'), None, 'head'), parts along dimension 0, may hold values from -6 to 6
- window_tiles: int32 [32, 6], P(('grp', 'ctx', 'sub')), parts along dimension 0, may hold values from 0 to 15, as said below
- window_count: int32 [32], P(('grp', 'ctx', 'sub')), parts along dimension 0, may hold values from 1 to 6
Outputs:
- attended: bfloat16 [32, 384, 2048], P(('grp', 'ctx', 'sub'), None, 'head'), parts along dimension 0
- grad_queries: bfloat16 [32, 384, 2048], P(('grp', 'ctx', 'sub'), None, 'head'), parts along dimension 0
- grad_keys: bfloat16 [32, 384, 2048], P(('grp', 'ctx', 'sub'), None, 'head'), parts along dimension 0
- grad_values: bfloat16 [32, 384, 2048], P(('grp', 'ctx', 'sub'), None, 'head'), parts along dimension 0
The draws below stay inside these ranges and needn't reach their ends.
There are 2 independent parts, one for each index of `grp`. The reference program is written for one: setup_inputs(seed, part) draws one part's arguments, and reference() takes and returns one part's arrays. A program takes and returns all parts, laid end to end along the dimension named above; each array names one. Nothing has to cross between parts.
Inputs may be any that keep to these rules, and one draw needn't show every extreme that they name: `window_tiles`: tile i lies in tile column i // 16, time slab (i // 2) % 8 and tile row i % 2. The first window_count[i] entries of row i are distinct tiles whose column, slab and row each differ from tile i's by at most 1, tile i among them; the other entries equal i. Tile j is a live entry of tile i's list exactly when tile i is a live entry of tile j's list.
All inputs are finite; a program needn't handle non-finite values.
Results may differ from the reference program's by a relative error of at most 0.022.
Values may be sent and summed in bfloat16 or wider, within the bound.
No kernel may reach another device: no remote copies, remote signals or barrier semaphores. Data moves between devices by JAX's collectives and lax.ppermute only.
A program may use at most 256 MiB of HBM per device.

```python
import math
import jax
import jax.numpy as jnp
from jax import lax

HEADS = 16
HD = 128
WIDTH = 2048
TILE = 384
TR = 2
TC = 1
NTT = 8
NTILES = 16
WMAX = 6


def window_lists(key):
    pair_key = jax.random.fold_in(key, 5)
    cut_draw = jax.random.randint(key, (NTT,), 0, 2)
    slab_pos = jnp.arange(NTT)
    kept = (slab_pos == 0) | (slab_pos == NTT // 2) | (slab_pos == NTT // 2 + 1)
    cuts = jnp.where(kept, 0, cut_draw).astype(jnp.int32)
    shot_ids = jnp.cumsum(cuts).astype(jnp.int32)
    tile_ids = jnp.arange(NTILES, dtype=jnp.int32)
    tile_col = tile_ids // (NTT * TR)
    tile_slab = tile_ids // TR % NTT
    tile_row = tile_ids % TR
    step_ids = jnp.arange(27, dtype=jnp.int32)
    slab_steps = step_ids // 9 - 1
    row_steps = step_ids // 3 % 3 - 1
    col_steps = step_ids % 3 - 1
    near_slab = tile_slab[:, None] + slab_steps[None, :]
    near_row = tile_row[:, None] + row_steps[None, :]
    near_col = tile_col[:, None] + col_steps[None, :]
    inside = (near_slab >= 0) & (near_slab < NTT) & (near_row >= 0) & (near_row < TR)
    inside = inside & (near_col >= 0) & (near_col < TC)
    slab_clip = jnp.clip(near_slab, 0, NTT - 1)
    row_clip = jnp.clip(near_row, 0, TR - 1)
    col_clip = jnp.clip(near_col, 0, TC - 1)
    usable = inside & (shot_ids[slab_clip] == shot_ids[tile_slab][:, None])
    candidate = (col_clip * NTT + slab_clip) * TR + row_clip
    coins = jax.random.randint(pair_key, (NTILES, NTILES), 0, 2)
    low_id = jnp.minimum(tile_ids[:, None], candidate)
    high_id = jnp.maximum(tile_ids[:, None], candidate)
    pair_coin = coins[low_id, high_id]
    corner = (slab_steps[None, :] != 0) & (row_steps[None, :] != 0)
    middle_pair = (tile_slab[:, None] == NTT // 2) | (slab_clip == NTT // 2)
    dropped = corner & (pair_coin == 0) & jnp.logical_not(middle_pair)
    usable = usable & jnp.logical_not(dropped)
    ranking = jnp.where(usable, 0, 1) * 32 + step_ids[None, :]
    order_ids = jnp.argsort(ranking, axis=1, stable=True)
    picked = jnp.take_along_axis(candidate, order_ids, axis=1)
    picked_ok = jnp.take_along_axis(usable, order_ids, axis=1)
    listed = jnp.where(picked_ok, picked, tile_ids[:, None])[:, :WMAX]
    counted = jnp.sum(usable.astype(jnp.int32), axis=1)
    return (listed.astype(jnp.int32), counted.astype(jnp.int32))


def draw_window_tiles(key, part):
    listed, counted = window_lists(key)
    return listed


def draw_window_count(key, part):
    listed, counted = window_lists(key)
    return counted


def draw_queries(key, part):
    base_key = key
    key = jax.random.fold_in(base_key, 11)
    field = jnp.clip(jax.random.normal(key, (NTILES, TILE, WIDTH)), -6.0, 6.0)
    return field.astype(jnp.bfloat16)


def draw_keys(key, part):
    base_key = key
    key = jax.random.fold_in(base_key, 23)
    field = jnp.clip(jax.random.normal(key, (NTILES, TILE, WIDTH)), -6.0, 6.0)
    return field.astype(jnp.bfloat16)


def steps_of(rng, shape, cuts, low, largest):
    factor_of, own = 1.0, jax.random.fold_in(rng, 6)
    for position, parts in cuts:
        draws = jnp.exp(jax.random.uniform(jax.random.fold_in(own, position), (parts,), jnp.float32, low / len(cuts), largest / len(cuts)))
        factor_of = factor_of * jnp.repeat(draws, shape[position] // parts).reshape([-1 if axis == position else 1 for axis in range(len(shape))])
    return factor_of


def noise(own_key, extent, spread, limit, pieces=(), kind=jnp.bfloat16):
    gain = steps_of(own_key, extent, pieces, -0.22, 0.18) if pieces else 1.0
    entries = jax.random.normal(own_key, extent, jnp.float32) * spread * gain
    return jnp.minimum(jnp.maximum(entries, -limit), limit).astype(kind)


def setup_inputs(seed: int = 0, part: int = 0) -> dict:
    arg_keys = jax.random.split(jax.random.key(seed), 7)
    own_keys = jax.random.split(jax.random.fold_in(arg_keys[6], part), 7)
    return {
        "queries": draw_queries(jax.random.fold_in(jax.random.fold_in(arg_keys[6], part), 71), part),
        "keys": draw_keys(jax.random.fold_in(jax.random.fold_in(arg_keys[6], part), 71), part),
        "values": noise(own_keys[2], (NTILES, TILE, WIDTH), 1.0, 6.0, ((0, 16),)),
        "grad_out": noise(own_keys[3], (NTILES, TILE, WIDTH), 1.0, 6.0, ((0, 16),)),
        "window_tiles": draw_window_tiles(jax.random.fold_in(jax.random.fold_in(arg_keys[6], part), 71), part),
        "window_count": draw_window_count(jax.random.fold_in(jax.random.fold_in(arg_keys[6], part), 71), part),
    }


def tile_pass(query_tile, grad_tile, key_rows, value_rows, live_slots):
    score_scale = 1.0 / math.sqrt(HD)
    query_heads = query_tile.reshape(TILE, HEADS, HD).astype(jnp.float32)
    grad_heads = grad_tile.reshape(TILE, HEADS, HD).astype(jnp.float32)
    key_heads = key_rows.reshape(WMAX * TILE, HEADS, HD).astype(jnp.float32)
    value_heads = value_rows.reshape(WMAX * TILE, HEADS, HD).astype(jnp.float32)
    live_keys = jnp.repeat(live_slots, TILE)
    scores = jnp.einsum('qhd,khd->hqk', query_heads, key_heads) * score_scale
    scores = jnp.where(live_keys[None, None, :], scores, -jnp.inf)
    row_max = lax.optimization_barrier(jnp.max(scores, axis=2, keepdims=True))
    weights = jnp.exp(scores - row_max)
    weights = weights / lax.optimization_barrier(jnp.sum(weights, axis=2, keepdims=True))
    weights_low = weights.astype(jnp.bfloat16)
    attended = jnp.einsum('hqk,khd->qhd', weights_low.astype(jnp.float32), value_heads).astype(jnp.bfloat16)
    offset = lax.optimization_barrier(jnp.sum(grad_heads * attended.astype(jnp.float32), axis=2))
    offset = jnp.transpose(offset, (1, 0))[:, :, None]
    grad_weights = jnp.einsum('qhd,khd->hqk', grad_heads, value_heads)
    grad_scores = (weights * (grad_weights - offset) * score_scale).astype(jnp.bfloat16)
    grad_query = jnp.einsum('hqk,khd->qhd', grad_scores.astype(jnp.float32), key_heads).astype(jnp.bfloat16)
    grad_key = jnp.einsum('hqk,qhd->khd', grad_scores.astype(jnp.float32), query_heads)
    grad_value = jnp.einsum('hqk,qhd->khd', weights_low.astype(jnp.float32), grad_heads)
    return (attended.reshape(TILE, WIDTH), grad_query.reshape(TILE, WIDTH), grad_key.reshape(WMAX, TILE, WIDTH), grad_value.reshape(WMAX, TILE, WIDTH))

def reference(queries, keys, values, grad_out, window_tiles, window_count):

    def tile_step(sums_carry, tile_item):
        key_sums, value_sums = sums_carry
        query_tile, grad_tile, window_ids, count_now = tile_item
        window_ids = window_ids.astype(jnp.int32)
        live_slots = jnp.arange(WMAX) < count_now
        key_rows = keys[window_ids]
        value_rows = values[window_ids]
        attended, grad_query, grad_key, grad_value = tile_pass(query_tile, grad_tile, key_rows, value_rows, live_slots)
        key_sums = key_sums.at[window_ids].add(grad_key)
        value_sums = value_sums.at[window_ids].add(grad_value)
        return ((key_sums, value_sums), (attended, grad_query))
    empty = jnp.zeros((NTILES, TILE, WIDTH), jnp.float32)
    (key_sums, value_sums), (attended, grad_queries) = lax.scan(tile_step, (empty, empty), (queries, grad_out, window_tiles, window_count))
    return (attended, grad_queries, key_sums.astype(jnp.bfloat16), value_sums.astype(jnp.bfloat16))
```

```python
import functools
import math

import jax
import jax.numpy as jnp
from jax import lax
from jax.experimental import pallas as pl
from jax.experimental.pallas import tpu as pltpu
from jax.sharding import PartitionSpec as P

HD = 128
RING = ("ctx", "sub")
F32 = jnp.float32
BF16 = jnp.bfloat16
SCALE = 1.0 / math.sqrt(HD)
ANY = pl.BlockSpec(memory_space=pl.ANY)
VMEM = pl.BlockSpec(memory_space=pltpu.VMEM)
SMEM = pl.BlockSpec(memory_space=pltpu.SMEM)
VMEM_LIMIT = 48 * 1024 * 1024


def struct(shape, dtype):
    return jax.ShapeDtypeStruct(shape, dtype)


def run_copies(copies, sems):
    started = [pltpu.make_async_copy(src, dst, sems.at[n]) for n, (src, dst) in enumerate(copies)]
    for copy in started:
        copy.start()
    for copy in started:
        copy.wait()


def pack_kernel(team, cols_ref, q_ref, g_ref, k_ref, v_ref, *refs):
    outs, sems = refs[:team], refs[team]
    copies = []
    for d in range(team):
        lanes = pl.ds(pl.multiple_of(cols_ref[d], HD), HD)
        for n, ref in enumerate((q_ref, g_ref, k_ref, v_ref)):
            copies.append((ref.at[0, :, lanes], outs[d].at[n]))
    run_copies(copies, sems)


def pack(team, cols, q, g, k, v):
    tile = q.shape[1]
    return pl.pallas_call(
        functools.partial(pack_kernel, team),
        out_shape=[struct((4, tile, HD), BF16)] * team,
        in_specs=[SMEM] + [ANY] * 4,
        out_specs=[ANY] * team,
        scratch_shapes=[pltpu.SemaphoreType.DMA((4 * team,))],
        cost_estimate=pl.CostEstimate(
            flops=0, bytes_accessed=team * 4 * tile * HD * 4, transcendentals=0
        ),
        name="pack",
    )(cols, q, g, k, v)


def unpack_kernel(team, pieces_per, cols_ref, *refs):
    count = team * pieces_per
    pieces = refs[:count]
    outs = refs[-1 - 2 * pieces_per : -1]
    sems = refs[-1]
    copies = []
    for d in range(team):
        lanes = pl.ds(pl.multiple_of(cols_ref[d], HD), HD)
        for n in range(2 * pieces_per):
            src = pieces[pieces_per * d + n // 2].at[n % 2]
            copies.append((src, outs[n].at[0, :, lanes]))
    run_copies(copies, sems)


def unpack(team, cols, pieces, outs, shape):
    pieces_per = len(pieces[0])
    flat = [piece for row in pieces for piece in row]
    held = [] if outs is None else list(outs)
    tile = shape[1]
    return pl.pallas_call(
        functools.partial(unpack_kernel, team, pieces_per),
        out_shape=[struct(shape, BF16)] * (2 * pieces_per),
        in_specs=[SMEM] + [ANY] * (len(flat) + len(held)),
        out_specs=[ANY] * (2 * pieces_per),
        scratch_shapes=[pltpu.SemaphoreType.DMA((2 * pieces_per * team,))],
        input_output_aliases={1 + len(flat) + n: n for n in range(len(held))},
        cost_estimate=pl.CostEstimate(
            flops=0, bytes_accessed=2 * pieces_per * team * tile * HD * 4, transcendentals=0
        ),
        name="unpack",
    )(cols, *flat, *held)


def nt(a, b):
    return lax.dot_general(a, b, (((1,), (1,)), ((), ())), preferred_element_type=F32)


def nn(a, b):
    return jnp.dot(a, b, preferred_element_type=F32)


def attend_kernel(team, rows, wmax, tbl_ref, *refs):
    pieces = refs[:team]
    lo_ref, hi_ref = refs[team : team + 2]
    outs = refs[team + 2 : 2 * team + 2]
    loc_ref, glo_ref, ghi_ref = refs[2 * team + 2 : 2 * team + 5]
    qbuf, gbuf, kbuf, vbuf, kt, vt, dk, dv, s_buf, p_buf, ot, dqt, stat, sems = refs[2 * team + 5 :]
    tile = qbuf.shape[1]
    slots = team + 2 * rows
    copies = []
    for d in range(team):
        copies.append((pieces[d].at[0], qbuf.at[d]))
        copies.append((pieces[d].at[1], gbuf.at[d]))
        copies.append((pieces[d].at[2], kbuf.at[rows + d]))
        copies.append((pieces[d].at[3], vbuf.at[rows + d]))
    for r in range(rows):
        copies.append((lo_ref.at[r, 0], kbuf.at[r]))
        copies.append((lo_ref.at[r, 1], vbuf.at[r]))
        copies.append((hi_ref.at[r, 0], kbuf.at[rows + team + r]))
        copies.append((hi_ref.at[r, 1], vbuf.at[rows + team + r]))
    run_copies(copies, sems)

    def prepare(n, carry):
        kt[n] = kbuf[n].T
        vt[n] = vbuf[n].T
        dk[n] = jnp.zeros((tile, HD), F32)
        dv[n] = jnp.zeros((tile, HD), F32)
        return carry

    lax.fori_loop(0, slots, prepare, 0)
    factor = SCALE * math.log2(math.e)

    for d in range(team):
        count = tbl_ref[d, wmax]
        query = qbuf[d]
        grad = gbuf[d]

        def scores(w, top):
            s = nt(kbuf[tbl_ref[d, w]], query)
            s_buf[w] = s
            return jnp.maximum(top, jnp.max(s, axis=0, keepdims=True))

        top = lax.fori_loop(0, count, scores, jnp.full((1, tile), -jnp.inf, F32))

        ot[...] = jnp.zeros((HD, tile), F32)

        def expo(w, total):
            p = jnp.exp2((s_buf[w] - top) * factor)
            low = p.astype(BF16)
            p_buf[w] = low
            ot[...] += nn(vt[tbl_ref[d, w]], low)
            return total + jnp.sum(p, axis=0, keepdims=True)

        total = lax.fori_loop(0, count, expo, jnp.zeros((1, tile), F32))
        inv = 1.0 / total
        out_t = (ot[...] * inv).astype(BF16)
        grad_t = grad.T.astype(F32)
        offset = jnp.sum(grad_t * out_t.astype(F32), axis=0, keepdims=True)
        outs[d][0] = out_t.T
        grad_over = (grad_t * inv).astype(BF16).T
        query_over = (query.T.astype(F32) * inv).astype(BF16).T
        dqt[...] = jnp.zeros((HD, tile), F32)

        def backward(w, carry):
            slot = tbl_ref[d, w]
            low = p_buf[w]
            dp = nt(vbuf[slot], grad)
            ds = (low.astype(F32) * (dp - offset)).astype(BF16)
            dv[slot] += nn(low, grad_over)
            dk[slot] += nn(ds, query_over)
            dqt[...] += nn(kt[slot], ds)
            return carry

        lax.fori_loop(0, count, backward, 0)
        outs[d][1] = (dqt[...] * (inv * SCALE)).astype(BF16).T

    for d in range(team):
        loc_ref[d, 0] = dk[rows + d] * SCALE
        loc_ref[d, 1] = dv[rows + d]
    for r in range(rows):
        glo_ref[r, 0] = (dk[r] * SCALE).astype(BF16)
        glo_ref[r, 1] = dv[r].astype(BF16)
        ghi_ref[r, 0] = (dk[rows + team + r] * SCALE).astype(BF16)
        ghi_ref[r, 1] = dv[rows + team + r].astype(BF16)


def attend(team, rows, wmax, table, pieces, low_halo, high_halo):
    tile = pieces[0].shape[1]
    slots = team + 2 * rows
    pairs = team * wmax * tile * tile
    outs = pl.pallas_call(
        functools.partial(attend_kernel, team, rows, wmax),
        out_shape=[struct((2, tile, HD), BF16)] * team
        + [struct((team, 2, tile, HD), F32)]
        + [struct((rows, 2, tile, HD), BF16)] * 2,
        in_specs=[SMEM] + [ANY] * (team + 2),
        out_specs=[VMEM] * (team + 3),
        scratch_shapes=[
            pltpu.VMEM((team, tile, HD), BF16),
            pltpu.VMEM((team, tile, HD), BF16),
            pltpu.VMEM((slots, tile, HD), BF16),
            pltpu.VMEM((slots, tile, HD), BF16),
            pltpu.VMEM((slots, HD, tile), BF16),
            pltpu.VMEM((slots, HD, tile), BF16),
            pltpu.VMEM((slots, tile, HD), F32),
            pltpu.VMEM((slots, tile, HD), F32),
            pltpu.VMEM((wmax, tile, tile), F32),
            pltpu.VMEM((wmax, tile, tile), BF16),
            pltpu.VMEM((HD, tile), F32),
            pltpu.VMEM((HD, tile), F32),
            pltpu.VMEM((8, tile), F32),
            pltpu.SemaphoreType.DMA((4 * team + 4 * rows,)),
        ],
        cost_estimate=pl.CostEstimate(
            flops=12 * pairs * HD, bytes_accessed=8 * 1024 * 1024, transcendentals=pairs
        ),
        compiler_params=pltpu.CompilerParams(vmem_limit_bytes=VMEM_LIMIT),
        name="attend",
    )(table, *pieces, low_halo, high_halo)
    return outs[:team], outs[team], outs[team + 1], outs[team + 2]


def body(queries, keys, values, grad_out, window_tiles, window_count):
    rows_here, tile, lane_width = queries.shape
    wmax = window_tiles.shape[1]
    heads = lane_width // HD
    rows = lax.axis_size("sub")
    slabs = lax.axis_size("ctx")
    span = 2 if heads % (2 * rows) == 0 and slabs % 2 == 0 else 1
    team = span * rows
    per = heads // team
    size = slabs * rows
    slab = lax.axis_index("ctx")
    row = lax.axis_index("sub")
    me = (slab % span) * rows + row

    def swap(value, d):
        if d == 0:
            return value
        return lax.ppermute(value, RING, [(i, i - i % team + (i % team ^ d)) for i in range(size)])

    def up(value):
        return lax.ppermute(value, RING, [(i, i + team) for i in range(size - team)])

    def down(value):
        return lax.ppermute(value, RING, [(i + team, i) for i in range(size - team)])

    relative = (window_tiles[0] // rows - slab + 1) * rows + window_tiles[0] % rows
    place = relative + (slab % span) * rows
    entry = jnp.concatenate([place, window_count, jnp.zeros((1,), jnp.int32)])[None]
    entries = jnp.concatenate([swap(entry, d) for d in range(team)], axis=0)
    spot = entries[:, :wmax]
    inside = (spot >= rows) & (spot < rows + team)
    ordered = jnp.where(inside, rows + ((spot - rows) ^ me), spot ^ row)
    table = jnp.concatenate([ordered, entries[:, wmax:]], axis=1)

    partners = jnp.arange(team, dtype=jnp.int32) ^ me
    first = me < rows
    outs = None
    for c in range(per):
        cols = (partners * per + c) * HD
        packed = pack(team, cols, queries, grad_out, keys, values)
        pieces = [swap(packed[d], d) for d in range(team)]
        near = jnp.stack([piece[2:] for piece in pieces[:rows]])
        if span == 1:
            going_down = going_up = near
        else:
            far = jnp.stack([piece[2:] for piece in pieces[rows:]])
            going_down = jnp.where(first, near, far)
            going_up = jnp.where(first, far, near)
        high_halo = down(going_down)
        low_halo = up(going_up)
        done, local, grad_low, grad_high = attend(
            team, rows, wmax, table, pieces, low_halo, high_halo
        )
        from_above = down(grad_low)
        from_below = up(grad_high)
        home = []
        for d in range(team):
            e = d % rows
            if span == 1:
                extra = from_below[e].astype(F32) + from_above[e].astype(F32)
            else:
                mine = first if d < rows else jnp.logical_not(first)
                extra = jnp.where(mine, from_below[e], from_above[e]).astype(F32)
            home.append([swap(done[d], d), swap((local[d] + extra).astype(BF16), d)])
        outs = unpack(team, cols, home, outs, queries.shape)
    attended, grad_queries, grad_keys, grad_values = outs
    return (attended, grad_queries, grad_keys, grad_values)


def solution(mesh):
    spec = P(("grp", "ctx", "sub"), None, "head")
    return jax.shard_map(
        body,
        mesh=mesh,
        in_specs=(spec, spec, spec, spec, P(("grp", "ctx", "sub"), None), P(("grp", "ctx", "sub"))),
        out_specs=(spec, spec, spec, spec),
        check_vma=False,
    )
```

```python
import functools
import math

import jax
import jax.numpy as jnp
from jax import lax
from jax.experimental import pallas as pl
from jax.experimental.pallas import tpu as pltpu
from jax.sharding import PartitionSpec as P

HD = 128
FLAG_ROWS = 16
RING = ("ctx", "sub")
F32 = jnp.float32
BF16 = jnp.bfloat16
SCALE = 1.0 / math.sqrt(HD)
FACTOR = SCALE * math.log2(math.e)
ANY = pl.BlockSpec(memory_space=pl.ANY)
VMEM = pl.BlockSpec(memory_space=pltpu.VMEM)
SMEM = pl.BlockSpec(memory_space=pltpu.SMEM)
PARAMS = pltpu.CompilerParams(vmem_limit_bytes=48 * 1024 * 1024)


def struct(shape, dtype):
    return jax.ShapeDtypeStruct(shape, dtype)


def moved(nbytes):
    return pl.CostEstimate(flops=0, bytes_accessed=nbytes, transcendentals=0)


def run_copies(copies, sems):
    started = [pltpu.make_async_copy(src, dst, sems.at[n]) for n, (src, dst) in enumerate(copies)]
    for copy in started:
        copy.start()
    for copy in started:
        copy.wait()


def pack_kernel(jobs, tile, cols_ref, flags_ref, *refs):
    sources, outs = refs[:4], refs[4 : 4 + len(jobs)]
    for out, (pieces, kinds, flagged) in zip(outs, jobs):
        at = 0
        for d, c in pieces:
            lanes = pl.ds(pl.multiple_of(cols_ref[c, d], HD), HD)
            for n in kinds:
                out[pl.ds(at, tile)] = sources[n][0, :, lanes]
                at += tile
        if flagged:
            lane = lax.broadcasted_iota(jnp.int32, (FLAG_ROWS, HD), 1)
            row = jnp.zeros((FLAG_ROWS, HD), F32)
            for w in range(flags_ref.shape[0]):
                row = jnp.where(lane == w, flags_ref[w].astype(F32), row)
            out[pl.ds(at, FLAG_ROWS)] = row.astype(BF16)


def pack(jobs, cols, flags, sources, after=()):
    tile = sources[0].shape[1]
    shapes = [
        (len(pieces) * len(kinds) * tile + (FLAG_ROWS if flagged else 0), HD)
        for pieces, kinds, flagged in jobs
    ]

    def kernel(cols_ref, flags_ref, *refs):
        pack_kernel(jobs, tile, cols_ref, flags_ref, *refs[:4], *refs[4 + len(after) :])

    return pl.pallas_call(
        kernel,
        out_shape=[struct(shape, BF16) for shape in shapes],
        in_specs=[SMEM, SMEM] + [VMEM] * 4 + [ANY] * len(after),
        out_specs=[VMEM] * len(jobs),
        cost_estimate=moved(sum(4 * HD * shape[0] for shape in shapes)),
        compiler_params=PARAMS,
        name="pack",
    )(cols, flags, *sources, *after)


def relay_kernel(rows, tile, *refs):
    pieces, out, sems = refs[:rows], refs[-2], refs[-1]
    run_copies(
        [
            (pieces[e].at[pl.ds(0, 2 * tile)], out.at[pl.ds(2 * tile * e, 2 * tile)])
            for e in range(rows)
        ],
        sems,
    )


def relay(rows, tile, pieces):
    return pl.pallas_call(
        functools.partial(relay_kernel, rows, tile),
        out_shape=struct((rows * 2 * tile, HD), BF16),
        in_specs=[ANY] * rows,
        out_specs=ANY,
        scratch_shapes=[pltpu.SemaphoreType.DMA((rows,))],
        cost_estimate=moved(rows * 8 * tile * HD),
        name="relay",
    )(*pieces)


def nt(a, b):
    return lax.dot_general(a, b, (((1,), (1,)), ((), ())), preferred_element_type=F32)


def nn(a, b):
    return jnp.dot(a, b, preferred_element_type=F32)


def attend_kernel(plan, rows, tile, live_ref, *refs):
    loads, windows, n_in, spare = plan
    slabs_here = len(windows)
    team = slabs_here * rows
    inputs = refs[:n_in]
    rest = refs[n_in + spare :]
    done, local, grads_one, grads_two = rest[:4]
    qbuf, gbuf, kbuf, vbuf, kt, vt, dk, dv, s_buf, p_buf, ds_buf, sems = rest[4:]
    targets = {"k": kbuf, "v": vbuf, "q": qbuf, "g": gbuf}
    run_copies(
        [
            (inputs[n].at[pl.ds(at, tile)], targets[kind].at[slab, pl.ds(e * tile, tile)])
            for n, at, kind, slab, e in loads
        ],
        sems,
    )
    width = rows * tile
    places = kbuf.shape[0]

    def prepare(n, carry):
        kt[n] = kbuf[n].T
        vt[n] = vbuf[n].T
        dk[n] = jnp.zeros((width, HD), F32)
        dv[n] = jnp.zeros((width, HD), F32)
        return carry

    lax.fori_loop(0, places, prepare, 0)
    lane = lax.broadcasted_iota(jnp.int32, (1, width), 1)

    for a, window in enumerate(windows):
        query = qbuf[a]
        grad = gbuf[a]

        def seen(b):
            total = 0
            for f in range(rows):
                for e in range(rows):
                    total = total + live_ref[a * rows + f, b * rows + e]
            return total > 0

        top = jnp.full((1, width), -jnp.inf, F32)
        for b, place in enumerate(window):

            def scores(_, b=b, place=place, top=top):
                best = top
                for e in range(rows):
                    keep = jnp.zeros((1, width), jnp.int32)
                    for f in range(rows):
                        inside = (lane >= f * tile) & (lane < (f + 1) * tile)
                        keep = jnp.where(inside, live_ref[a * rows + f, b * rows + e], keep)
                    mask = jnp.where(keep > 0, 0.0, -jnp.inf)
                    s = nt(kbuf[place, pl.ds(e * tile, tile)], query) + mask
                    s_buf[b, pl.ds(e * tile, tile)] = s
                    best = jnp.maximum(best, jnp.max(s, axis=0, keepdims=True))
                return best

            top = lax.cond(seen(b), scores, lambda _, top=top: top, 0)

        total = jnp.zeros((1, width), F32)
        out_t = jnp.zeros((HD, width), F32)
        for b, place in enumerate(window):

            def expo(_, b=b, place=place, total=total, out_t=out_t):
                for e in range(rows):
                    at = pl.ds(e * tile, tile)
                    p = jnp.exp2((s_buf[b, at] - top) * FACTOR)
                    total = total + jnp.sum(p, axis=0, keepdims=True)
                    p_buf[b, at] = p.astype(BF16)
                return total, out_t + nn(vt[place], p_buf[b])

            total, out_t = lax.cond(
                seen(b), expo, lambda _, total=total, out_t=out_t: (total, out_t), 0
            )

        inv = 1.0 / total
        low_t = (out_t * inv).astype(BF16)
        grad_t = grad.T.astype(F32)
        offset = jnp.sum(grad_t * low_t.astype(F32), axis=0, keepdims=True)
        grad_over = (grad_t * inv).astype(BF16).T
        query_over = (query.T.astype(F32) * inv).astype(BF16).T
        out = low_t.T
        dq_t = jnp.zeros((HD, width), F32)
        for b, place in enumerate(window):

            def backward(_, b=b, place=place, dq_t=dq_t):
                for e in range(rows):
                    at = pl.ds(e * tile, tile)
                    p = p_buf[b, at]
                    dp = nt(vbuf[place, at], grad)
                    ds = (p.astype(F32) * (dp - offset)).astype(BF16)
                    ds_buf[at] = ds
                    dv[place, at] += nn(p, grad_over)
                    dk[place, at] += nn(ds, query_over)
                return dq_t + nn(kt[place], ds_buf[...])

            dq_t = lax.cond(seen(b), backward, lambda _, dq_t=dq_t: dq_t, 0)
        dq = (dq_t * (inv * SCALE)).astype(BF16).T
        for f in range(rows):
            done[a * rows + f, 0] = out[f * tile : (f + 1) * tile]
            done[a * rows + f, 1] = dq[f * tile : (f + 1) * tile]

    for d in range(team):
        at = pl.ds(d % rows * tile, tile)
        local[d, 0] = dk[d // rows, at] * SCALE
        local[d, 1] = dv[d // rows, at]
    for n, grads in enumerate((grads_one, grads_two)):
        for e in range(rows):
            at = pl.ds(e * tile, tile)
            grads[e, 0] = (dk[slabs_here + n, at] * SCALE).astype(BF16)
            grads[e, 1] = dv[slabs_here + n, at].astype(BF16)


def attend(rows, tile, live, loads, windows, inputs, spare):
    places = len(windows) + 2
    team = len(windows) * rows
    width = rows * tile
    scores = 3 * len(windows) * width * width
    plan = (loads, windows, len(inputs), len(spare))
    return pl.pallas_call(
        functools.partial(attend_kernel, plan, rows, tile),
        out_shape=[
            struct((team, 2, tile, HD), BF16),
            struct((team, 2, tile, HD), F32),
            struct((rows, 2, tile, HD), BF16),
            struct((rows, 2, tile, HD), BF16),
        ],
        in_specs=[SMEM] + [ANY] * (len(inputs) + len(spare)),
        out_specs=[VMEM] * 4,
        scratch_shapes=[
            pltpu.VMEM((len(windows), width, HD), BF16),
            pltpu.VMEM((len(windows), width, HD), BF16),
            pltpu.VMEM((places, width, HD), BF16),
            pltpu.VMEM((places, width, HD), BF16),
            pltpu.VMEM((places, HD, width), BF16),
            pltpu.VMEM((places, HD, width), BF16),
            pltpu.VMEM((places, width, HD), F32),
            pltpu.VMEM((places, width, HD), F32),
            pltpu.VMEM((3, width, width), F32),
            pltpu.VMEM((3, width, width), BF16),
            pltpu.VMEM((width, width), BF16),
            pltpu.SemaphoreType.DMA((len(loads),)),
        ],
        cost_estimate=pl.CostEstimate(
            flops=12 * scores * HD, bytes_accessed=8 * 1024 * 1024, transcendentals=scores
        ),
        compiler_params=PARAMS,
        name="attend",
    )(live, *inputs, *spare)


def finish_kernel(team, rows, extras, done, local, *refs):
    grads, outs = refs[: len(extras)], refs[-team:]
    for d in range(team):
        for n in range(2):
            outs[d][n] = done[d, n]
            total = local[d, n]
            for grad, slab in zip(grads, extras):
                if d // rows == slab:
                    total = total + grad[d % rows, n].astype(F32)
            outs[d][2 + n] = total.astype(BF16)


def finish(team, rows, extras, done, local, grads, spare):
    tile = done.shape[2]
    return pl.pallas_call(
        functools.partial(finish_kernel, team, rows, extras),
        out_shape=[struct((4, tile, HD), BF16)] * team,
        in_specs=[VMEM] * (2 + len(grads)) + [ANY] * len(spare),
        out_specs=[VMEM] * team,
        cost_estimate=moved(team * 24 * tile * HD),
        compiler_params=PARAMS,
        name="finish",
    )(done, local, *grads, *spare)


def unpack_kernel(team, per, cols_ref, *refs):
    pieces, outs = refs[: team * per], refs[team * per :]
    for c in range(per):
        for d in range(team):
            lanes = pl.ds(pl.multiple_of(cols_ref[c, d], HD), HD)
            for n in range(4):
                outs[n][0, :, lanes] = pieces[c * team + d][n]


def unpack(team, per, cols, pieces, shape):
    tile = shape[1]
    step = tile // 4 if tile % 64 == 0 else tile
    return pl.pallas_call(
        functools.partial(unpack_kernel, team, per),
        grid=(tile // step,),
        out_shape=[struct(shape, BF16)] * 4,
        in_specs=[SMEM] + [pl.BlockSpec((4, step, HD), lambda i: (0, i, 0))] * len(pieces),
        out_specs=[pl.BlockSpec((1, step, shape[2]), lambda i: (0, i, 0))] * 4,
        cost_estimate=moved(len(pieces) * 16 * tile * HD),
        compiler_params=PARAMS,
        name="unpack",
    )(cols, *pieces)


def body(queries, keys, values, grad_out, window_tiles, window_count):
    rows_here, tile, lane_width = queries.shape
    wmax = window_tiles.shape[1]
    heads = lane_width // HD
    rows = lax.axis_size("sub")
    slabs = lax.axis_size("ctx")
    span = 2 if heads % (2 * rows) == 0 and slabs % 2 == 0 else 1
    team = span * rows
    per = heads // team
    size = slabs * rows
    slab = lax.axis_index("ctx")
    row = lax.axis_index("sub")
    odd = slab % span
    me = odd * rows + row

    def swap(value, d):
        if d == 0:
            return value
        return lax.ppermute(value, RING, [(i, i - i % team + (i % team ^ d)) for i in range(size)])

    def shift(value, way, flip=0):
        pairs = []
        for i in range(size):
            place = i % team // rows
            forward = (place == span - 1) if way == 0 else (place == 0)
            if span == 1:
                forward = way == 0
            j = i + team if forward else i - team
            if 0 <= j < size:
                pairs.append((i, j ^ flip))
        return lax.ppermute(value, RING, pairs)

    places = (window_tiles[0] // rows - slab + 1) * rows + window_tiles[0] % rows
    listed = jnp.arange(wmax) < window_count[0]
    flags = jnp.any(
        (places[None, :] == jnp.arange(3 * rows)[:, None]) & listed[None, :], axis=1
    ).astype(jnp.int32)

    partners = jnp.arange(team, dtype=jnp.int32) ^ me
    heads_of = (partners[None, :] * per + jnp.arange(per, dtype=jnp.int32)[:, None]) * HD
    sources = (keys, values, queries, grad_out)
    kinds = (0, 1, 2, 3)
    every = tuple(range(per))
    far = tuple(range(rows, team))

    sent = {}
    if far:
        first = pack([(((d, 0),), kinds, True) for d in far], heads_of, flags, sources)
        for d, value in zip(far, first):
            sent[0, d] = value
    jobs = [
        (tuple((0, c) for c in every), kinds, True),
        (tuple((1, c) for c in every), kinds, True),
        (tuple((0, c) for c in every), (0, 1), False),
        (tuple((1, c) for c in every), (0, 1), False),
    ]
    later = [(c, d) for c in every[1:] for d in far]
    jobs += [(((d, c),), kinds, False) for c, d in later]
    packed = pack(jobs, heads_of, flags, sources, after=tuple(sent.values())[:1])
    own, beside, own_kv, beside_kv = packed[:4]
    for key, value in zip(later, packed[4:]):
        sent[key] = value

    mates = [own, swap(beside, 1)]
    arrived = {}
    for c in every:
        for d in far:
            arrived[c, d] = swap(sent[c, d], d)
    near_one = [shift(own_kv, 0), shift(beside_kv, 0, flip=1)]
    if span == 1:
        near_two = [shift(own_kv, 1), shift(beside_kv, 1, flip=1)]

    lists = [mate[-FLAG_ROWS] for mate in mates] + [arrived[0, d][-FLAG_ROWS] for d in far]
    table = jnp.stack([value[: 3 * rows] for value in lists]).astype(jnp.int32)
    table = table.reshape(team, 3, rows)
    table = jnp.where(row == 0, table, table[:, :, ::-1])
    turned = table[:, ::-1]
    if span == 1:
        live = table
    else:
        live = jnp.concatenate(
            [
                jnp.where(odd == 0, table[:rows], turned[:rows]),
                jnp.where(odd == 0, turned[rows:], table[rows:]),
            ]
        )
    live = live.reshape(team, 3 * rows)

    if span == 1:
        windows = ((1, 0, 2),)
        extras = (0, 0)
    else:
        windows = ((3, 0, 1), (2, 1, 0))
        extras = (0, 1)

    two_bytes = 2 * tile
    pieces = []
    for c in every:
        inputs = [mates[0], mates[1]]
        loads = []
        for e in range(rows):
            for n, kind in enumerate("kvqg"):
                loads.append((e, (4 * c + n) * tile, kind, 0, e))
        for d in far:
            for n, kind in enumerate("kvqg"):
                loads.append((len(inputs), n * tile, kind, 1, d - rows))
            inputs.append(arrived[c, d])
        for e in range(rows):
            for n, kind in enumerate("kv"):
                loads.append((len(inputs), (2 * c + n) * tile, kind, span, e))
            inputs.append(near_one[e])
        if span == 1:
            for e in range(rows):
                for n, kind in enumerate("kv"):
                    loads.append((len(inputs), (2 * c + n) * tile, kind, span + 1, e))
                inputs.append(near_two[e])
        else:
            beyond = shift(relay(rows, tile, [arrived[c, d] for d in far]), 1)
            for e in range(rows):
                for n, kind in enumerate("kv"):
                    loads.append((len(inputs), (2 * e + n) * tile, kind, span + 1, e))
            inputs.append(beyond)
        done, local, grads_one, grads_two = attend(
            rows, tile, live, tuple(loads), windows, inputs, ()
        )
        back = (shift(grads_one, 1), shift(grads_two, 0))
        home = finish(team, rows, extras, done, local, back, ())
        pieces += [swap(home[d], d) for d in range(team)]
    grad_keys, grad_values = None, None
    attended, grad_queries, grad_keys, grad_values = unpack(
        team, per, heads_of, pieces, queries.shape
    )
    return (attended, grad_queries, grad_keys, grad_values)


def solution(mesh):
    spec = P(("grp", "ctx", "sub"), None, "head")
    return jax.shard_map(
        body,
        mesh=mesh,
        in_specs=(spec, spec, spec, spec, P(("grp", "ctx", "sub"), None), P(("grp", "ctx", "sub"))),
        out_specs=(spec, spec, spec, spec),
        check_vma=False,
    )
```

```python
import functools
import math

import jax
import jax.numpy as jnp
from jax import lax
from jax.experimental import pallas as pl
from jax.experimental.pallas import tpu as pltpu
from jax.sharding import PartitionSpec as P

HD = 128
FLAG_ROWS = 16
BLOCKS = 4
RING = ("ctx", "sub")
F32 = jnp.float32
BF16 = jnp.bfloat16
SCALE = 1.0 / math.sqrt(HD)
FACTOR = SCALE * math.log2(math.e)
ANY = pl.BlockSpec(memory_space=pl.ANY)
VMEM = pl.BlockSpec(memory_space=pltpu.VMEM)
SMEM = pl.BlockSpec(memory_space=pltpu.SMEM)
PARAMS = pltpu.CompilerParams(vmem_limit_bytes=48 * 1024 * 1024)


def struct(shape, dtype):
    return jax.ShapeDtypeStruct(shape, dtype)


def moved(nbytes):
    return pl.CostEstimate(flops=0, bytes_accessed=nbytes, transcendentals=0)


def pack_kernel(jobs, step, cols_ref, flags_ref, *refs):
    sources, outs = refs[:4], refs[4 : 4 + len(jobs)]
    lane = lax.broadcasted_iota(jnp.int32, (FLAG_ROWS, HD), 1)
    flags = jnp.zeros((FLAG_ROWS, HD), F32)
    for w in range(flags_ref.shape[0]):
        flags = jnp.where(lane == w, flags_ref[w].astype(F32), flags)
    flags = flags.astype(BF16)
    for out, (d, heads, kinds, flagged) in zip(outs, jobs):
        for m, c in enumerate(heads):
            lanes = pl.ds(pl.multiple_of(cols_ref[c, d], HD), HD)
            for at, n in enumerate(kinds):
                out[m, 0, pl.ds(at * step, step)] = sources[n][0, :, lanes]
            if flagged:
                out[m, 0, pl.ds(len(kinds) * step, FLAG_ROWS)] = flags


def pack(jobs, cols, flags, sources):
    _, tile, lane_width = sources[0].shape
    step = tile // BLOCKS
    shapes = [
        (len(heads), BLOCKS, len(kinds) * step + (FLAG_ROWS if flagged else 0), HD)
        for _, heads, kinds, flagged in jobs
    ]
    return pl.pallas_call(
        functools.partial(pack_kernel, jobs, step),
        grid=(BLOCKS,),
        out_shape=[struct(shape, BF16) for shape in shapes],
        in_specs=[SMEM, SMEM] + [pl.BlockSpec((1, step, lane_width), lambda i: (0, i, 0))] * 4,
        out_specs=[
            pl.BlockSpec((shape[0], 1, shape[2], HD), lambda i: (0, i, 0, 0)) for shape in shapes
        ],
        cost_estimate=moved(sum(4 * HD * math.prod(shape[:3]) for shape in shapes)),
        compiler_params=PARAMS,
        name="pack",
    )(cols, flags, *sources)


def relay_kernel(step, rows, *refs):
    pieces, out = refs[:rows], refs[-1]
    for e, piece in enumerate(pieces):
        out[0, :, pl.ds(2 * step * e, 2 * step)] = piece[0, :, pl.ds(0, 2 * step)]


def relay(step, pieces, passed, spare):
    rows = len(pieces)

    def kernel(*refs):
        relay_kernel(step, rows, *refs[:rows], refs[rows + len(passed) + len(spare)])

    outs = pl.pallas_call(
        kernel,
        out_shape=[struct((1, BLOCKS, rows * 2 * step, HD), BF16)]
        + [struct(value.shape, value.dtype) for value in passed],
        in_specs=[VMEM] * rows + [ANY] * (len(passed) + len(spare)),
        out_specs=[VMEM] + [ANY] * len(passed),
        input_output_aliases={rows + n: 1 + n for n in range(len(passed))},
        cost_estimate=moved(rows * 8 * BLOCKS * step * HD),
        compiler_params=PARAMS,
        name="relay",
    )(*pieces, *passed, *spare)
    return outs[0], outs[1:]


def hold(passed, spare):
    return pl.pallas_call(
        lambda *refs: None,
        out_shape=[struct(value.shape, value.dtype) for value in passed],
        in_specs=[ANY] * (len(passed) + len(spare)),
        out_specs=[ANY] * len(passed),
        input_output_aliases={n: n for n in range(len(passed))},
        cost_estimate=moved(0),
        name="hold",
    )(*passed, *spare)


def nt(a, b):
    return lax.dot_general(a, b, (((1,), (1,)), ((), ())), preferred_element_type=F32)


def nn(a, b):
    return jnp.dot(a, b, preferred_element_type=F32)


def attend_kernel(plan, rows, tile, table_ref, *refs):
    loads, slabs_here, n_in, spare = plan
    inputs = refs[:n_in]
    rest = refs[n_in + spare :]
    done, local, grads_one, grads_two = rest[:4]
    qbuf, gbuf, kbuf, vbuf, kt, vt, dk, dv, s_buf, p_buf, ds_buf, ot = rest[4:]
    targets = {"k": kbuf, "v": vbuf, "q": qbuf, "g": gbuf}
    step = tile // BLOCKS
    for n, at, kind, slab, e in loads:
        for g in range(BLOCKS):
            targets[kind][slab, pl.ds(e * tile + g * step, step)] = inputs[n][
                0, g, pl.ds(at * step, step)
            ]
    width = rows * tile
    team = slabs_here * rows
    places = kbuf.shape[0]

    def prepare(n, carry):
        kt[n] = kbuf[n].T
        vt[n] = vbuf[n].T
        dk[n] = jnp.zeros((width, HD), F32)
        dv[n] = jnp.zeros((width, HD), F32)
        return carry

    lax.fori_loop(0, places, prepare, 0)
    lane = lax.broadcasted_iota(jnp.int32, (1, width), 1)

    def slab_pass(a, carry):
        query = qbuf[a]
        grad = gbuf[a]

        def seen(b):
            count = 0
            for f in range(rows):
                for e in range(rows):
                    count = count + table_ref[a * rows + f, b * rows + e]
            return count > 0

        def scores(b, top):
            def live(top):
                place = table_ref[a * rows, 3 * rows + b]
                for e in range(rows):
                    keep = jnp.zeros((1, width), jnp.int32)
                    for f in range(rows):
                        inside = (lane >= f * tile) & (lane < (f + 1) * tile)
                        keep = jnp.where(inside, table_ref[a * rows + f, b * rows + e], keep)
                    mask = jnp.where(keep > 0, 0.0, -jnp.inf)
                    s = nt(kbuf[place, pl.ds(e * tile, tile)], query) + mask
                    s_buf[b, pl.ds(e * tile, tile)] = s
                    top = jnp.maximum(top, jnp.max(s, axis=0, keepdims=True))
                return top

            return lax.cond(seen(b), live, lambda top: top, top)

        top = lax.fori_loop(0, 3, scores, jnp.full((1, width), -jnp.inf, F32))
        ot[...] = jnp.zeros((HD, width), F32)

        def expo(b, total):
            def live(total):
                place = table_ref[a * rows, 3 * rows + b]
                for e in range(rows):
                    at = pl.ds(e * tile, tile)
                    p = jnp.exp2((s_buf[b, at] - top) * FACTOR)
                    total = total + jnp.sum(p, axis=0, keepdims=True)
                    p_buf[b, at] = p.astype(BF16)
                ot[...] += nn(vt[place], p_buf[b])
                return total

            return lax.cond(seen(b), live, lambda total: total, total)

        total = lax.fori_loop(0, 3, expo, jnp.zeros((1, width), F32))
        inv = 1.0 / total
        low_t = (ot[...] * inv).astype(BF16)
        grad_t = grad.T.astype(F32)
        offset = jnp.sum(grad_t * low_t.astype(F32), axis=0, keepdims=True)
        grad_over = (grad_t * inv).astype(BF16).T
        query_over = (query.T.astype(F32) * (inv * SCALE)).astype(BF16).T
        out = low_t.T
        ot[...] = jnp.zeros((HD, width), F32)

        def backward(b, carry):
            @pl.when(seen(b))
            def _():
                place = table_ref[a * rows, 3 * rows + b]
                for e in range(rows):
                    at = pl.ds(e * tile, tile)
                    p = p_buf[b, at]
                    dp = nt(vbuf[place, at], grad)
                    ds = (p.astype(F32) * (dp - offset)).astype(BF16)
                    ds_buf[at] = ds
                    dv[place, at] += nn(p, grad_over)
                    dk[place, at] += nn(ds, query_over)
                ot[...] += nn(kt[place], ds_buf[...])

            return carry

        lax.fori_loop(0, 3, backward, 0)
        dq = (ot[...] * (inv * SCALE)).astype(BF16).T
        for f in range(rows):
            done[a * rows + f, 0] = out[f * tile : (f + 1) * tile]
            done[a * rows + f, 1] = dq[f * tile : (f + 1) * tile]
        return carry

    lax.fori_loop(0, slabs_here, slab_pass, 0)

    for d in range(team):
        at = pl.ds(d % rows * tile, tile)
        local[d, 0] = dk[d // rows, at]
        local[d, 1] = dv[d // rows, at]
    for n, grads in enumerate((grads_one, grads_two)):
        for e in range(rows):
            at = pl.ds(e * tile, tile)
            grads[e, 0] = dk[slabs_here + n, at].astype(BF16)
            grads[e, 1] = dv[slabs_here + n, at].astype(BF16)


def attend(rows, tile, slabs_here, table, loads, inputs, spare):
    places = slabs_here + 2
    team = slabs_here * rows
    width = rows * tile
    scores = 3 * slabs_here * width * width

    def head_spec(value, c):
        return pl.BlockSpec((1,) + value.shape[1:], lambda i: (c, 0, 0, 0))

    def whole(shape):
        return pl.BlockSpec(shape, lambda i: (0,) * len(shape))

    shapes = [
        struct((team, 2, tile, HD), BF16),
        struct((team, 2, tile, HD), F32),
        struct((rows, 2, tile, HD), BF16),
        struct((rows, 2, tile, HD), BF16),
    ]
    plan = (loads, slabs_here, len(inputs), len(spare))
    return pl.pallas_call(
        functools.partial(attend_kernel, plan, rows, tile),
        grid=(1,),
        out_shape=shapes,
        in_specs=[SMEM] + [head_spec(value, c) for value, c in inputs] + [ANY] * len(spare),
        out_specs=[whole(shape.shape) for shape in shapes],
        scratch_shapes=[
            pltpu.VMEM((slabs_here, width, HD), BF16),
            pltpu.VMEM((slabs_here, width, HD), BF16),
            pltpu.VMEM((places, width, HD), BF16),
            pltpu.VMEM((places, width, HD), BF16),
            pltpu.VMEM((places, HD, width), BF16),
            pltpu.VMEM((places, HD, width), BF16),
            pltpu.VMEM((places, width, HD), F32),
            pltpu.VMEM((places, width, HD), F32),
            pltpu.VMEM((3, width, width), F32),
            pltpu.VMEM((3, width, width), BF16),
            pltpu.VMEM((width, width), BF16),
            pltpu.VMEM((HD, width), F32),
        ],
        cost_estimate=pl.CostEstimate(
            flops=12 * scores * HD, bytes_accessed=8 * 1024 * 1024, transcendentals=scores
        ),
        compiler_params=PARAMS,
        name="attend",
    )(table, *[value for value, _ in inputs], *spare)


def finish_kernel(team, rows, extras, done, local, *refs):
    grads, outs = refs[: len(extras)], refs[-team:]
    for d in range(team):
        for n in range(2):
            outs[d][n] = done[d, n]
            total = local[d, n]
            for grad, slab in zip(grads, extras):
                if d // rows == slab:
                    total = total + grad[d % rows, n].astype(F32)
            outs[d][2 + n] = total.astype(BF16)


def finish(team, rows, extras, done, local, grads, spare):
    tile = done.shape[2]
    return pl.pallas_call(
        functools.partial(finish_kernel, team, rows, extras),
        out_shape=[struct((4, tile, HD), BF16)] * team,
        in_specs=[VMEM] * (2 + len(grads)) + [ANY] * len(spare),
        out_specs=[VMEM] * team,
        cost_estimate=moved(team * 24 * tile * HD),
        compiler_params=PARAMS,
        name="finish",
    )(done, local, *grads, *spare)


def unpack_kernel(team, per, cols_ref, *refs):
    pieces, outs = refs[: team * per], refs[team * per :]
    for c in range(per):
        for d in range(team):
            lanes = pl.ds(pl.multiple_of(cols_ref[c, d], HD), HD)
            for n in range(4):
                outs[n][0, :, lanes] = pieces[c * team + d][n]


def unpack(team, per, cols, pieces, shape):
    tile = shape[1]
    step = tile // 4 if tile % 64 == 0 else tile
    return pl.pallas_call(
        functools.partial(unpack_kernel, team, per),
        grid=(tile // step,),
        out_shape=[struct(shape, BF16)] * 4,
        in_specs=[SMEM] + [pl.BlockSpec((4, step, HD), lambda i: (0, i, 0))] * len(pieces),
        out_specs=[pl.BlockSpec((1, step, shape[2]), lambda i: (0, i, 0))] * 4,
        cost_estimate=moved(len(pieces) * 16 * tile * HD),
        compiler_params=PARAMS,
        name="unpack",
    )(cols, *pieces)


def body(queries, keys, values, grad_out, window_tiles, window_count):
    rows_here, tile, lane_width = queries.shape
    wmax = window_tiles.shape[1]
    heads = lane_width // HD
    rows = lax.axis_size("sub")
    slabs = lax.axis_size("ctx")
    span = 2 if heads % (2 * rows) == 0 and slabs % 2 == 0 else 1
    team = span * rows
    per = heads // team
    size = slabs * rows
    slab = lax.axis_index("ctx")
    row = lax.axis_index("sub")
    odd = slab % span
    me = odd * rows + row

    def swap(value, d):
        if d == 0:
            return value
        return lax.ppermute(value, RING, [(i, i - i % team + (i % team ^ d)) for i in range(size)])

    def shift(value, way, flip=0):
        pairs = []
        for i in range(size):
            place = i % team // rows
            forward = (place == span - 1) if way == 0 else (place == 0)
            if span == 1:
                forward = way == 0
            j = i + team if forward else i - team
            if 0 <= j < size:
                pairs.append((i, j ^ flip))
        return lax.ppermute(value, RING, pairs)

    places = (window_tiles[0] // rows - slab + 1) * rows + window_tiles[0] % rows
    listed = jnp.arange(wmax) < window_count[0]
    flags = jnp.any(
        (places[None, :] == jnp.arange(3 * rows)[:, None]) & listed[None, :], axis=1
    ).astype(jnp.int32)

    partners = jnp.arange(team, dtype=jnp.int32) ^ me
    heads_of = (partners[None, :] * per + jnp.arange(per, dtype=jnp.int32)[:, None]) * HD
    sources = (keys, values, queries, grad_out)
    kinds = (0, 1, 2, 3)
    every = tuple(range(per))
    far = tuple(range(rows, team))
    step = tile // BLOCKS

    jobs = [(d, (c,), kinds, c == 0) for c in every for d in far]
    jobs += [
        (1, every, kinds, True),
        (0, every, (0, 1), False),
        (1, every, (0, 1), False),
        (0, every, kinds, True),
    ]
    packed = pack(jobs, heads_of, flags, sources)
    sent = {(c, d): packed[c * len(far) + n] for c in every for n, d in enumerate(far)}
    beside, own_kv, beside_kv, own = packed[-4:]

    mates = [own, swap(beside, 1)]
    arrived = {(0, d): swap(sent[0, d], d) for d in far}
    held = []
    if span == 2 and per > 1:
        held = hold([sent[1, d] for d in far], [mates[1]])
        arrived.update({(1, d): swap(value, d) for d, value in zip(far, held)})
    near_one = [shift(own_kv, 0), shift(beside_kv, 0, flip=1)]
    if span == 1:
        near_two = [shift(own_kv, 1), shift(beside_kv, 1, flip=1)]

    lists = mates + [arrived[0, d] for d in far]
    table = jnp.stack([value[0, 0, -FLAG_ROWS, : 3 * rows] for value in lists]).astype(jnp.int32)
    table = table.reshape(team, 3, rows)
    table = jnp.where(row == 0, table, table[:, :, ::-1])
    if span == 2:
        turned = table[:, ::-1]
        table = jnp.concatenate(
            [
                jnp.where(odd == 0, table[:rows], turned[:rows]),
                jnp.where(odd == 0, turned[rows:], table[rows:]),
            ]
        )
    if span == 1:
        windows = ((1, 0, 2),)
        extras = (0, 0)
    else:
        windows = ((3, 0, 1), (2, 1, 0))
        extras = (0, 1)
    spots = jnp.repeat(jnp.asarray(windows, jnp.int32), rows, axis=0)
    table = jnp.concatenate([table.reshape(team, 3 * rows), spots], axis=1)

    beyond = {}

    def pass_on(c, spare):
        if span == 1 or c >= per:
            return
        waiting = [(c + 2, d) for d in far if c + 2 < per]
        value, passed = relay(
            step, [arrived[c, d] for d in far], [sent[key] for key in waiting], spare
        )
        beyond[c] = shift(value, 1)
        for key, payload in zip(waiting, passed):
            arrived[key] = swap(payload, key[1])
        ready[c] = value

    ready = {}
    pass_on(0, held[:1])
    pass_on(1, list(ready.values()))
    worked = {}
    homes = {}
    for c in every:
        inputs = []
        loads = []

        def add(value, at, held, wanted, slab_at, e):
            for n, kind in enumerate(wanted):
                loads.append((len(inputs), at + n, kind, slab_at, e))
            inputs.append((value, held))

        for e in range(rows):
            add(mates[e], 0, c, "kvqg", 0, e)
        for d in far:
            add(arrived[c, d], 0, 0, "kvqg", 1, d - rows)
        for e in range(rows):
            add(near_one[e], 0, c, "kv", span, e)
        if span == 1:
            for e in range(rows):
                add(near_two[e], 0, c, "kv", span + 1, e)
        else:
            for n, (kind, e) in enumerate((kind, e) for e in range(rows) for kind in "kv"):
                loads.append((len(inputs), n, kind, span + 1, e))
            inputs.append((beyond[c], 0))
        spare = []
        if c + 1 in ready:
            spare.append(ready[c + 1])
        if c >= 2:
            homes[c - 2] = finish(
                team, rows, extras, *worked[c - 2][:2], worked[c - 2][2], [worked[c - 1][0]]
            )
            spare.append(homes[c - 2][-1])
        done, local, grads_one, grads_two = attend(
            rows, tile, span, table, tuple(loads), inputs, spare
        )
        worked[c] = (done, local, (shift(grads_one, 1), shift(grads_two, 0)))
        pass_on(c + 2, [done])
    for c in every[-2:]:
        homes[c] = finish(team, rows, extras, *worked[c], [])
    pieces = [swap(homes[c][d], d) for c in every for d in range(team)]
    attended, grad_queries, grad_keys, grad_values = unpack(
        team, per, heads_of, pieces, queries.shape
    )
    return (attended, grad_queries, grad_keys, grad_values)


def solution(mesh):
    spec = P(("grp", "ctx", "sub"), None, "head")
    return jax.shard_map(
        body,
        mesh=mesh,
        in_specs=(spec, spec, spec, spec, P(("grp", "ctx", "sub"), None), P(("grp", "ctx", "sub"))),
        out_specs=(spec, spec, spec, spec),
        check_vma=False,
    )
```

```python
import functools
import math

import jax
import jax.numpy as jnp
from jax import lax
from jax.experimental import pallas as pl
from jax.experimental.pallas import tpu as pltpu
from jax.sharding import PartitionSpec as P

HD = 128
FLAG_ROWS = 16
BLOCKS = 4
RING = ("ctx", "sub")
F32 = jnp.float32
BF16 = jnp.bfloat16
SCALE = 1.0 / math.sqrt(HD)
FACTOR = SCALE * math.log2(math.e)
ANY = pl.BlockSpec(memory_space=pl.ANY)
SMEM = pl.BlockSpec(memory_space=pltpu.SMEM)
PARAMS = pltpu.CompilerParams(vmem_limit_bytes=48 * 1024 * 1024)


def struct(shape, dtype):
    return jax.ShapeDtypeStruct(shape, dtype)


def moved(nbytes):
    return pl.CostEstimate(flops=0, bytes_accessed=nbytes, transcendentals=0)


def pack_kernel(jobs, step, first, places_ref, flags_ref, *refs):
    sources, outs = refs[:4], refs[-len(jobs) :]
    lane = lax.broadcasted_iota(jnp.int32, (FLAG_ROWS, HD), 1)
    flags = jnp.zeros((FLAG_ROWS, HD), F32)
    for w in range(flags_ref.shape[0]):
        flags = jnp.where(lane == w, flags_ref[w].astype(F32), flags)
    flags = flags.astype(BF16)
    team = places_ref.shape[0]
    for out, (d, heads, kinds, flagged) in zip(outs, jobs):
        for m, c in enumerate(heads):
            lanes = pl.ds(pl.multiple_of(((c - first) * team + places_ref[d]) * HD, HD), HD)
            for at, n in enumerate(kinds):
                out[m, 0, pl.ds(at * step, step)] = sources[n][0, :, lanes]
            if flagged:
                out[m, 0, pl.ds(len(kinds) * step, FLAG_ROWS)] = flags


def pack(jobs, heads, places, flags, sources, spare):
    _, tile, lane_width = sources[0].shape
    step = tile // BLOCKS
    team = places.shape[0]
    first = heads[0]
    count = len(heads)
    wide = count * team * HD if first % count == 0 else lane_width
    block = first // count if first % count == 0 else 0
    start = first if first % count == 0 else 0
    shapes = [
        (len(held), BLOCKS, len(kinds) * step + (FLAG_ROWS if flagged else 0), HD)
        for _, held, kinds, flagged in jobs
    ]
    return pl.pallas_call(
        functools.partial(pack_kernel, jobs, step, start),
        grid=(BLOCKS,),
        out_shape=[struct(shape, BF16) for shape in shapes],
        in_specs=[SMEM, SMEM]
        + [pl.BlockSpec((1, step, wide), lambda i: (0, i, block))] * 4
        + [ANY] * len(spare),
        out_specs=[
            pl.BlockSpec((shape[0], 1, shape[2], HD), lambda i: (0, i, 0, 0)) for shape in shapes
        ],
        cost_estimate=moved(sum(4 * HD * math.prod(shape[:3]) for shape in shapes)),
        compiler_params=PARAMS,
        name="pack",
    )(places, flags, *sources, *spare)


def relay_kernel(step, rows, near, far, grads, outs):
    for out, pieces, grad in zip(outs, (near, far), grads):
        for e, (piece, at) in enumerate(pieces):
            out[0, :, pl.ds(2 * step * e, 2 * step)] = piece[at, :, pl.ds(0, 2 * step)]
        if grad is not None:
            for e in range(rows):
                for n in range(2):
                    for g in range(BLOCKS):
                        at = pl.ds((2 * rows + 2 * e + n) * step, step)
                        out[0, g, at] = grad[e, n, pl.ds(g * step, step)]


def relay(step, held, near, far, grads, passed, spare):
    rows = len(near)
    kinds = 2 if far else 1
    high = (4 if grads else 2) * rows * step

    def kernel(*refs):
        refs = list(refs)
        near_refs = [(refs.pop(0), 0) for _ in range(rows)]
        far_refs = [(refs.pop(0), 0) for _ in far]
        grad_refs = [refs.pop(0) for _ in grads] or [None] * kinds
        outs = refs[len(passed) + len(spare) :][:kinds]
        relay_kernel(step, rows, near_refs, far_refs, grad_refs, outs)

    def whole(shape):
        return pl.BlockSpec(shape, lambda i: (0,) * len(shape))

    before = rows + len(far) + len(grads)
    shape = (1, BLOCKS, high, HD)
    outs = pl.pallas_call(
        kernel,
        grid=(1,),
        out_shape=[struct(shape, BF16)] * kinds
        + [struct(value.shape, value.dtype) for value in passed],
        in_specs=[
            pl.BlockSpec((1, BLOCKS, 2 * step, HD), lambda i, at=at: (at, 0, 0, 0))
            for at in [held] * rows + [0] * len(far)
        ]
        + [whole(value.shape) for value in grads]
        + [ANY] * (len(passed) + len(spare)),
        out_specs=[whole(shape)] * kinds + [ANY] * len(passed),
        input_output_aliases={before + n: kinds + n for n in range(len(passed))},
        cost_estimate=moved(kinds * 4 * BLOCKS * high * HD),
        compiler_params=PARAMS,
        name="relay",
    )(*near, *far, *grads, *passed, *spare)
    return outs[:kinds], outs[kinds:]


def nt(a, b):
    return lax.dot_general(a, b, (((1,), (1,)), ((), ())), preferred_element_type=F32)


def nn(a, b):
    return jnp.dot(a, b, preferred_element_type=F32)


def attend_kernel(plan, rows, tile, table_ref, *refs):
    loads, slabs_here, n_in, spare = plan
    inputs = refs[:n_in]
    rest = refs[n_in + spare :]
    done, local, grads_one, grads_two = rest[:4]
    qbuf, gbuf, kbuf, vbuf, kt, vt, dk_t, dv_t, s_buf, p_buf, ds_buf, ot = rest[4:]
    targets = {"k": kbuf, "v": vbuf, "q": qbuf, "g": gbuf}
    step = tile // BLOCKS
    for n, at, kind, slab, e in loads:
        for g in range(BLOCKS):
            targets[kind][slab, pl.ds(e * tile + g * step, step)] = inputs[n][
                0, g, pl.ds(at * step, step)
            ]
    width = rows * tile
    team = slabs_here * rows
    places = kbuf.shape[0]

    def prepare(n, carry):
        kt[n] = kbuf[n].T
        vt[n] = vbuf[n].T
        dk_t[n] = jnp.zeros((HD, width), F32)
        dv_t[n] = jnp.zeros((HD, width), F32)
        return carry

    lax.fori_loop(0, places, prepare, 0)
    lane = lax.broadcasted_iota(jnp.int32, (1, width), 1)

    def slab_pass(a, carry):
        query = qbuf[a]
        grad = gbuf[a]

        def seen(b):
            count = 0
            for f in range(rows):
                for e in range(rows):
                    count = count + table_ref[a * rows + f, b * rows + e]
            return count > 0

        def scores(b, top):
            def live(top):
                place = table_ref[a * rows, 3 * rows + b]
                for e in range(rows):
                    keep = jnp.zeros((1, width), jnp.int32)
                    for f in range(rows):
                        inside = (lane >= f * tile) & (lane < (f + 1) * tile)
                        keep = jnp.where(inside, table_ref[a * rows + f, b * rows + e], keep)
                    mask = jnp.where(keep > 0, 0.0, -jnp.inf)
                    s = nt(kbuf[place, pl.ds(e * tile, tile)], query) + mask
                    s_buf[b, pl.ds(e * tile, tile)] = s
                    top = jnp.maximum(top, jnp.max(s, axis=0, keepdims=True))
                return top

            return lax.cond(seen(b), live, lambda top: top, top)

        top = lax.fori_loop(0, 3, scores, jnp.full((1, width), -jnp.inf, F32))
        ot[...] = jnp.zeros((HD, width), F32)

        def expo(b, total):
            def live(total):
                place = table_ref[a * rows, 3 * rows + b]
                for e in range(rows):
                    at = pl.ds(e * tile, tile)
                    p = jnp.exp2((s_buf[b, at] - top) * FACTOR)
                    total = total + jnp.sum(p, axis=0, keepdims=True)
                    p_buf[b, at] = p.astype(BF16)
                ot[...] += nn(vt[place], p_buf[b])
                return total

            return lax.cond(seen(b), live, lambda total: total, total)

        total = lax.fori_loop(0, 3, expo, jnp.zeros((1, width), F32))
        inv = 1.0 / total
        low_t = (ot[...] * inv).astype(BF16)
        grad_t = grad.T.astype(F32)
        offset = jnp.sum(grad_t * low_t.astype(F32), axis=0, keepdims=True)
        grad_over = (grad_t * inv).astype(BF16)
        query_over = (query.T.astype(F32) * (inv * SCALE)).astype(BF16)
        out = low_t.T
        ot[...] = jnp.zeros((HD, width), F32)

        def backward(b, carry):
            @pl.when(seen(b))
            def _():
                place = table_ref[a * rows, 3 * rows + b]
                for e in range(rows):
                    at = pl.ds(e * tile, tile)
                    p = p_buf[b, at]
                    dp = nt(vbuf[place, at], grad)
                    ds = (p.astype(F32) * (dp - offset)).astype(BF16)
                    ds_buf[at] = ds
                dv_t[place] += nt(grad_over, p_buf[b])
                dk_t[place] += nt(query_over, ds_buf[...])
                ot[...] += nn(kt[place], ds_buf[...])

            return carry

        lax.fori_loop(0, 3, backward, 0)
        dq = (ot[...] * (inv * SCALE)).astype(BF16).T
        for f in range(rows):
            done[a * rows + f, 0] = out[f * tile : (f + 1) * tile]
            done[a * rows + f, 1] = dq[f * tile : (f + 1) * tile]
        return carry

    lax.fori_loop(0, slabs_here, slab_pass, 0)

    for n, sums in enumerate((dk_t, dv_t)):
        for d in range(team):
            local[d, n] = sums[d // rows, :, pl.ds(d % rows * tile, tile)].T
        for m, grads in enumerate((grads_one, grads_two)):
            for e in range(rows):
                terms = sums[slabs_here + m, :, pl.ds(e * tile, tile)]
                grads[e, n] = terms.astype(BF16).T


def attend(rows, tile, slabs_here, table, loads, inputs, spare):
    places = slabs_here + 2
    team = slabs_here * rows
    width = rows * tile
    scores = 3 * slabs_here * width * width

    def head_spec(value, c):
        return pl.BlockSpec((1,) + value.shape[1:], lambda i: (c, 0, 0, 0))

    def whole(shape):
        return pl.BlockSpec(shape, lambda i: (0,) * len(shape))

    shapes = [
        struct((team, 2, tile, HD), BF16),
        struct((team, 2, tile, HD), F32),
        struct((rows, 2, tile, HD), BF16),
        struct((rows, 2, tile, HD), BF16),
    ]
    plan = (loads, slabs_here, len(inputs), len(spare))
    return pl.pallas_call(
        functools.partial(attend_kernel, plan, rows, tile),
        grid=(1,),
        out_shape=shapes,
        in_specs=[SMEM] + [head_spec(value, c) for value, c in inputs] + [ANY] * len(spare),
        out_specs=[whole(shape.shape) for shape in shapes],
        scratch_shapes=[
            pltpu.VMEM((slabs_here, width, HD), BF16),
            pltpu.VMEM((slabs_here, width, HD), BF16),
            pltpu.VMEM((places, width, HD), BF16),
            pltpu.VMEM((places, width, HD), BF16),
            pltpu.VMEM((places, HD, width), BF16),
            pltpu.VMEM((places, HD, width), BF16),
            pltpu.VMEM((places, HD, width), F32),
            pltpu.VMEM((places, HD, width), F32),
            pltpu.VMEM((3, width, width), F32),
            pltpu.VMEM((3, width, width), BF16),
            pltpu.VMEM((width, width), BF16),
            pltpu.VMEM((HD, width), F32),
        ],
        cost_estimate=pl.CostEstimate(
            flops=12 * scores * HD, bytes_accessed=8 * 1024 * 1024, transcendentals=scores
        ),
        compiler_params=PARAMS,
        name="attend",
    )(table, *[value for value, _ in inputs], *spare)


def finish(rows, extras, done, local, grads, spare):
    team, _, tile, _ = done.shape
    step = tile // BLOCKS

    def kernel(done, local, *refs):
        terms, outs = refs[: len(grads)], refs[-team:]
        for d in range(team):
            out = outs[d].at[0]
            for n in range(2):
                out[n] = done[d, n]
                for g in range(BLOCKS):
                    at = pl.ds(g * step, step)
                    total = local[d, n, at]
                    for term, (_, packed), slab in zip(terms, grads, extras):
                        if d // rows != slab:
                            continue
                        if packed:
                            row = pl.ds((2 * (d % rows) + n) * step, step)
                            total = total + term[0, g, row].astype(F32)
                        else:
                            total = total + term[d % rows, n, at].astype(F32)
                    out[2 + n, at] = total.astype(BF16)

    def whole(shape):
        return pl.BlockSpec(shape, lambda i: (0,) * len(shape))

    def grad_spec(value, packed):
        if not packed:
            return whole(value.shape)
        return pl.BlockSpec((1, BLOCKS, 2 * rows * step, HD), lambda i: (0, 0, 1, 0))

    piece = (1, 4, tile, HD)
    return pl.pallas_call(
        kernel,
        grid=(1,),
        out_shape=[struct(piece, BF16)] * team,
        in_specs=[whole(done.shape), whole(local.shape)]
        + [grad_spec(*grad) for grad in grads]
        + [ANY] * len(spare),
        out_specs=[whole(piece)] * team,
        cost_estimate=moved(team * 24 * tile * HD),
        compiler_params=PARAMS,
        name="finish",
    )(done, local, *[value for value, _ in grads], *spare)


def unpack(c, places, pieces, outs, shape):
    tile = shape[1]
    step = tile // BLOCKS
    team = len(pieces)
    held = [] if outs is None else list(outs)

    def kernel(places_ref, *refs):
        for d in range(team):
            lanes = pl.ds(pl.multiple_of(places_ref[d] * HD, HD), HD)
            for n in range(4):
                refs[n - 4][0, :, lanes] = refs[d][0, n]

    return pl.pallas_call(
        kernel,
        grid=(BLOCKS,),
        out_shape=[struct(shape, BF16)] * 4,
        in_specs=[SMEM]
        + [pl.BlockSpec((1, 4, step, HD), lambda i: (0, 0, i, 0))] * team
        + [ANY] * len(held),
        out_specs=[pl.BlockSpec((1, step, team * HD), lambda i: (0, i, c))] * 4,
        input_output_aliases={1 + team + n: n for n in range(len(held))},
        cost_estimate=moved(16 * tile * team * HD),
        compiler_params=PARAMS,
        name="unpack",
    )(places, *pieces, *held)


def body(queries, keys, values, grad_out, window_tiles, window_count):
    rows_here, tile, lane_width = queries.shape
    wmax = window_tiles.shape[1]
    heads = lane_width // HD
    rows = lax.axis_size("sub")
    slabs = lax.axis_size("ctx")
    span = 2 if heads % (2 * rows) == 0 and slabs % 2 == 0 else 1
    team = span * rows
    per = heads // team
    size = slabs * rows
    slab = lax.axis_index("ctx")
    row = lax.axis_index("sub")
    odd = slab % span
    me = odd * rows + row

    def swap(value, d):
        if d == 0:
            return value
        return lax.ppermute(value, RING, [(i, i - i % team + (i % team ^ d)) for i in range(size)])

    def shift(value, way, flip=0):
        pairs = []
        for i in range(size):
            place = i % team // rows
            forward = (place == span - 1) if way == 0 else (place == 0)
            if span == 1:
                forward = way == 0
            j = i + team if forward else i - team
            if 0 <= j < size:
                pairs.append((i, j ^ flip))
        return lax.ppermute(value, RING, pairs)

    places = (window_tiles[0] // rows - slab + 1) * rows + window_tiles[0] % rows
    listed = jnp.arange(wmax) < window_count[0]
    flags = jnp.any(
        (places[None, :] == jnp.arange(3 * rows)[:, None]) & listed[None, :], axis=1
    ).astype(jnp.int32)

    members = jnp.arange(team, dtype=jnp.int32) ^ me
    sources = (keys, values, queries, grad_out)
    kinds = (0, 1, 2, 3)
    every = tuple(range(per))
    far = tuple(range(rows, team))
    step = tile // BLOCKS

    jobs = [(d, (0,), part, part[0] == 0) for part in ((0, 1), (2, 3)) for d in far]
    jobs += [(1, (0,), kinds, True), (0, (0,), kinds, True)]
    packed = pack(jobs, (0,), members, flags, sources, [])
    count = len(far)
    first_kv = [swap(packed[n], d) for n, d in enumerate(far)]
    first_qg = [swap(packed[count + n], d) for n, d in enumerate(far)]
    mates = {0: (packed[-1], swap(packed[-2], 1), 0)}
    sent = {}
    rest = every[1:]
    if rest:
        jobs = [(d, (c,), kinds, False) for c in rest for d in far]
        jobs += [(1, rest, kinds, False), (0, rest, kinds, False)]
        packed = pack(jobs, rest, members, flags, sources, [mates[0][1]])
        sent = {(c, d): packed[m * count + n] for m, c in enumerate(rest) for n, d in enumerate(far)}
        beside = swap(packed[-2], 1)
        mates.update({c: (packed[-1], beside, m) for m, c in enumerate(rest)})

    lists = list(mates[0][:2]) + first_kv
    table = jnp.stack([value[0, 0, -FLAG_ROWS, : 3 * rows] for value in lists]).astype(jnp.int32)
    table = table.reshape(team, 3, rows)
    table = jnp.where(row == 0, table, table[:, :, ::-1])
    if span == 2:
        turned = table[:, ::-1]
        table = jnp.concatenate(
            [
                jnp.where(odd == 0, table[:rows], turned[:rows]),
                jnp.where(odd == 0, turned[rows:], table[rows:]),
            ]
        )
    if span == 1:
        windows = ((1, 0, 2),)
        extras = (0, 0)
    else:
        windows = ((3, 0, 1), (2, 1, 0))
        extras = (0, 1)
    spots = jnp.repeat(jnp.asarray(windows, jnp.int32), rows, axis=0)
    table = jnp.concatenate([table.reshape(team, 3 * rows), spots], axis=1)

    arrived = {}
    halos = {}
    ready = {}
    worked = {}
    home = {}

    def pass_on(c):
        later = [k for k in ((1, 2) if c == 0 else (c + 2,)) if k < per]
        keys = [(k, d) for k in later for d in far]
        pieces = first_kv if c == 0 else [arrived[c, d] for d in far]
        grads = worked[c - 2][2:] if c >= 2 else []
        payloads, passed = relay(
            step,
            mates[c][2],
            mates[c][:2],
            pieces,
            [grads[1], grads[0]] if grads else [],
            [sent[key] for key in keys],
            [],
        )
        ready[c] = payloads[0]
        halos[c] = (shift(payloads[0], 0), shift(payloads[-1], 1))
        for key, payload in zip(keys, passed):
            arrived[key] = swap(payload, key[1])

    def finished(c, spare):
        done, local, grads_one, grads_two = worked[c]
        if c + 2 < per:
            grads = [(halos[c + 2][1], True), (halos[c + 2][0], True)]
        else:
            grads = [(shift(grads_one, 1), False), (shift(grads_two, 0), False)]
        pieces = finish(rows, extras, done, local, grads, spare)
        home[c] = [swap(piece, d) for d, piece in enumerate(pieces)]
        return pieces[0]

    pass_on(0)
    if per > 1:
        pass_on(1)
    for c in every:
        inputs = []
        loads = []

        def add(value, held, wanted, slab_at, tiles):
            for at, (e, kind) in enumerate((e, kind) for e in tiles for kind in wanted):
                loads.append((len(inputs), at, kind, slab_at, e))
            inputs.append((value, held))

        for e in range(rows):
            add(mates[c][e], mates[c][2], "kvqg", 0, [e])
        for n in range(len(far)):
            if c == 0:
                add(first_kv[n], 0, "kv", 1, [n])
                add(first_qg[n], 0, "qg", 1, [n])
            else:
                add(arrived[c, far[n]], 0, "kvqg", 1, [n])
        for n in range(2):
            add(halos[c][n], 0, "kv", span + n, range(rows))
        spare = [ready[c + 1]] if 1 <= c < per - 1 else []
        if c >= 2:
            spare.append(finished(c - 2, [worked[c - 1][0]]))
        worked[c] = attend(rows, tile, span, table, tuple(loads), inputs, spare)
        if c + 2 < per:
            pass_on(c + 2)
    for c in every[-2:]:
        early = [k for k in (c - 2, c - 1) if k in home and (k == c - 2 or c == per - 1)]
        finished(c, [worked[per - 1][0]] + [home[k][d] for k in early for d in far])
    outs = None
    for c in every:
        outs = unpack(c, members, home[c], outs, queries.shape)
    attended, grad_queries, grad_keys, grad_values = outs
    return (attended, grad_queries, grad_keys, grad_values)


def solution(mesh):
    spec = P(("grp", "ctx", "sub"), None, "head")
    return jax.shard_map(
        body,
        mesh=mesh,
        in_specs=(spec, spec, spec, spec, P(("grp", "ctx", "sub"), None), P(("grp", "ctx", "sub"))),
        out_specs=(spec, spec, spec, spec),
        check_vma=False,
    )
```

```python
import functools
import math

import jax
import jax.numpy as jnp
from jax import lax
from jax.experimental import pallas as pl
from jax.experimental.pallas import tpu as pltpu
from jax.sharding import PartitionSpec as P

HD = 128
FLAG_ROWS = 16
BLOCKS = 4
RING = ("ctx", "sub")
F32 = jnp.float32
BF16 = jnp.bfloat16
SCALE = 1.0 / math.sqrt(HD)
FACTOR = SCALE * math.log2(math.e)
ANY = pl.BlockSpec(memory_space=pl.ANY)
SMEM = pl.BlockSpec(memory_space=pltpu.SMEM)
PARAMS = pltpu.CompilerParams(vmem_limit_bytes=34 * 1024 * 1024)
LIGHT = pltpu.CompilerParams(vmem_limit_bytes=20 * 1024 * 1024)


def struct(shape, dtype):
    return jax.ShapeDtypeStruct(shape, dtype)


def hbm(values):
    return [pltpu.with_memory_space_constraint(value, pltpu.HBM) for value in values]


def moved(nbytes):
    return pl.CostEstimate(flops=0, bytes_accessed=nbytes, transcendentals=0)


def pack_kernel(jobs, step, first, places_ref, flags_ref, *refs):
    sources, outs = refs[:4], refs[-len(jobs) :]
    lane = lax.broadcasted_iota(jnp.int32, (FLAG_ROWS, HD), 1)
    flags = jnp.zeros((FLAG_ROWS, HD), F32)
    for w in range(flags_ref.shape[0]):
        flags = jnp.where(lane == w, flags_ref[w].astype(F32), flags)
    flags = flags.astype(BF16)
    team = places_ref.shape[0]
    for out, (d, heads, kinds, flagged) in zip(outs, jobs):
        for m, c in enumerate(heads):
            lanes = pl.ds(pl.multiple_of(((c - first) * team + places_ref[d]) * HD, HD), HD)
            for at, n in enumerate(kinds):
                out[m, 0, pl.ds(at * step, step)] = sources[n][0, :, lanes]
            if flagged:
                out[m, 0, pl.ds(len(kinds) * step, FLAG_ROWS)] = flags


def pack(jobs, heads, places, flags, sources, spare):
    _, tile, lane_width = sources[0].shape
    step = tile // BLOCKS
    team = places.shape[0]
    first = heads[0]
    count = len(heads)
    wide = count * team * HD if first % count == 0 else lane_width
    block = first // count if first % count == 0 else 0
    start = first if first % count == 0 else 0
    shapes = [
        (len(held), BLOCKS, len(kinds) * step + (FLAG_ROWS if flagged else 0), HD)
        for _, held, kinds, flagged in jobs
    ]
    return pl.pallas_call(
        functools.partial(pack_kernel, jobs, step, start),
        grid=(BLOCKS,),
        out_shape=[struct(shape, BF16) for shape in shapes],
        in_specs=[SMEM, SMEM]
        + [pl.BlockSpec((1, step, wide), lambda i: (0, i, block))] * 4
        + [ANY] * len(spare),
        out_specs=[
            pl.BlockSpec((shape[0], 1, shape[2], HD), lambda i: (0, i, 0, 0)) for shape in shapes
        ],
        cost_estimate=moved(sum(4 * HD * math.prod(shape[:3]) for shape in shapes)),
        compiler_params=LIGHT,
        name="pack",
    )(places, flags, *hbm(sources), *spare)


def relay_kernel(step, rows, near, far, grads, outs):
    for out, pieces, grad in zip(outs, (near, far), grads):
        for e, (piece, at) in enumerate(pieces):
            out[0, :, pl.ds(2 * step * e, 2 * step)] = piece[at, :, pl.ds(0, 2 * step)]
        if grad is not None:
            for e in range(rows):
                for n in range(2):
                    for g in range(BLOCKS):
                        at = pl.ds((2 * rows + 2 * e + n) * step, step)
                        out[0, g, at] = grad[e, n, pl.ds(g * step, step)]


def relay(step, held, near, far, grads, spare):
    rows = len(near)
    kinds = 2 if far else 1
    high = (4 if grads else 2) * rows * step

    def kernel(*refs):
        refs = list(refs)
        near_refs = [(refs.pop(0), 0) for _ in range(rows)]
        far_refs = [(refs.pop(0), 0) for _ in far]
        grad_refs = [refs.pop(0) for _ in grads] or [None] * kinds
        outs = refs[len(spare) :]
        relay_kernel(step, rows, near_refs, far_refs, grad_refs, outs)

    def whole(shape):
        return pl.BlockSpec(shape, lambda i: (0,) * len(shape))

    shape = (1, BLOCKS, high, HD)
    return pl.pallas_call(
        kernel,
        grid=(1,),
        out_shape=[struct(shape, BF16)] * kinds,
        in_specs=[
            pl.BlockSpec((1, BLOCKS, 2 * step, HD), lambda i, at=at: (at, 0, 0, 0))
            for at in [held] * rows + [0] * len(far)
        ]
        + [whole(value.shape) for value in grads]
        + [ANY] * len(spare),
        out_specs=[whole(shape)] * kinds,
        cost_estimate=moved(kinds * 4 * BLOCKS * high * HD),
        compiler_params=LIGHT,
        name="relay",
    )(*near, *far, *grads, *spare)


def nt(a, b):
    return lax.dot_general(a, b, (((1,), (1,)), ((), ())), preferred_element_type=F32)


def nn(a, b):
    return jnp.dot(a, b, preferred_element_type=F32)


def attend_kernel(plan, rows, tile, table_ref, *refs):
    loads, slabs_here, n_in, spare = plan
    inputs = refs[:n_in]
    rest = refs[n_in + spare :]
    done, local, grads_one, grads_two = rest[:4]
    qbuf, gbuf, kbuf, vbuf, kt, vt, dk_t, dv_t, s_buf, p_buf, ds_buf, ot = rest[4:]
    targets = {"k": kbuf, "v": vbuf, "q": qbuf, "g": gbuf}
    step = tile // BLOCKS
    for n, at, kind, slab, e in loads:
        for g in range(BLOCKS):
            targets[kind][slab, pl.ds(e * tile + g * step, step)] = inputs[n][
                0, g, pl.ds(at * step, step)
            ]
    width = rows * tile
    team = slabs_here * rows
    places = kbuf.shape[0]

    def prepare(n, carry):
        kt[n] = kbuf[n].T
        vt[n] = vbuf[n].T
        dk_t[n] = jnp.zeros((HD, width), F32)
        dv_t[n] = jnp.zeros((HD, width), F32)
        return carry

    lax.fori_loop(0, places, prepare, 0)
    lane = lax.broadcasted_iota(jnp.int32, (1, width), 1)

    def slab_pass(a, carry):
        query = qbuf[a]
        grad = gbuf[a]

        def seen(b):
            count = 0
            for f in range(rows):
                for e in range(rows):
                    count = count + table_ref[a * rows + f, b * rows + e]
            return count > 0

        def scores(b, top):
            def live(top):
                place = table_ref[a * rows, 3 * rows + b]
                for e in range(rows):
                    keep = jnp.zeros((1, width), jnp.int32)
                    for f in range(rows):
                        inside = (lane >= f * tile) & (lane < (f + 1) * tile)
                        keep = jnp.where(inside, table_ref[a * rows + f, b * rows + e], keep)
                    mask = jnp.where(keep > 0, 0.0, -jnp.inf)
                    s = nt(kbuf[place, pl.ds(e * tile, tile)], query) + mask
                    s_buf[b, pl.ds(e * tile, tile)] = s
                    top = jnp.maximum(top, jnp.max(s, axis=0, keepdims=True))
                return top

            return lax.cond(seen(b), live, lambda top: top, top)

        top = lax.fori_loop(0, 3, scores, jnp.full((1, width), -jnp.inf, F32))
        ot[...] = jnp.zeros((HD, width), F32)

        def expo(b, total):
            def live(total):
                place = table_ref[a * rows, 3 * rows + b]
                for e in range(rows):
                    at = pl.ds(e * tile, tile)
                    p = jnp.exp2((s_buf[b, at] - top) * FACTOR)
                    total = total + jnp.sum(p, axis=0, keepdims=True)
                    p_buf[b, at] = p.astype(BF16)
                ot[...] += nn(vt[place], p_buf[b])
                return total

            return lax.cond(seen(b), live, lambda total: total, total)

        total = lax.fori_loop(0, 3, expo, jnp.zeros((1, width), F32))
        inv = 1.0 / total
        low_t = (ot[...] * inv).astype(BF16)
        grad_t = grad.T.astype(F32)
        offset = jnp.sum(grad_t * low_t.astype(F32), axis=0, keepdims=True)
        grad_over = (grad_t * inv).astype(BF16)
        query_over = (query.T.astype(F32) * (inv * SCALE)).astype(BF16)
        out = low_t.T
        ot[...] = jnp.zeros((HD, width), F32)

        def backward(b, carry):
            @pl.when(seen(b))
            def _():
                place = table_ref[a * rows, 3 * rows + b]
                for e in range(rows):
                    at = pl.ds(e * tile, tile)
                    p = p_buf[b, at]
                    dp = nt(vbuf[place, at], grad)
                    ds = (p.astype(F32) * (dp - offset)).astype(BF16)
                    ds_buf[at] = ds
                dv_t[place] += nt(grad_over, p_buf[b])
                dk_t[place] += nt(query_over, ds_buf[...])
                ot[...] += nn(kt[place], ds_buf[...])

            return carry

        lax.fori_loop(0, 3, backward, 0)
        dq = (ot[...] * (inv * SCALE)).astype(BF16).T
        for f in range(rows):
            done[a * rows + f, 0] = out[f * tile : (f + 1) * tile]
            done[a * rows + f, 1] = dq[f * tile : (f + 1) * tile]
        return carry

    lax.fori_loop(0, slabs_here, slab_pass, 0)

    for n, sums in enumerate((dk_t, dv_t)):
        for d in range(team):
            local[d, n] = sums[d // rows, :, pl.ds(d % rows * tile, tile)].T
        for m, grads in enumerate((grads_one, grads_two)):
            for e in range(rows):
                terms = sums[slabs_here + m, :, pl.ds(e * tile, tile)]
                grads[e, n] = terms.astype(BF16).T


def attend(rows, tile, slabs_here, table, loads, inputs, spare):
    places = slabs_here + 2
    team = slabs_here * rows
    width = rows * tile
    scores = 3 * slabs_here * width * width

    def head_spec(value, c):
        return pl.BlockSpec((1,) + value.shape[1:], lambda i: (c, 0, 0, 0))

    def whole(shape):
        return pl.BlockSpec(shape, lambda i: (0,) * len(shape))

    shapes = [
        struct((team, 2, tile, HD), BF16),
        struct((team, 2, tile, HD), F32),
        struct((rows, 2, tile, HD), BF16),
        struct((rows, 2, tile, HD), BF16),
    ]
    plan = (loads, slabs_here, len(inputs), len(spare))
    return pl.pallas_call(
        functools.partial(attend_kernel, plan, rows, tile),
        grid=(1,),
        out_shape=shapes,
        in_specs=[SMEM] + [head_spec(value, c) for value, c in inputs] + [ANY] * len(spare),
        out_specs=[whole(shape.shape) for shape in shapes],
        scratch_shapes=[
            pltpu.VMEM((slabs_here, width, HD), BF16),
            pltpu.VMEM((slabs_here, width, HD), BF16),
            pltpu.VMEM((places, width, HD), BF16),
            pltpu.VMEM((places, width, HD), BF16),
            pltpu.VMEM((places, HD, width), BF16),
            pltpu.VMEM((places, HD, width), BF16),
            pltpu.VMEM((places, HD, width), F32),
            pltpu.VMEM((places, HD, width), F32),
            pltpu.VMEM((3, width, width), F32),
            pltpu.VMEM((3, width, width), BF16),
            pltpu.VMEM((width, width), BF16),
            pltpu.VMEM((HD, width), F32),
        ],
        cost_estimate=pl.CostEstimate(
            flops=12 * scores * HD, bytes_accessed=8 * 1024 * 1024, transcendentals=scores
        ),
        compiler_params=PARAMS,
        name="attend",
    )(table, *[value for value, _ in inputs], *spare)


def finish(rows, extras, done, local, grads, spare):
    team, _, tile, _ = done.shape
    step = tile // BLOCKS

    def kernel(done, local, *refs):
        terms, outs = refs[: len(grads)], refs[-team:]
        for d in range(team):
            out = outs[d].at[0]
            for n in range(2):
                out[n] = done[d, n]
                for g in range(BLOCKS):
                    at = pl.ds(g * step, step)
                    total = local[d, n, at]
                    for term, (_, packed), slab in zip(terms, grads, extras):
                        if d // rows != slab:
                            continue
                        if packed:
                            row = pl.ds((2 * (d % rows) + n) * step, step)
                            total = total + term[0, g, row].astype(F32)
                        else:
                            total = total + term[d % rows, n, at].astype(F32)
                    out[2 + n, at] = total.astype(BF16)

    def whole(shape):
        return pl.BlockSpec(shape, lambda i: (0,) * len(shape))

    def grad_spec(value, packed):
        if not packed:
            return whole(value.shape)
        return pl.BlockSpec((1, BLOCKS, 2 * rows * step, HD), lambda i: (0, 0, 1, 0))

    piece = (1, 4, tile, HD)
    return pl.pallas_call(
        kernel,
        grid=(1,),
        out_shape=[struct(piece, BF16)] * team,
        in_specs=[whole(done.shape), whole(local.shape)]
        + [grad_spec(*grad) for grad in grads]
        + [ANY] * len(spare),
        out_specs=[whole(piece)] * team,
        cost_estimate=moved(team * 24 * tile * HD),
        compiler_params=LIGHT,
        name="finish",
    )(done, local, *[value for value, _ in grads], *spare)


def unpack(c, places, pieces, outs, shape):
    tile = shape[1]
    step = tile // BLOCKS
    team = len(pieces)
    held = [] if outs is None else list(outs)

    def kernel(places_ref, *refs):
        for d in range(team):
            lanes = pl.ds(pl.multiple_of(places_ref[d] * HD, HD), HD)
            for n in range(4):
                refs[n - 4][0, :, lanes] = refs[d][0, n]

    return pl.pallas_call(
        kernel,
        grid=(BLOCKS,),
        out_shape=[struct(shape, BF16)] * 4,
        in_specs=[SMEM]
        + [pl.BlockSpec((1, 4, step, HD), lambda i: (0, 0, i, 0))] * team
        + [ANY] * len(held),
        out_specs=[pl.BlockSpec((1, step, team * HD), lambda i: (0, i, c))] * 4,
        input_output_aliases={1 + team + n: n for n in range(len(held))},
        cost_estimate=moved(16 * tile * team * HD),
        compiler_params=LIGHT,
        name="unpack",
    )(places, *pieces, *held)


def body(queries, keys, values, grad_out, window_tiles, window_count):
    rows_here, tile, lane_width = queries.shape
    wmax = window_tiles.shape[1]
    heads = lane_width // HD
    rows = lax.axis_size("sub")
    slabs = lax.axis_size("ctx")
    span = 2 if heads % (2 * rows) == 0 and slabs % 2 == 0 else 1
    team = span * rows
    per = heads // team
    size = slabs * rows
    slab = lax.axis_index("ctx")
    row = lax.axis_index("sub")
    odd = slab % span
    me = odd * rows + row

    def swap(value, d):
        if d == 0:
            return value
        return lax.ppermute(value, RING, [(i, i - i % team + (i % team ^ d)) for i in range(size)])

    def shift(value, way, flip=0):
        pairs = []
        for i in range(size):
            place = i % team // rows
            forward = (place == span - 1) if way == 0 else (place == 0)
            if span == 1:
                forward = way == 0
            j = i + team if forward else i - team
            if 0 <= j < size:
                pairs.append((i, j ^ flip))
        return lax.ppermute(value, RING, pairs)

    places = (window_tiles[0] // rows - slab + 1) * rows + window_tiles[0] % rows
    listed = jnp.arange(wmax) < window_count[0]
    flags = jnp.any(
        (places[None, :] == jnp.arange(3 * rows)[:, None]) & listed[None, :], axis=1
    ).astype(jnp.int32)

    members = jnp.arange(team, dtype=jnp.int32) ^ me
    sources = (keys, values, queries, grad_out)
    kinds = (0, 1, 2, 3)
    every = tuple(range(per))
    far = tuple(range(rows, team))
    step = tile // BLOCKS

    jobs = [(d, (0,), part, part[0] == 0) for part in ((0, 1), (2, 3)) for d in far]
    jobs += [(1, (0,), kinds, True), (0, (0,), kinds, True)]
    packed = pack(jobs, (0,), members, flags, sources, [])
    count = len(far)
    first_kv = [swap(packed[n], d) for n, d in enumerate(far)]
    first_qg = [swap(packed[count + n], d) for n, d in enumerate(far)]
    mates = {0: (packed[-1], swap(packed[-2], 1), 0)}
    sent = {}
    rest = every[1:]
    if rest:
        jobs = [(d, (c,), kinds, False) for c in rest for d in far]
        jobs += [(1, rest, kinds, False), (0, rest, kinds, False)]
        packed = pack(jobs, rest, members, flags, sources, [mates[0][1]])
        sent = {(c, d): packed[m * count + n] for m, c in enumerate(rest) for n, d in enumerate(far)}
        beside = swap(packed[-2], 1)
        mates.update({c: (packed[-1], beside, m) for m, c in enumerate(rest)})

    lists = list(mates[0][:2]) + first_kv
    table = jnp.stack([value[0, 0, -FLAG_ROWS, : 3 * rows] for value in lists]).astype(jnp.int32)
    table = table.reshape(team, 3, rows)
    table = jnp.where(row == 0, table, table[:, :, ::-1])
    if span == 2:
        turned = table[:, ::-1]
        table = jnp.concatenate(
            [
                jnp.where(odd == 0, table[:rows], turned[:rows]),
                jnp.where(odd == 0, turned[rows:], table[rows:]),
            ]
        )
    if span == 1:
        windows = ((1, 0, 2),)
        extras = (0, 0)
    else:
        windows = ((3, 0, 1), (2, 1, 0))
        extras = (0, 1)
    spots = jnp.repeat(jnp.asarray(windows, jnp.int32), rows, axis=0)
    table = jnp.concatenate([table.reshape(team, 3 * rows), spots], axis=1)

    arrived = {key: swap(value, key[1]) for key, value in sent.items()}
    halos = {}
    ready = {}
    worked = {}
    home = {}

    def pass_on(c, spare):
        pieces = first_kv if c == 0 else [arrived[c, d] for d in far]
        grads = worked[c - 2][2:] if c >= 2 else []
        payloads = relay(
            step, mates[c][2], mates[c][:2], pieces, [grads[1], grads[0]] if grads else [], spare
        )
        ready[c] = payloads[0]
        halos[c] = (shift(payloads[0], 0), shift(payloads[-1], 1))

    def finished(c, spare):
        done, local, grads_one, grads_two = worked[c]
        if c + 2 < per:
            grads = [(halos[c + 2][1], True), (halos[c + 2][0], True)]
        else:
            grads = [(shift(grads_one, 1), False), (shift(grads_two, 0), False)]
        pieces = finish(rows, extras, done, local, grads, spare)
        home[c] = [swap(piece, d) for d, piece in enumerate(pieces)]
        return pieces[0]

    pass_on(0, [])
    for c in every:
        inputs = []
        loads = []

        def add(value, held, wanted, slab_at, tiles):
            for at, (e, kind) in enumerate((e, kind) for e in tiles for kind in wanted):
                loads.append((len(inputs), at, kind, slab_at, e))
            inputs.append((value, held))

        for e in range(rows):
            add(mates[c][e], mates[c][2], "kvqg", 0, [e])
        for n in range(len(far)):
            if c == 0:
                add(first_kv[n], 0, "kv", 1, [n])
                add(first_qg[n], 0, "qg", 1, [n])
            else:
                add(arrived[c, far[n]], 0, "kvqg", 1, [n])
        for n in range(2):
            add(halos[c][n], 0, "kv", span + n, range(rows))
        spare = [ready[c + 1]] if 1 <= c < per - 1 else []
        if c >= 2:
            spare.append(finished(c - 2, [worked[c - 1][0]]))
        worked[c] = attend(rows, tile, span, table, tuple(loads), inputs, spare)
        if c == 0 and per > 1:
            pass_on(1, [worked[0][0]])
        if c + 2 < per:
            pass_on(c + 2, [])
    for c in every[-2:]:
        early = [k for k in (c - 2, c - 1) if k in home and (k == c - 2 or c == per - 1)]
        finished(c, [worked[per - 1][0]] + [home[k][d] for k in early for d in far])
    outs = None
    for c in every:
        outs = unpack(c, members, home[c], outs, queries.shape)
    attended, grad_queries, grad_keys, grad_values = outs
    return (attended, grad_queries, grad_keys, grad_values)


def solution(mesh):
    spec = P(("grp", "ctx", "sub"), None, "head")
    return jax.shard_map(
        body,
        mesh=mesh,
        in_specs=(spec, spec, spec, spec, P(("grp", "ctx", "sub"), None), P(("grp", "ctx", "sub"))),
        out_specs=(spec, spec, spec, spec),
        check_vma=False,
    )
```

```python
import functools
import math

import jax
import jax.numpy as jnp
from jax import lax
from jax.experimental import pallas as pl
from jax.experimental.pallas import tpu as pltpu
from jax.sharding import PartitionSpec as P

HD = 128
FLAG_ROWS = 16
BLOCKS = 4
RING = ("ctx", "sub")
F32 = jnp.float32
BF16 = jnp.bfloat16
SCALE = 1.0 / math.sqrt(HD)
FACTOR = SCALE * math.log2(math.e)
ANY = pl.BlockSpec(memory_space=pl.ANY)
SMEM = pl.BlockSpec(memory_space=pltpu.SMEM)
PARAMS = pltpu.CompilerParams(vmem_limit_bytes=36 * 1024 * 1024)
LIGHT = pltpu.CompilerParams(vmem_limit_bytes=20 * 1024 * 1024)


def struct(shape, dtype):
    return jax.ShapeDtypeStruct(shape, dtype)


def hbm(values):
    return [pltpu.with_memory_space_constraint(value, pltpu.HBM) for value in values]


def moved(nbytes):
    return pl.CostEstimate(flops=0, bytes_accessed=nbytes, transcendentals=0)


def pack_kernel(jobs, step, first, places_ref, flags_ref, *refs):
    sources, outs = refs[:4], refs[-len(jobs) :]
    lane = lax.broadcasted_iota(jnp.int32, (FLAG_ROWS, HD), 1)
    flags = jnp.zeros((FLAG_ROWS, HD), F32)
    for w in range(flags_ref.shape[0]):
        flags = jnp.where(lane == w, flags_ref[w].astype(F32), flags)
    flags = flags.astype(BF16)
    team = places_ref.shape[0]
    for out, (d, heads, kinds, flagged) in zip(outs, jobs):
        for m, c in enumerate(heads):
            lanes = pl.ds(pl.multiple_of(((c - first) * team + places_ref[d]) * HD, HD), HD)
            for at, n in enumerate(kinds):
                out[m, 0, pl.ds(at * step, step)] = sources[n][0, :, lanes]
            if flagged:
                out[m, 0, pl.ds(len(kinds) * step, FLAG_ROWS)] = flags


def pack(jobs, heads, places, flags, sources, spare, kept=jax.ShapeDtypeStruct):
    _, tile, lane_width = sources[0].shape
    step = tile // BLOCKS
    team = places.shape[0]
    first = heads[0]
    count = len(heads)
    wide = count * team * HD if first % count == 0 else lane_width
    block = first // count if first % count == 0 else 0
    start = first if first % count == 0 else 0
    shapes = [
        (len(held), BLOCKS, len(kinds) * step + (FLAG_ROWS if flagged else 0), HD)
        for _, held, kinds, flagged in jobs
    ]
    return pl.pallas_call(
        functools.partial(pack_kernel, jobs, step, start),
        grid=(BLOCKS,),
        out_shape=[kept(shape, BF16) for shape in shapes],
        in_specs=[SMEM, SMEM]
        + [pl.BlockSpec((1, step, wide), lambda i: (0, i, block))] * 4
        + [ANY] * len(spare),
        out_specs=[
            pl.BlockSpec((shape[0], 1, shape[2], HD), lambda i: (0, i, 0, 0)) for shape in shapes
        ],
        cost_estimate=moved(sum(4 * HD * math.prod(shape[:3]) for shape in shapes)),
        compiler_params=LIGHT,
        name="pack",
    )(places, flags, *hbm(sources), *spare)


def relay_kernel(step, rows, near, far, grads, outs):
    for out, pieces, grad in zip(outs, (near, far), grads):
        for e, (piece, at) in enumerate(pieces):
            out[0, :, pl.ds(2 * step * e, 2 * step)] = piece[at, :, pl.ds(0, 2 * step)]
        if grad is not None:
            for e in range(rows):
                for n in range(2):
                    for g in range(BLOCKS):
                        at = pl.ds((2 * rows + 2 * e + n) * step, step)
                        out[0, g, at] = grad[e, n, pl.ds(g * step, step)]


def relay(step, held, near, far, grads, spare, flagged=False):
    rows = len(near)
    kinds = 2 if far else 1
    high = (4 if grads else 2) * rows * step
    flag_sources = [*near, *far] if flagged else []

    def kernel(*refs):
        refs = list(refs)
        near_refs = [(refs.pop(0), 0) for _ in range(rows)]
        far_refs = [(refs.pop(0), 0) for _ in far]
        grad_refs = [refs.pop(0) for _ in grads] or [None] * kinds
        flag_refs = [refs.pop(0) for _ in flag_sources]
        outs = refs[len(spare) :]
        relay_kernel(step, rows, near_refs, far_refs, grad_refs, outs[:kinds])
        for d, ref in enumerate(flag_refs):
            outs[kinds][d] = ref[0, 0]

    def whole(shape):
        return pl.BlockSpec(shape, lambda i: (0,) * len(shape))

    shape = (1, BLOCKS, high, HD)
    return pl.pallas_call(
        kernel,
        grid=(1,),
        out_shape=[struct(shape, BF16)] * kinds
        + ([struct((len(flag_sources), FLAG_ROWS, HD), BF16)] if flagged else []),
        in_specs=[
            pl.BlockSpec((1, BLOCKS, 2 * step, HD), lambda i, at=at: (at, 0, 0, 0))
            for at in [held] * rows + [0] * len(far)
        ]
        + [whole(value.shape) for value in grads]
        + [
            pl.BlockSpec(
                (1, 1, FLAG_ROWS, HD),
                lambda i, at=value.shape[2] // FLAG_ROWS - 1: (0, 0, at, 0),
            )
            for value in flag_sources
        ]
        + [ANY] * len(spare),
        out_specs=[whole(shape)] * kinds
        + ([whole((len(flag_sources), FLAG_ROWS, HD))] if flagged else []),
        cost_estimate=moved(kinds * 4 * BLOCKS * high * HD),
        compiler_params=LIGHT,
        name="relay",
    )(*near, *far, *grads, *flag_sources, *spare)


def nt(a, b):
    return lax.dot_general(a, b, (((1,), (1,)), ((), ())), preferred_element_type=F32)


def nn(a, b):
    return jnp.dot(a, b, preferred_element_type=F32)


def attend_kernel(plan, rows, tile, table_ref, *refs):
    loads, slabs_here, n_in, spare = plan
    inputs = refs[:n_in]
    rest = refs[n_in + spare :]
    done, local, grads_one, grads_two = rest[:4]
    qbuf, gbuf, kbuf, vbuf, kt, vt, dk_t, dv_t, s_buf, p_buf, ds_buf, ot = rest[4:]
    targets = {"k": kbuf, "v": vbuf, "q": qbuf, "g": gbuf}
    step = tile // BLOCKS
    for n, at, kind, slab, e in loads:
        for g in range(BLOCKS):
            targets[kind][slab, pl.ds(e * tile + g * step, step)] = inputs[n][
                0, g, pl.ds(at * step, step)
            ]
    width = rows * tile
    team = slabs_here * rows
    places = kbuf.shape[0]

    def prepare(n, carry):
        kt[n] = kbuf[n].T
        vt[n] = vbuf[n].T
        dk_t[n] = jnp.zeros((HD, width), F32)
        dv_t[n] = jnp.zeros((HD, width), F32)
        return carry

    lax.fori_loop(0, places, prepare, 0)
    lane = lax.broadcasted_iota(jnp.int32, (1, width), 1)

    def slab_pass(a, carry):
        query = qbuf[a]
        grad = gbuf[a]

        blocks = range(3)
        spots = [table_ref[a * rows, 3 * rows + b] for b in blocks]
        top = jnp.full((1, width), -jnp.inf, F32)
        for b in blocks:
            for e in range(rows):
                at = pl.ds(e * tile, tile)
                keep = jnp.zeros((1, width), jnp.int32)
                for f in range(rows):
                    inside = (lane >= f * tile) & (lane < (f + 1) * tile)
                    keep = jnp.where(inside, table_ref[a * rows + f, b * rows + e], keep)
                mask = jnp.where(keep > 0, 0.0, -jnp.inf)
                s = nt(kbuf[spots[b], at], query) + mask
                s_buf[b, at] = s
                top = jnp.maximum(top, jnp.max(s, axis=0, keepdims=True))

        total = jnp.zeros((1, width), F32)
        for b in blocks:
            for e in range(rows):
                at = pl.ds(e * tile, tile)
                p = jnp.exp2((s_buf[b, at] - top) * FACTOR)
                total = total + jnp.sum(p, axis=0, keepdims=True)
                p_buf[b, at] = p.astype(BF16)
            term = nn(vt[spots[b]], p_buf[b])
            ot[...] = term if b == 0 else ot[...] + term
        inv = 1.0 / total
        low_t = (ot[...] * inv).astype(BF16)
        grad_t = grad.T.astype(F32)
        offset = jnp.sum(grad_t * low_t.astype(F32), axis=0, keepdims=True)
        grad_over = (grad_t * inv).astype(BF16)
        query_over = (query.T.astype(F32) * (inv * SCALE)).astype(BF16)
        out = low_t.T

        for b in blocks:
            for e in range(rows):
                at = pl.ds(e * tile, tile)
                dp = nt(vbuf[spots[b], at], grad)
                ds_buf[b, at] = p_buf[b, at] * (dp - offset).astype(BF16)
            dv_t[spots[b]] += nt(grad_over, p_buf[b])
            dk_t[spots[b]] += nt(query_over, ds_buf[b])
            term = nn(kt[spots[b]], ds_buf[b])
            ot[...] = term if b == 0 else ot[...] + term
        dq = (ot[...] * (inv * SCALE)).astype(BF16).T
        for f in range(rows):
            done[a * rows + f, 0] = out[f * tile : (f + 1) * tile]
            done[a * rows + f, 1] = dq[f * tile : (f + 1) * tile]
        return carry

    lax.fori_loop(0, slabs_here, slab_pass, 0)

    for n, sums in enumerate((dk_t, dv_t)):
        for d in range(team):
            local[d, n] = sums[d // rows, :, pl.ds(d % rows * tile, tile)].T
        for m, grads in enumerate((grads_one, grads_two)):
            for e in range(rows):
                terms = sums[slabs_here + m, :, pl.ds(e * tile, tile)]
                grads[e, n] = terms.astype(BF16).T


def attend(rows, tile, slabs_here, table, loads, inputs, spare):
    places = slabs_here + 2
    team = slabs_here * rows
    width = rows * tile
    scores = 3 * slabs_here * width * width

    def head_spec(value, c):
        return pl.BlockSpec((1,) + value.shape[1:], lambda i: (c, 0, 0, 0))

    def whole(shape):
        return pl.BlockSpec(shape, lambda i: (0,) * len(shape))

    shapes = [
        struct((team, 2, tile, HD), BF16),
        struct((team, 2, tile, HD), F32),
        struct((rows, 2, tile, HD), BF16),
        struct((rows, 2, tile, HD), BF16),
    ]
    plan = (loads, slabs_here, len(inputs), len(spare))
    return pl.pallas_call(
        functools.partial(attend_kernel, plan, rows, tile),
        grid=(1,),
        out_shape=shapes,
        in_specs=[SMEM] + [head_spec(value, c) for value, c in inputs] + [ANY] * len(spare),
        out_specs=[whole(shape.shape) for shape in shapes],
        scratch_shapes=[
            pltpu.VMEM((slabs_here, width, HD), BF16),
            pltpu.VMEM((slabs_here, width, HD), BF16),
            pltpu.VMEM((places, width, HD), BF16),
            pltpu.VMEM((places, width, HD), BF16),
            pltpu.VMEM((places, HD, width), BF16),
            pltpu.VMEM((places, HD, width), BF16),
            pltpu.VMEM((places, HD, width), F32),
            pltpu.VMEM((places, HD, width), F32),
            pltpu.VMEM((3, width, width), F32),
            pltpu.VMEM((3, width, width), BF16),
            pltpu.VMEM((3, width, width), BF16),
            pltpu.VMEM((HD, width), F32),
        ],
        cost_estimate=pl.CostEstimate(
            flops=12 * scores * HD, bytes_accessed=8 * 1024 * 1024, transcendentals=scores
        ),
        compiler_params=PARAMS,
        name="attend",
    )(table, *[value for value, _ in inputs], *spare)


def finish(rows, extras, done, local, grads, spare):
    team, _, tile, _ = done.shape
    step = tile // BLOCKS

    def kernel(done, local, *refs):
        terms, outs = refs[: len(grads)], refs[-team:]
        for d in range(team):
            out = outs[d].at[0]
            for n in range(2):
                out[n] = done[d, n]
                for g in range(BLOCKS):
                    at = pl.ds(g * step, step)
                    total = local[d, n, at]
                    for term, (_, packed), slab in zip(terms, grads, extras):
                        if d // rows != slab:
                            continue
                        if packed:
                            row = pl.ds((2 * (d % rows) + n) * step, step)
                            total = total + term[0, g, row].astype(F32)
                        else:
                            total = total + term[d % rows, n, at].astype(F32)
                    out[2 + n, at] = total.astype(BF16)

    def whole(shape):
        return pl.BlockSpec(shape, lambda i: (0,) * len(shape))

    def grad_spec(value, packed):
        if not packed:
            return whole(value.shape)
        return pl.BlockSpec((1, BLOCKS, 2 * rows * step, HD), lambda i: (0, 0, 1, 0))

    piece = (1, 4, tile, HD)
    return pl.pallas_call(
        kernel,
        grid=(1,),
        out_shape=[struct(piece, BF16)] * team,
        in_specs=[whole(done.shape), whole(local.shape)]
        + [grad_spec(*grad) for grad in grads]
        + [ANY] * len(spare),
        out_specs=[whole(piece)] * team,
        cost_estimate=moved(team * 24 * tile * HD),
        compiler_params=LIGHT,
        name="finish",
    )(done, local, *[value for value, _ in grads], *spare)


def unpack(c, places, pieces, outs, shape):
    tile = shape[1]
    step = tile // BLOCKS
    team = len(pieces)
    held = [] if outs is None else list(outs)

    def kernel(places_ref, *refs):
        for d in range(team):
            lanes = pl.ds(pl.multiple_of(places_ref[d] * HD, HD), HD)
            for n in range(4):
                refs[n - 4][0, :, lanes] = refs[d][0, n]

    return pl.pallas_call(
        kernel,
        grid=(BLOCKS,),
        out_shape=[struct(shape, BF16)] * 4,
        in_specs=[SMEM]
        + [pl.BlockSpec((1, 4, step, HD), lambda i: (0, 0, i, 0))] * team
        + [ANY] * len(held),
        out_specs=[pl.BlockSpec((1, step, team * HD), lambda i: (0, i, c))] * 4,
        input_output_aliases={1 + team + n: n for n in range(len(held))},
        cost_estimate=moved(16 * tile * team * HD),
        compiler_params=LIGHT,
        name="unpack",
    )(places, *pieces, *held)


def body(queries, keys, values, grad_out, window_tiles, window_count):
    rows_here, tile, lane_width = queries.shape
    wmax = window_tiles.shape[1]
    heads = lane_width // HD
    rows = lax.axis_size("sub")
    slabs = lax.axis_size("ctx")
    span = 2 if heads % (2 * rows) == 0 and slabs % 2 == 0 else 1
    team = span * rows
    per = heads // team
    size = slabs * rows
    slab = lax.axis_index("ctx")
    row = lax.axis_index("sub")
    odd = slab % span
    me = odd * rows + row

    def swap(value, d):
        if d == 0:
            return value
        return lax.ppermute(value, RING, [(i, i - i % team + (i % team ^ d)) for i in range(size)])

    def shift(value, way, flip=0):
        pairs = []
        for i in range(size):
            place = i % team // rows
            forward = (place == span - 1) if way == 0 else (place == 0)
            if span == 1:
                forward = way == 0
            j = i + team if forward else i - team
            if 0 <= j < size:
                pairs.append((i, j ^ flip))
        return lax.ppermute(value, RING, pairs)

    places = (window_tiles[0] // rows - slab + 1) * rows + window_tiles[0] % rows
    listed = jnp.arange(wmax) < window_count[0]
    flags = jnp.any(
        (places[None, :] == jnp.arange(3 * rows)[:, None]) & listed[None, :], axis=1
    ).astype(jnp.int32)

    members = jnp.arange(team, dtype=jnp.int32) ^ me
    sources = (keys, values, queries, grad_out)
    kinds = (0, 1, 2, 3)
    every = tuple(range(per))
    far = tuple(range(rows, team))
    step = tile // BLOCKS

    jobs = [(d, (0,), kinds, True) for d in (*far, 1, 0)]
    packed = pack(jobs, (0,), members, flags, sources, [])
    count = len(far)
    mates = {0: (packed[-1], swap(packed[-2], 1), 0)}
    sent = {(0, d): packed[n] for n, d in enumerate(far)}
    rest = every[1:]
    if rest:
        jobs = [(d, (c,), kinds, False) for c in rest for d in far]
        jobs += [(1, rest, kinds, False), (0, rest, kinds, False)]
        packed = pack(jobs, rest, members, flags, sources, [mates[0][1]], pltpu.HBM)
        sent.update(
            {(c, d): packed[m * count + n] for m, c in enumerate(rest) for n, d in enumerate(far)}
        )
        beside = swap(packed[-2], 1)
        mates.update({c: (packed[-1], beside, m) for m, c in enumerate(rest)})

    arrived = {key: swap(value, key[1]) for key, value in sent.items()}
    halos = {}
    ready = {}
    worked = {}
    home = {}

    def pass_on(c, spare):
        pieces = [arrived[c, d] for d in far]
        grads = [worked[c - 2][3], worked[c - 2][2]] if c >= 2 else []
        outs = relay(step, mates[c][2], mates[c][:2], pieces, grads, spare, c == 0)
        ready[c] = outs[0]
        halos[c] = (shift(outs[0], 0), shift(outs[span - 1], 1))
        return outs[-1]

    def finished(c, spare):
        done, local, grads_one, grads_two = worked[c]
        if c + 2 < per:
            grads = [(halos[c + 2][1], True), (halos[c + 2][0], True)]
        else:
            grads = [(shift(grads_one, 1), False), (shift(grads_two, 0), False)]
        pieces = finish(rows, extras, done, local, grads, spare)
        home[c] = [swap(piece, d) for d, piece in enumerate(pieces)]
        return pieces[0]

    all_flags = pass_on(0, hbm([packed[0]]))
    if per > 1:
        pass_on(1, [ready[0]])
    table = all_flags[:, 0, : 3 * rows].astype(jnp.int32)
    table = table.reshape(team, 3, rows)
    table = jnp.where(row == 0, table, table[:, :, ::-1])
    if span == 2:
        turned = table[:, ::-1]
        table = jnp.concatenate(
            [
                jnp.where(odd == 0, table[:rows], turned[:rows]),
                jnp.where(odd == 0, turned[rows:], table[rows:]),
            ]
        )
    if span == 1:
        windows = ((1, 0, 2),)
        extras = (0, 0)
    else:
        windows = ((3, 0, 1), (2, 1, 0))
        extras = (0, 1)
    spots = jnp.repeat(jnp.asarray(windows, jnp.int32), rows, axis=0)
    table = jnp.concatenate([table.reshape(team, 3 * rows), spots], axis=1)

    for c in every:
        inputs = []
        loads = []

        def add(value, held, wanted, slab_at, tiles):
            for at, (e, kind) in enumerate((e, kind) for e in tiles for kind in wanted):
                loads.append((len(inputs), at, kind, slab_at, e))
            inputs.append((value, held))

        for e in range(rows):
            add(mates[c][e], mates[c][2], "kvqg", 0, [e])
        for n in range(len(far)):
            add(arrived[c, far[n]], 0, "kvqg", 1, [n])
        for n in range(2):
            add(halos[c][n], 0, "kv", span + n, range(rows))
        spare = [ready[c + 1]] if c < per - 1 else []
        if c >= 2:
            spare.append(finished(c - 2, [worked[c - 1][0]]))
        worked[c] = attend(rows, tile, span, table, tuple(loads), inputs, spare)
        if c + 2 < per:
            pass_on(c + 2, [])
    for c in every[-2:]:
        early = [k for k in (c - 2, c - 1) if k in home and (k == c - 2 or c == per - 1)]
        finished(c, [worked[per - 1][0]] + [home[k][d] for k in early for d in far])
    outs = None
    for c in every:
        outs = unpack(c, members, home[c], outs, queries.shape)
    attended, grad_queries, grad_keys, grad_values = outs
    return (attended, grad_queries, grad_keys, grad_values)


def solution(mesh):
    spec = P(("grp", "ctx", "sub"), None, "head")
    return jax.shard_map(
        body,
        mesh=mesh,
        in_specs=(spec, spec, spec, spec, P(("grp", "ctx", "sub"), None), P(("grp", "ctx", "sub"))),
        out_specs=(spec, spec, spec, spec),
        check_vma=False,
    )
```

```python
import functools
import math

import jax
import jax.numpy as jnp
from jax import lax
from jax.experimental import pallas as pl
from jax.experimental.pallas import tpu as pltpu
from jax.sharding import PartitionSpec as P

HD = 128
FLAG_ROWS = 16
BLOCKS = 4
RING = ("ctx", "sub")
F32 = jnp.float32
BF16 = jnp.bfloat16
SCALE = 1.0 / math.sqrt(HD)
FACTOR = SCALE * math.log2(math.e)
ANY = pl.BlockSpec(memory_space=pl.ANY)
SMEM = pl.BlockSpec(memory_space=pltpu.SMEM)
PARAMS = pltpu.CompilerParams(vmem_limit_bytes=36 * 1024 * 1024)
LIGHT = pltpu.CompilerParams(vmem_limit_bytes=20 * 1024 * 1024)


def struct(shape, dtype):
    return jax.ShapeDtypeStruct(shape, dtype)


def hbm(values):
    return [pltpu.with_memory_space_constraint(value, pltpu.HBM) for value in values]


def moved(nbytes):
    return pl.CostEstimate(flops=0, bytes_accessed=nbytes, transcendentals=0)


def pack_kernel(jobs, step, first, places_ref, flags_ref, *refs):
    sources, outs = refs[:4], refs[-len(jobs) :]
    lane = lax.broadcasted_iota(jnp.int32, (FLAG_ROWS, HD), 1)
    flags = jnp.zeros((FLAG_ROWS, HD), F32)
    for w in range(flags_ref.shape[0]):
        flags = jnp.where(lane == w, flags_ref[w].astype(F32), flags)
    flags = flags.astype(BF16)
    team = places_ref.shape[0]
    for out, (d, heads, kinds, flagged) in zip(outs, jobs):
        for m, c in enumerate(heads):
            lanes = pl.ds(pl.multiple_of(((c - first) * team + places_ref[d]) * HD, HD), HD)
            for at, n in enumerate(kinds):
                out[m, 0, pl.ds(at * step, step)] = sources[n][0, :, lanes]
            if flagged:
                out[m, 0, pl.ds(len(kinds) * step, FLAG_ROWS)] = flags


def pack(jobs, heads, places, flags, sources, spare, kept=jax.ShapeDtypeStruct):
    _, tile, lane_width = sources[0].shape
    step = tile // BLOCKS
    team = places.shape[0]
    first = heads[0]
    count = len(heads)
    wide = count * team * HD if first % count == 0 else lane_width
    block = first // count if first % count == 0 else 0
    start = first if first % count == 0 else 0
    shapes = [
        (len(held), BLOCKS, len(kinds) * step + (FLAG_ROWS if flagged else 0), HD)
        for _, held, kinds, flagged in jobs
    ]
    return pl.pallas_call(
        functools.partial(pack_kernel, jobs, step, start),
        grid=(BLOCKS,),
        out_shape=[kept(shape, BF16) for shape in shapes],
        in_specs=[SMEM, SMEM]
        + [pl.BlockSpec((1, step, wide), lambda i: (0, i, block))] * 4
        + [ANY] * len(spare),
        out_specs=[
            pl.BlockSpec((shape[0], 1, shape[2], HD), lambda i: (0, i, 0, 0)) for shape in shapes
        ],
        cost_estimate=moved(sum(4 * HD * math.prod(shape[:3]) for shape in shapes)),
        compiler_params=LIGHT,
        name="pack",
    )(places, flags, *hbm(sources), *spare)


def relay_kernel(step, rows, near, far, grads, outs):
    for out, pieces, grad in zip(outs, (near, far), grads):
        for e, (piece, at) in enumerate(pieces):
            out[0, :, pl.ds(2 * step * e, 2 * step)] = piece[at, :, pl.ds(0, 2 * step)]
        if grad is not None:
            for e in range(rows):
                for n in range(2):
                    for g in range(BLOCKS):
                        at = pl.ds((2 * rows + 2 * e + n) * step, step)
                        out[0, g, at] = grad[e, n, pl.ds(g * step, step)]


def relay(step, held, near, far, grads, spare, flagged=False):
    rows = len(near)
    kinds = 2 if far else 1
    high = (4 if grads else 2) * rows * step
    flag_sources = [*near, *far] if flagged else []

    def kernel(*refs):
        refs = list(refs)
        near_refs = [(refs.pop(0), 0) for _ in range(rows)]
        far_refs = [(refs.pop(0), 0) for _ in far]
        grad_refs = [refs.pop(0) for _ in grads] or [None] * kinds
        flag_refs = [refs.pop(0) for _ in flag_sources]
        outs = refs[len(spare) :]
        relay_kernel(step, rows, near_refs, far_refs, grad_refs, outs[:kinds])
        for d, ref in enumerate(flag_refs):
            outs[kinds][d] = ref[0, 0]

    def whole(shape):
        return pl.BlockSpec(shape, lambda i: (0,) * len(shape))

    shape = (1, BLOCKS, high, HD)
    return pl.pallas_call(
        kernel,
        grid=(1,),
        out_shape=[struct(shape, BF16)] * kinds
        + ([struct((len(flag_sources), FLAG_ROWS, HD), BF16)] if flagged else []),
        in_specs=[
            pl.BlockSpec((1, BLOCKS, 2 * step, HD), lambda i, at=at: (at, 0, 0, 0))
            for at in [held] * rows + [0] * len(far)
        ]
        + [whole(value.shape) for value in grads]
        + [
            pl.BlockSpec(
                (1, 1, FLAG_ROWS, HD),
                lambda i, at=value.shape[2] // FLAG_ROWS - 1: (0, 0, at, 0),
            )
            for value in flag_sources
        ]
        + [ANY] * len(spare),
        out_specs=[whole(shape)] * kinds
        + ([whole((len(flag_sources), FLAG_ROWS, HD))] if flagged else []),
        cost_estimate=moved(kinds * 4 * BLOCKS * high * HD),
        compiler_params=LIGHT,
        name="relay",
    )(*near, *far, *grads, *flag_sources, *spare)


def nt(a, b):
    return lax.dot_general(a, b, (((1,), (1,)), ((), ())), preferred_element_type=F32)


def nn(a, b):
    return jnp.dot(a, b, preferred_element_type=F32)


def attend_kernel(plan, rows, tile, table_ref, *refs):
    loads, slabs_here, n_in, spare = plan
    inputs = refs[:n_in]
    rest = refs[n_in + spare :]
    done, local, grads_one, grads_two = rest[:4]
    qbuf, gbuf, kbuf, vbuf, kt, vt, dk_t, dv_t, s_buf, p_buf, ds_buf, ot = rest[4:]
    targets = {"k": kbuf, "v": vbuf, "q": qbuf, "g": gbuf}
    step = tile // BLOCKS
    for n, at, kind, slab, e in loads:
        for g in range(BLOCKS):
            targets[kind][slab, pl.ds(e * tile + g * step, step)] = inputs[n][
                0, g, pl.ds(at * step, step)
            ]
    width = rows * tile
    team = slabs_here * rows
    places = kbuf.shape[0]

    def prepare(n, carry):
        kt[n] = kbuf[n].T
        vt[n] = vbuf[n].T
        dk_t[n] = jnp.zeros((HD, width), F32)
        dv_t[n] = jnp.zeros((HD, width), F32)
        return carry

    lax.fori_loop(0, places, prepare, 0)
    lane = lax.broadcasted_iota(jnp.int32, (1, width), 1)

    every = [(a, b) for a in range(slabs_here) for b in range(3)]
    spots = {(a, b): table_ref[a * rows, 3 * rows + b] for a, b in every}
    queries = [qbuf[a] for a in range(slabs_here)]
    grads_in = [gbuf[a] for a in range(slabs_here)]
    top = [jnp.full((1, width), -jnp.inf, F32) for _ in range(slabs_here)]
    total = [jnp.zeros((1, width), F32) for _ in range(slabs_here)]
    late = {}

    def by_query(a, b, e, seen, unseen):
        keep = jnp.zeros((1, width), jnp.int32)
        for f in range(rows):
            inside = (lane >= f * tile) & (lane < (f + 1) * tile)
            keep = jnp.where(inside, table_ref[a * rows + f, b * rows + e], keep)
        return jnp.where(keep > 0, seen, unseen)

    def scores(a, b):
        for e in range(rows):
            at = pl.ds(e * tile, tile)
            s = nt(kbuf[spots[a, b], at], queries[a])
            s_buf[a, b, at] = s
            best = jnp.max(s, axis=0, keepdims=True)
            top[a] = jnp.maximum(top[a], by_query(a, b, e, best, -jnp.inf))

    def expo(a, b):
        for e in range(rows):
            at = pl.ds(e * tile, tile)
            p = jnp.exp2((s_buf[a, b, at] - by_query(a, b, e, top[a], jnp.inf)) * FACTOR)
            total[a] = total[a] + jnp.sum(p, axis=0, keepdims=True)
            p_buf[a, b, at] = p.astype(BF16)
        term = nn(vt[spots[a, b]], p_buf[a, b])
        ot[a] = term if b == 0 else ot[a] + term

    def between(a):
        inv = 1.0 / total[a]
        low_t = (ot[a] * inv).astype(BF16)
        grad_t = grads_in[a].T.astype(F32)
        offset = jnp.sum(grad_t * low_t.astype(F32), axis=0, keepdims=True)
        grad_over = (grad_t * inv).astype(BF16)
        query_over = (queries[a].T.astype(F32) * (inv * SCALE)).astype(BF16)
        out = low_t.T
        for f in range(rows):
            done[a * rows + f, 0] = out[f * tile : (f + 1) * tile]
        late[a] = (inv, offset, grad_over, query_over)

    def backward(a, b):
        inv, offset, grad_over, query_over = late[a]
        place = spots[a, b]
        for e in range(rows):
            at = pl.ds(e * tile, tile)
            dp = nt(vbuf[place, at], grads_in[a])
            ds_buf[b % 2, at] = p_buf[a, b, at] * (dp - offset).astype(BF16)
        dv_t[place] += nt(grad_over, p_buf[a, b])
        dk_t[place] += nt(query_over, ds_buf[b % 2])
        term = nn(kt[place], ds_buf[b % 2])
        ot[a] = term if b == 0 else ot[a] + term
        if b == 2:
            dq = (ot[a] * (inv * SCALE)).astype(BF16).T
            for f in range(rows):
                done[a * rows + f, 1] = dq[f * tile : (f + 1) * tile]

    for turn in range(slabs_here + 2):
        for b in range(3):
            for a in range(slabs_here):
                if turn - a == 2 and b == 0:
                    between(a)
                if 0 <= turn - a <= 2:
                    (scores, expo, backward)[turn - a](a, b)

    for n, sums in enumerate((dk_t, dv_t)):
        for d in range(team):
            local[d, n] = sums[d // rows, :, pl.ds(d % rows * tile, tile)].T
        for m, grads in enumerate((grads_one, grads_two)):
            for e in range(rows):
                terms = sums[slabs_here + m, :, pl.ds(e * tile, tile)]
                grads[e, n] = terms.astype(BF16).T


def attend(rows, tile, slabs_here, table, loads, inputs, spare):
    places = slabs_here + 2
    team = slabs_here * rows
    width = rows * tile
    scores = 3 * slabs_here * width * width

    def head_spec(value, c):
        shape = (1,) + value.shape[1:]
        return pl.BlockSpec(shape, lambda i: (c, 0, 0, 0), pipeline_mode=pl.Buffered(1))

    def whole(shape):
        return pl.BlockSpec(shape, lambda i: (0,) * len(shape), pipeline_mode=pl.Buffered(1))

    shapes = [
        struct((team, 2, tile, HD), BF16),
        struct((team, 2, tile, HD), F32),
        struct((rows, 2, tile, HD), BF16),
        struct((rows, 2, tile, HD), BF16),
    ]
    plan = (loads, slabs_here, len(inputs), len(spare))
    return pl.pallas_call(
        functools.partial(attend_kernel, plan, rows, tile),
        grid=(1,),
        out_shape=shapes,
        in_specs=[SMEM] + [head_spec(value, c) for value, c in inputs] + [ANY] * len(spare),
        out_specs=[whole(shape.shape) for shape in shapes],
        scratch_shapes=[
            pltpu.VMEM((slabs_here, width, HD), BF16),
            pltpu.VMEM((slabs_here, width, HD), BF16),
            pltpu.VMEM((places, width, HD), BF16),
            pltpu.VMEM((places, width, HD), BF16),
            pltpu.VMEM((places, HD, width), BF16),
            pltpu.VMEM((places, HD, width), BF16),
            pltpu.VMEM((places, HD, width), F32),
            pltpu.VMEM((places, HD, width), F32),
            pltpu.VMEM((slabs_here, 3, width, width), F32),
            pltpu.VMEM((slabs_here, 3, width, width), BF16),
            pltpu.VMEM((2, width, width), BF16),
            pltpu.VMEM((slabs_here, HD, width), F32),
        ],
        cost_estimate=pl.CostEstimate(
            flops=12 * scores * HD, bytes_accessed=8 * 1024 * 1024, transcendentals=scores
        ),
        compiler_params=PARAMS,
        name="attend",
    )(table, *[value for value, _ in inputs], *spare)


def finish(rows, extras, done, local, grads, spare):
    team, _, tile, _ = done.shape
    step = tile // BLOCKS

    def kernel(done, local, *refs):
        terms, outs = refs[: len(grads)], refs[-team:]
        for d in range(team):
            out = outs[d].at[0]
            for n in range(2):
                out[n] = done[d, n]
                for g in range(BLOCKS):
                    at = pl.ds(g * step, step)
                    total = local[d, n, at]
                    for term, (_, packed), slab in zip(terms, grads, extras):
                        if d // rows != slab:
                            continue
                        if packed:
                            row = pl.ds((2 * (d % rows) + n) * step, step)
                            total = total + term[0, g, row].astype(F32)
                        else:
                            total = total + term[d % rows, n, at].astype(F32)
                    out[2 + n, at] = total.astype(BF16)

    def whole(shape):
        return pl.BlockSpec(shape, lambda i: (0,) * len(shape))

    def grad_spec(value, packed):
        if not packed:
            return whole(value.shape)
        return pl.BlockSpec((1, BLOCKS, 2 * rows * step, HD), lambda i: (0, 0, 1, 0))

    piece = (1, 4, tile, HD)
    return pl.pallas_call(
        kernel,
        grid=(1,),
        out_shape=[struct(piece, BF16)] * team,
        in_specs=[whole(done.shape), whole(local.shape)]
        + [grad_spec(*grad) for grad in grads]
        + [ANY] * len(spare),
        out_specs=[whole(piece)] * team,
        cost_estimate=moved(team * 24 * tile * HD),
        compiler_params=LIGHT,
        name="finish",
    )(done, local, *[value for value, _ in grads], *spare)


def unpack(c, places, pieces, outs, shape):
    tile = shape[1]
    step = tile // BLOCKS
    team = len(pieces)
    held = [] if outs is None else list(outs)

    def kernel(places_ref, *refs):
        for d in range(team):
            lanes = pl.ds(pl.multiple_of(places_ref[d] * HD, HD), HD)
            for n in range(4):
                refs[n - 4][0, :, lanes] = refs[d][0, n]

    return pl.pallas_call(
        kernel,
        grid=(BLOCKS,),
        out_shape=[struct(shape, BF16)] * 4,
        in_specs=[SMEM]
        + [pl.BlockSpec((1, 4, step, HD), lambda i: (0, 0, i, 0))] * team
        + [ANY] * len(held),
        out_specs=[pl.BlockSpec((1, step, team * HD), lambda i: (0, i, c))] * 4,
        input_output_aliases={1 + team + n: n for n in range(len(held))},
        cost_estimate=moved(16 * tile * team * HD),
        compiler_params=LIGHT,
        name="unpack",
    )(places, *pieces, *held)


def body(queries, keys, values, grad_out, window_tiles, window_count):
    rows_here, tile, lane_width = queries.shape
    wmax = window_tiles.shape[1]
    heads = lane_width // HD
    rows = lax.axis_size("sub")
    slabs = lax.axis_size("ctx")
    span = 2 if heads % (2 * rows) == 0 and slabs % 2 == 0 else 1
    team = span * rows
    per = heads // team
    size = slabs * rows
    slab = lax.axis_index("ctx")
    row = lax.axis_index("sub")
    odd = slab % span
    me = odd * rows + row

    def swap(value, d):
        if d == 0:
            return value
        return lax.ppermute(value, RING, [(i, i - i % team + (i % team ^ d)) for i in range(size)])

    def shift(value, way, flip=0):
        pairs = []
        for i in range(size):
            place = i % team // rows
            forward = (place == span - 1) if way == 0 else (place == 0)
            if span == 1:
                forward = way == 0
            j = i + team if forward else i - team
            if 0 <= j < size:
                pairs.append((i, j ^ flip))
        return lax.ppermute(value, RING, pairs)

    places = (window_tiles[0] // rows - slab + 1) * rows + window_tiles[0] % rows
    listed = jnp.arange(wmax) < window_count[0]
    flags = jnp.any(
        (places[None, :] == jnp.arange(3 * rows)[:, None]) & listed[None, :], axis=1
    ).astype(jnp.int32)

    members = jnp.arange(team, dtype=jnp.int32) ^ me
    sources = (keys, values, queries, grad_out)
    kinds = (0, 1, 2, 3)
    every = tuple(range(per))
    far = tuple(range(rows, team))
    step = tile // BLOCKS

    jobs = [(d, (0,), kinds, True) for d in (*far, 1, 0)]
    packed = pack(jobs, (0,), members, flags, sources, [])
    count = len(far)
    mates = {0: (packed[-1], swap(packed[-2], 1), 0)}
    sent = {(0, d): packed[n] for n, d in enumerate(far)}
    rest = every[1:]
    if rest:
        jobs = [(d, (c,), kinds, False) for c in rest for d in far]
        jobs += [(1, rest, kinds, False), (0, rest, kinds, False)]
        packed = pack(jobs, rest, members, flags, sources, [mates[0][1]], pltpu.HBM)
        sent.update(
            {(c, d): packed[m * count + n] for m, c in enumerate(rest) for n, d in enumerate(far)}
        )
        beside = swap(packed[-2], 1)
        mates.update({c: (packed[-1], beside, m) for m, c in enumerate(rest)})

    arrived = {key: swap(value, key[1]) for key, value in sent.items()}
    halos = {}
    ready = {}
    worked = {}
    home = {}

    def pass_on(c, spare):
        pieces = [arrived[c, d] for d in far]
        grads = [worked[c - 2][3], worked[c - 2][2]] if c >= 2 else []
        outs = relay(step, mates[c][2], mates[c][:2], pieces, grads, spare, c == 0)
        ready[c] = outs[0]
        halos[c] = (shift(outs[0], 0), shift(outs[span - 1], 1))
        return outs[-1]

    def finished(c, spare):
        done, local, grads_one, grads_two = worked[c]
        if c + 2 < per:
            grads = [(halos[c + 2][1], True), (halos[c + 2][0], True)]
        else:
            grads = [(shift(grads_one, 1), False), (shift(grads_two, 0), False)]
        pieces = finish(rows, extras, done, local, grads, spare)
        home[c] = [swap(piece, d) for d, piece in enumerate(pieces)]
        return pieces[0]

    all_flags = pass_on(0, hbm([packed[0]]))
    if per > 1:
        pass_on(1, [ready[0]])
    table = all_flags[:, 0, : 3 * rows].astype(jnp.int32)
    table = table.reshape(team, 3, rows)
    table = jnp.where(row == 0, table, table[:, :, ::-1])
    if span == 2:
        turned = table[:, ::-1]
        table = jnp.concatenate(
            [
                jnp.where(odd == 0, table[:rows], turned[:rows]),
                jnp.where(odd == 0, turned[rows:], table[rows:]),
            ]
        )
    if span == 1:
        windows = ((1, 0, 2),)
        extras = (0, 0)
    else:
        windows = ((3, 0, 1), (2, 1, 0))
        extras = (0, 1)
    spots = jnp.repeat(jnp.asarray(windows, jnp.int32), rows, axis=0)
    table = jnp.concatenate([table.reshape(team, 3 * rows), spots], axis=1)

    for c in every:
        inputs = []
        loads = []

        def add(value, held, wanted, slab_at, tiles):
            for at, (e, kind) in enumerate((e, kind) for e in tiles for kind in wanted):
                loads.append((len(inputs), at, kind, slab_at, e))
            inputs.append((value, held))

        for e in range(rows):
            add(mates[c][e], mates[c][2], "kvqg", 0, [e])
        for n in range(len(far)):
            add(arrived[c, far[n]], 0, "kvqg", 1, [n])
        for n in range(2):
            add(halos[c][n], 0, "kv", span + n, range(rows))
        spare = [ready[c + 1]] if c < per - 1 else []
        if c >= 2:
            spare.append(finished(c - 2, [worked[c - 1][0]]))
        worked[c] = attend(rows, tile, span, table, tuple(loads), inputs, spare)
        if c + 2 < per:
            pass_on(c + 2, [])
    for c in every[-2:]:
        early = [k for k in (c - 2, c - 1) if k in home and (k == c - 2 or c == per - 1)]
        gone = [home[k][d] for k in early for d in (far if k == c - 2 else far[:1])]
        finished(c, [worked[per - 1][0]] + gone)
    outs = None
    for c in every:
        outs = unpack(c, members, home[c], outs, queries.shape)
    attended, grad_queries, grad_keys, grad_values = outs
    return (attended, grad_queries, grad_keys, grad_values)


def solution(mesh):
    spec = P(("grp", "ctx", "sub"), None, "head")
    return jax.shard_map(
        body,
        mesh=mesh,
        in_specs=(spec, spec, spec, spec, P(("grp", "ctx", "sub"), None), P(("grp", "ctx", "sub"))),
        out_specs=(spec, spec, spec, spec),
        check_vma=False,
    )
```

```python
import functools
import math

import jax
import jax.numpy as jnp
from jax import lax
from jax.experimental import pallas as pl
from jax.experimental.pallas import tpu as pltpu
from jax.sharding import PartitionSpec as P

HD = 128
FLAG_ROWS = 16
BLOCKS = 4
RING = ("ctx", "sub")
F32 = jnp.float32
BF16 = jnp.bfloat16
SCALE = 1.0 / math.sqrt(HD)
FACTOR = SCALE * math.log2(math.e)
ANY = pl.BlockSpec(memory_space=pl.ANY)
SMEM = pl.BlockSpec(memory_space=pltpu.SMEM)
PARAMS = pltpu.CompilerParams(vmem_limit_bytes=36 * 1024 * 1024)
LIGHT = pltpu.CompilerParams(vmem_limit_bytes=20 * 1024 * 1024)


def struct(shape, dtype):
    return jax.ShapeDtypeStruct(shape, dtype)


def hbm(values):
    return [pltpu.with_memory_space_constraint(value, pltpu.HBM) for value in values]


def moved(nbytes):
    return pl.CostEstimate(flops=0, bytes_accessed=nbytes, transcendentals=0)


def pack_kernel(jobs, step, first, places_ref, flags_ref, *refs):
    sources, outs = refs[:4], refs[-len(jobs) :]
    lane = lax.broadcasted_iota(jnp.int32, (FLAG_ROWS, HD), 1)
    flags = jnp.zeros((FLAG_ROWS, HD), F32)
    for w in range(flags_ref.shape[0]):
        flags = jnp.where(lane == w, flags_ref[w].astype(F32), flags)
    flags = flags.astype(BF16)
    team = places_ref.shape[0]
    for out, (d, heads, kinds, flagged) in zip(outs, jobs):
        for m, c in enumerate(heads):
            lanes = pl.ds(pl.multiple_of(((c - first) * team + places_ref[d]) * HD, HD), HD)
            for at, n in enumerate(kinds):
                out[m, 0, pl.ds(at * step, step)] = sources[n][0, :, lanes]
            if flagged:
                out[m, 0, pl.ds(len(kinds) * step, FLAG_ROWS)] = flags


def pack(jobs, heads, places, flags, sources, spare, kept=jax.ShapeDtypeStruct):
    _, tile, lane_width = sources[0].shape
    step = tile // BLOCKS
    team = places.shape[0]
    first = heads[0]
    count = len(heads)
    wide = count * team * HD if first % count == 0 else lane_width
    block = first // count if first % count == 0 else 0
    start = first if first % count == 0 else 0
    shapes = [
        (len(held), BLOCKS, len(kinds) * step + (FLAG_ROWS if flagged else 0), HD)
        for _, held, kinds, flagged in jobs
    ]
    return pl.pallas_call(
        functools.partial(pack_kernel, jobs, step, start),
        grid=(BLOCKS,),
        out_shape=[kept(shape, BF16) for shape in shapes],
        in_specs=[SMEM, SMEM]
        + [pl.BlockSpec((1, step, wide), lambda i: (0, i, block))] * 4
        + [ANY] * len(spare),
        out_specs=[
            pl.BlockSpec((shape[0], 1, shape[2], HD), lambda i: (0, i, 0, 0)) for shape in shapes
        ],
        cost_estimate=moved(sum(4 * HD * math.prod(shape[:3]) for shape in shapes)),
        compiler_params=LIGHT,
        name="pack",
    )(places, flags, *hbm(sources), *spare)


def relay_kernel(step, rows, near, far, grads, outs):
    for out, pieces, grad in zip(outs, (near, far), grads):
        for e, (piece, at) in enumerate(pieces):
            out[0, :, pl.ds(2 * step * e, 2 * step)] = piece[at, :, pl.ds(0, 2 * step)]
        if grad is not None:
            for e in range(rows):
                for n in range(2):
                    for g in range(BLOCKS):
                        at = pl.ds((2 * rows + 2 * e + n) * step, step)
                        out[0, g, at] = grad[e, n, pl.ds(g * step, step)]


def relay(step, held, near, far, grads, spare, flagged=False, kept=jax.ShapeDtypeStruct):
    rows = len(near)
    kinds = 2 if far else 1
    high = (4 if grads else 2) * rows * step
    flag_sources = [*near, *far] if flagged else []

    def kernel(*refs):
        refs = list(refs)
        near_refs = [(refs.pop(0), 0) for _ in range(rows)]
        far_refs = [(refs.pop(0), 0) for _ in far]
        grad_refs = [refs.pop(0) for _ in grads] or [None] * kinds
        flag_refs = [refs.pop(0) for _ in flag_sources]
        outs = refs[len(spare) :]
        relay_kernel(step, rows, near_refs, far_refs, grad_refs, outs[:kinds])
        for d, ref in enumerate(flag_refs):
            outs[kinds][d] = ref[0, 0]

    def whole(shape):
        return pl.BlockSpec(shape, lambda i: (0,) * len(shape))

    shape = (1, BLOCKS, high, HD)
    return pl.pallas_call(
        kernel,
        grid=(1,),
        out_shape=[kept(shape, BF16)] * kinds
        + ([struct((len(flag_sources), FLAG_ROWS, HD), BF16)] if flagged else []),
        in_specs=[
            pl.BlockSpec((1, BLOCKS, 2 * step, HD), lambda i, at=at: (at, 0, 0, 0))
            for at in [held] * rows + [0] * len(far)
        ]
        + [whole(value.shape) for value in grads]
        + [
            pl.BlockSpec(
                (1, 1, FLAG_ROWS, HD),
                lambda i, at=value.shape[2] // FLAG_ROWS - 1: (0, 0, at, 0),
            )
            for value in flag_sources
        ]
        + [ANY] * len(spare),
        out_specs=[whole(shape)] * kinds
        + ([whole((len(flag_sources), FLAG_ROWS, HD))] if flagged else []),
        cost_estimate=moved(kinds * 4 * BLOCKS * high * HD),
        compiler_params=LIGHT,
        name="relay",
    )(*near, *far, *grads, *flag_sources, *spare)


def nt(a, b):
    return lax.dot_general(a, b, (((1,), (1,)), ((), ())), preferred_element_type=F32)


def nn(a, b):
    return jnp.dot(a, b, preferred_element_type=F32)


def attend_kernel(plan, rows, tile, table_ref, *refs):
    loads, slabs_here, n_in, spare = plan
    inputs = refs[:n_in]
    rest = refs[n_in + spare :]
    done, local, grads_one, grads_two = rest[:4]
    qbuf, gbuf, kbuf, vbuf, kt, vt, dk_t, dv_t, s_buf, p_buf, ds_buf, ot = rest[4:]
    targets = {"k": kbuf, "v": vbuf, "q": qbuf, "g": gbuf}
    step = tile // BLOCKS
    for n, at, kind, slab, e in loads:
        for g in range(BLOCKS):
            targets[kind][slab, pl.ds(e * tile + g * step, step)] = inputs[n][
                0, g, pl.ds(at * step, step)
            ]
    width = rows * tile
    team = slabs_here * rows
    places = kbuf.shape[0]

    def prepare(n, carry):
        kt[n] = kbuf[n].T
        vt[n] = vbuf[n].T
        dk_t[n] = jnp.zeros((HD, width), F32)
        dv_t[n] = jnp.zeros((HD, width), F32)
        return carry

    lax.fori_loop(0, places, prepare, 0)
    lane = lax.broadcasted_iota(jnp.int32, (1, width), 1)

    queries = [qbuf[a] for a in range(slabs_here)]
    grads_in = [gbuf[a] for a in range(slabs_here)]
    late = {}

    def spot(a, b):
        return table_ref[a * rows, 3 * rows + b]

    def by_query(a, b, e, seen, unseen):
        keep = jnp.zeros((1, width), jnp.int32)
        for f in range(rows):
            inside = (lane >= f * tile) & (lane < (f + 1) * tile)
            keep = jnp.where(inside, table_ref[a * rows + f, b * rows + e], keep)
        return jnp.where(keep > 0, seen, unseen)

    def scores(a, b, top):
        for e in range(rows):
            at = pl.ds(e * tile, tile)
            s = nt(kbuf[spot(a, b), at], queries[a])
            s_buf[a, b, at] = s
            best = jnp.max(s, axis=0, keepdims=True)
            top = jnp.maximum(top, by_query(a, b, e, best, -jnp.inf))
        return top

    def expo(a, b, top, total):
        for e in range(rows):
            at = pl.ds(e * tile, tile)
            p = jnp.exp2((s_buf[a, b, at] - by_query(a, b, e, top, jnp.inf)) * FACTOR)
            total = total + jnp.sum(p, axis=0, keepdims=True)
            p_buf[a, b, at] = p.astype(BF16)
        ot[a] += nn(vt[spot(a, b)], p_buf[a, b])
        return total

    def between(a, total):
        inv = 1.0 / total
        low_t = (ot[a] * inv).astype(BF16)
        grad_t = grads_in[a].T.astype(F32)
        offset = jnp.sum(grad_t * low_t.astype(F32), axis=0, keepdims=True)
        grad_over = (grad_t * inv).astype(BF16)
        query_over = (queries[a].T.astype(F32) * (inv * SCALE)).astype(BF16)
        out = low_t.T
        for f in range(rows):
            done[a * rows + f, 0] = out[f * tile : (f + 1) * tile]
        ot[a] = jnp.zeros((HD, width), F32)
        late[a] = (inv, offset, grad_over, query_over)

    def backward(a, b):
        _, offset, grad_over, query_over = late[a]
        place = spot(a, b)
        for e in range(rows):
            at = pl.ds(e * tile, tile)
            dp = nt(vbuf[place, at], grads_in[a])
            ds_buf[at] = p_buf[a, b, at] * (dp - offset).astype(BF16)
        dv_t[place] += nt(grad_over, p_buf[a, b])
        dk_t[place] += nt(query_over, ds_buf[...])
        ot[a] += nn(kt[place], ds_buf[...])

    def after(a):
        dq = (ot[a] * (late[a][0] * SCALE)).astype(BF16).T
        for f in range(rows):
            done[a * rows + f, 1] = dq[f * tile : (f + 1) * tile]

    tops = [jnp.full((1, width), -jnp.inf, F32) for _ in range(slabs_here)]
    totals = [jnp.zeros((1, width), F32) for _ in range(slabs_here)]
    for a in range(slabs_here):
        ot[a] = jnp.zeros((HD, width), F32)
    for turn in range(slabs_here + 2):
        here = [a for a in range(slabs_here) if 0 <= turn - a <= 2]

        def blocks(b, carry, turn=turn, here=here):
            tops, totals = list(carry[0]), list(carry[1])
            for a in here:
                if turn - a == 0:
                    tops[a] = scores(a, b, tops[a])
                elif turn - a == 1:
                    totals[a] = expo(a, b, tops[a], totals[a])
                else:
                    backward(a, b)
            return tuple(tops), tuple(totals)

        tops, totals = lax.fori_loop(0, 3, blocks, (tuple(tops), tuple(totals)))
        for a in here:
            if turn - a == 1:
                between(a, totals[a])
            elif turn - a == 2:
                after(a)

    for n, sums in enumerate((dk_t, dv_t)):
        for d in range(team):
            local[d, n] = sums[d // rows, :, pl.ds(d % rows * tile, tile)].T
        for m, grads in enumerate((grads_one, grads_two)):
            for e in range(rows):
                terms = sums[slabs_here + m, :, pl.ds(e * tile, tile)]
                grads[e, n] = terms.astype(BF16).T


def attend(rows, tile, slabs_here, table, loads, inputs, spare):
    places = slabs_here + 2
    team = slabs_here * rows
    width = rows * tile
    scores = 3 * slabs_here * width * width

    def head_spec(value, c):
        shape = (1,) + value.shape[1:]
        return pl.BlockSpec(shape, lambda i: (c, 0, 0, 0), pipeline_mode=pl.Buffered(1))

    def whole(shape):
        return pl.BlockSpec(shape, lambda i: (0,) * len(shape), pipeline_mode=pl.Buffered(1))

    shapes = [
        struct((team, 2, tile, HD), BF16),
        struct((team, 2, tile, HD), F32),
        struct((rows, 2, tile, HD), BF16),
        struct((rows, 2, tile, HD), BF16),
    ]
    plan = (loads, slabs_here, len(inputs), len(spare))
    return pl.pallas_call(
        functools.partial(attend_kernel, plan, rows, tile),
        grid=(1,),
        out_shape=shapes,
        in_specs=[SMEM] + [head_spec(value, c) for value, c in inputs] + [ANY] * len(spare),
        out_specs=[whole(shape.shape) for shape in shapes],
        scratch_shapes=[
            pltpu.VMEM((slabs_here, width, HD), BF16),
            pltpu.VMEM((slabs_here, width, HD), BF16),
            pltpu.VMEM((places, width, HD), BF16),
            pltpu.VMEM((places, width, HD), BF16),
            pltpu.VMEM((places, HD, width), BF16),
            pltpu.VMEM((places, HD, width), BF16),
            pltpu.VMEM((places, HD, width), F32),
            pltpu.VMEM((places, HD, width), F32),
            pltpu.VMEM((slabs_here, 3, width, width), F32),
            pltpu.VMEM((slabs_here, 3, width, width), BF16),
            pltpu.VMEM((width, width), BF16),
            pltpu.VMEM((slabs_here, HD, width), F32),
        ],
        cost_estimate=pl.CostEstimate(
            flops=12 * scores * HD, bytes_accessed=8 * 1024 * 1024, transcendentals=scores
        ),
        compiler_params=PARAMS,
        name="attend",
    )(table, *[value for value, _ in inputs], *spare)


def finish(rows, extras, done, local, grads, spare):
    team, _, tile, _ = done.shape
    step = tile // BLOCKS

    def kernel(done, local, *refs):
        terms, outs = refs[: len(grads)], refs[-team:]
        for d in range(team):
            out = outs[d].at[0]
            for n in range(2):
                out[n] = done[d, n]
                for g in range(BLOCKS):
                    at = pl.ds(g * step, step)
                    total = local[d, n, at]
                    for term, (_, packed), slab in zip(terms, grads, extras):
                        if d // rows != slab:
                            continue
                        if packed:
                            row = pl.ds((2 * (d % rows) + n) * step, step)
                            total = total + term[0, g, row].astype(F32)
                        else:
                            total = total + term[d % rows, n, at].astype(F32)
                    out[2 + n, at] = total.astype(BF16)

    def whole(shape):
        return pl.BlockSpec(shape, lambda i: (0,) * len(shape))

    def grad_spec(value, packed):
        if not packed:
            return whole(value.shape)
        return pl.BlockSpec((1, BLOCKS, 2 * rows * step, HD), lambda i: (0, 0, 1, 0))

    piece = (1, 4, tile, HD)
    return pl.pallas_call(
        kernel,
        grid=(1,),
        out_shape=[struct(piece, BF16)] * team,
        in_specs=[whole(done.shape), whole(local.shape)]
        + [grad_spec(*grad) for grad in grads]
        + [ANY] * len(spare),
        out_specs=[whole(piece)] * team,
        cost_estimate=moved(team * 24 * tile * HD),
        compiler_params=LIGHT,
        name="finish",
    )(done, local, *[value for value, _ in grads], *spare)


def unpack(c, places, pieces, outs, shape):
    tile = shape[1]
    step = tile // BLOCKS
    team = len(pieces)
    held = [] if outs is None else list(outs)

    def kernel(places_ref, *refs):
        for d in range(team):
            lanes = pl.ds(pl.multiple_of(places_ref[d] * HD, HD), HD)
            for n in range(4):
                refs[n - 4][0, :, lanes] = refs[d][0, n]

    return pl.pallas_call(
        kernel,
        grid=(BLOCKS,),
        out_shape=[struct(shape, BF16)] * 4,
        in_specs=[SMEM]
        + [pl.BlockSpec((1, 4, step, HD), lambda i: (0, 0, i, 0))] * team
        + [ANY] * len(held),
        out_specs=[pl.BlockSpec((1, step, team * HD), lambda i: (0, i, c))] * 4,
        input_output_aliases={1 + team + n: n for n in range(len(held))},
        cost_estimate=moved(16 * tile * team * HD),
        compiler_params=LIGHT,
        name="unpack",
    )(places, *pieces, *held)


def body(queries, keys, values, grad_out, window_tiles, window_count):
    rows_here, tile, lane_width = queries.shape
    wmax = window_tiles.shape[1]
    heads = lane_width // HD
    rows = lax.axis_size("sub")
    slabs = lax.axis_size("ctx")
    span = 2 if heads % (2 * rows) == 0 and slabs % 2 == 0 else 1
    team = span * rows
    per = heads // team
    size = slabs * rows
    slab = lax.axis_index("ctx")
    row = lax.axis_index("sub")
    odd = slab % span
    me = odd * rows + row

    def swap(value, d):
        if d == 0:
            return value
        return lax.ppermute(value, RING, [(i, i - i % team + (i % team ^ d)) for i in range(size)])

    def shift(value, way, flip=0):
        pairs = []
        for i in range(size):
            place = i % team // rows
            forward = (place == span - 1) if way == 0 else (place == 0)
            if span == 1:
                forward = way == 0
            j = i + team if forward else i - team
            if 0 <= j < size:
                pairs.append((i, j ^ flip))
        return lax.ppermute(value, RING, pairs)

    places = (window_tiles[0] // rows - slab + 1) * rows + window_tiles[0] % rows
    listed = jnp.arange(wmax) < window_count[0]
    flags = jnp.any(
        (places[None, :] == jnp.arange(3 * rows)[:, None]) & listed[None, :], axis=1
    ).astype(jnp.int32)

    members = jnp.arange(team, dtype=jnp.int32) ^ me
    sources = (keys, values, queries, grad_out)
    kinds = (0, 1, 2, 3)
    every = tuple(range(per))
    far = tuple(range(rows, team))
    step = tile // BLOCKS

    jobs = [(d, (0,), kinds, True) for d in (*far, 1, 0)]
    packed = pack(jobs, (0,), members, flags, sources, [])
    count = len(far)
    mates = {0: (packed[-1], swap(packed[-2], 1), 0)}
    sent = {(0, d): packed[n] for n, d in enumerate(far)}
    rest = every[1:]
    if rest:
        jobs = [(d, (c,), kinds, False) for c in rest for d in far]
        jobs += [(1, rest, kinds, False), (0, rest, kinds, False)]
        packed = pack(jobs, rest, members, flags, sources, [mates[0][1]], pltpu.HBM)
        sent.update(
            {(c, d): packed[m * count + n] for m, c in enumerate(rest) for n, d in enumerate(far)}
        )
        beside = swap(packed[-2], 1)
        mates.update({c: (packed[-1], beside, m) for m, c in enumerate(rest)})

    arrived = {key: swap(value, key[1]) for key, value in sent.items()}
    halos = {}
    ready = {}
    worked = {}
    home = {}

    def pass_on(c, spare):
        pieces = [arrived[c, d] for d in far]
        if c == 0:
            pieces = hbm(pieces)
        kept = pltpu.HBM if c < 2 else jax.ShapeDtypeStruct
        grads = [worked[c - 2][3], worked[c - 2][2]] if c >= 2 else []
        outs = relay(step, mates[c][2], mates[c][:2], pieces, grads, spare, c == 0, kept)
        ready[c] = outs[0]
        halos[c] = (shift(outs[0], 0), shift(outs[span - 1], 1))
        return outs[-1]

    def finished(c, spare):
        done, local, grads_one, grads_two = worked[c]
        if c + 2 < per:
            grads = [(halos[c + 2][1], True), (halos[c + 2][0], True)]
        else:
            grads = [(shift(grads_one, 1), False), (shift(grads_two, 0), False)]
        pieces = finish(rows, extras, done, local, grads, spare)
        home[c] = [swap(piece, d) for d, piece in enumerate(pieces)]
        return pieces[0]

    all_flags = pass_on(0, hbm([packed[0]]))
    if per > 1:
        pass_on(1, hbm([ready[0]]))
    table = all_flags[:, 0, : 3 * rows].astype(jnp.int32)
    table = table.reshape(team, 3, rows)
    table = jnp.where(row == 0, table, table[:, :, ::-1])
    if span == 2:
        turned = table[:, ::-1]
        table = jnp.concatenate(
            [
                jnp.where(odd == 0, table[:rows], turned[:rows]),
                jnp.where(odd == 0, turned[rows:], table[rows:]),
            ]
        )
    if span == 1:
        windows = ((1, 0, 2),)
        extras = (0, 0)
    else:
        windows = ((3, 0, 1), (2, 1, 0))
        extras = (0, 1)
    spots = jnp.repeat(jnp.asarray(windows, jnp.int32), rows, axis=0)
    table = jnp.concatenate([table.reshape(team, 3 * rows), spots], axis=1)

    for c in every:
        inputs = []
        loads = []

        def add(value, held, wanted, slab_at, tiles):
            for at, (e, kind) in enumerate((e, kind) for e in tiles for kind in wanted):
                loads.append((len(inputs), at, kind, slab_at, e))
            inputs.append((value, held))

        for e in range(rows):
            add(mates[c][e], mates[c][2], "kvqg", 0, [e])
        for n in range(len(far)):
            piece = arrived[c, far[n]]
            add(hbm([piece])[0] if c == 0 else piece, 0, "kvqg", 1, [n])
        for n in range(2):
            add(halos[c][n], 0, "kv", span + n, range(rows))
        spare = [ready[c + 1]] if c < per - 1 else []
        if c == 0:
            spare = hbm(spare)
        if c >= 2:
            spare.append(finished(c - 2, [worked[c - 1][0]]))
        if c >= 3:
            spare += home[c - 3][1:]
        worked[c] = attend(rows, tile, span, table, tuple(loads), inputs, spare)
        if c + 2 < per:
            pass_on(c + 2, [])
    for c in every[-2:]:
        early = [k for k in (c - 2, c - 1) if k in home and (k == c - 2 or c == per - 1)]
        gone = [home[k][d] for k in early for d in (range(1, team) if k == c - 2 else far[:1])]
        finished(c, [worked[per - 1][0]] + gone)
    outs = None
    for c in every:
        outs = unpack(c, members, home[c], outs, queries.shape)
    attended, grad_queries, grad_keys, grad_values = outs
    return (attended, grad_queries, grad_keys, grad_values)


def solution(mesh):
    spec = P(("grp", "ctx", "sub"), None, "head")
    return jax.shard_map(
        body,
        mesh=mesh,
        in_specs=(spec, spec, spec, spec, P(("grp", "ctx", "sub"), None), P(("grp", "ctx", "sub"))),
        out_specs=(spec, spec, spec, spec),
        check_vma=False,
    )
```

```python
import functools
import math

import jax
import jax.numpy as jnp
from jax import lax
from jax.experimental import pallas as pl
from jax.experimental.pallas import tpu as pltpu
from jax.sharding import PartitionSpec as P

HD = 128
FLAG_ROWS = 16
BLOCKS = 4
RING = ("ctx", "sub")
F32 = jnp.float32
BF16 = jnp.bfloat16
SCALE = 1.0 / math.sqrt(HD)
FACTOR = SCALE * math.log2(math.e)
ANY = pl.BlockSpec(memory_space=pl.ANY)
SMEM = pl.BlockSpec(memory_space=pltpu.SMEM)
PARAMS = pltpu.CompilerParams(vmem_limit_bytes=36 * 1024 * 1024)
LIGHT = pltpu.CompilerParams(vmem_limit_bytes=20 * 1024 * 1024)


def struct(shape, dtype):
    return jax.ShapeDtypeStruct(shape, dtype)


def hbm(values):
    return [pltpu.with_memory_space_constraint(value, pltpu.HBM) for value in values]


def moved(nbytes):
    return pl.CostEstimate(flops=0, bytes_accessed=nbytes, transcendentals=0)


def pack_kernel(jobs, step, first, places_ref, flags_ref, *refs):
    sources, outs = refs[:4], refs[-len(jobs) :]
    lane = lax.broadcasted_iota(jnp.int32, (FLAG_ROWS, HD), 1)
    flags = jnp.zeros((FLAG_ROWS, HD), F32)
    for w in range(flags_ref.shape[0]):
        flags = jnp.where(lane == w, flags_ref[w].astype(F32), flags)
    flags = flags.astype(BF16)
    team = places_ref.shape[0]
    for out, (d, heads, kinds, flagged) in zip(outs, jobs):
        for m, c in enumerate(heads):
            lanes = pl.ds(pl.multiple_of(((c - first) * team + places_ref[d]) * HD, HD), HD)
            for at, n in enumerate(kinds):
                out[m, 0, pl.ds(at * step, step)] = sources[n][0, :, lanes]
            if flagged:
                out[m, 0, pl.ds(len(kinds) * step, FLAG_ROWS)] = flags


def pack(jobs, heads, places, flags, sources, spare, kept=jax.ShapeDtypeStruct):
    _, tile, lane_width = sources[0].shape
    step = tile // BLOCKS
    team = places.shape[0]
    first = heads[0]
    count = len(heads)
    wide = count * team * HD if first % count == 0 else lane_width
    block = first // count if first % count == 0 else 0
    start = first if first % count == 0 else 0
    shapes = [
        (len(held), BLOCKS, len(kinds) * step + (FLAG_ROWS if flagged else 0), HD)
        for _, held, kinds, flagged in jobs
    ]
    return pl.pallas_call(
        functools.partial(pack_kernel, jobs, step, start),
        grid=(BLOCKS,),
        out_shape=[kept(shape, BF16) for shape in shapes],
        in_specs=[SMEM, SMEM]
        + [pl.BlockSpec((1, step, wide), lambda i: (0, i, block))] * 4
        + [ANY] * len(spare),
        out_specs=[
            pl.BlockSpec((shape[0], 1, shape[2], HD), lambda i: (0, i, 0, 0)) for shape in shapes
        ],
        cost_estimate=moved(sum(4 * HD * math.prod(shape[:3]) for shape in shapes)),
        compiler_params=LIGHT,
        name="pack",
    )(places, flags, *hbm(sources), *spare)


def relay_kernel(step, rows, near, far, grads, outs):
    for out, pieces, grad in zip(outs, (near, far), grads):
        for e, (piece, at) in enumerate(pieces):
            out[0, :, pl.ds(2 * step * e, 2 * step)] = piece[at, :, pl.ds(0, 2 * step)]
        if grad is not None:
            for e in range(rows):
                for n in range(2):
                    for g in range(BLOCKS):
                        at = pl.ds((2 * rows + 2 * e + n) * step, step)
                        out[0, g, at] = grad[e, n, pl.ds(g * step, step)]


def relay(step, held, near, far, grads, spare, flagged=False, kept=jax.ShapeDtypeStruct):
    rows = len(near)
    kinds = 2 if far else 1
    high = (4 if grads else 2) * rows * step
    flag_sources = [*near, *far] if flagged else []

    def kernel(*refs):
        refs = list(refs)
        near_refs = [(refs.pop(0), 0) for _ in range(rows)]
        far_refs = [(refs.pop(0), 0) for _ in far]
        grad_refs = [refs.pop(0) for _ in grads] or [None] * kinds
        flag_refs = [refs.pop(0) for _ in flag_sources]
        outs = refs[len(spare) :]
        relay_kernel(step, rows, near_refs, far_refs, grad_refs, outs[:kinds])
        for d, ref in enumerate(flag_refs):
            outs[kinds][d] = ref[0, 0]

    def whole(shape):
        return pl.BlockSpec(shape, lambda i: (0,) * len(shape))

    shape = (1, BLOCKS, high, HD)
    return pl.pallas_call(
        kernel,
        grid=(1,),
        out_shape=[kept(shape, BF16)] * kinds
        + ([struct((len(flag_sources), FLAG_ROWS, HD), BF16)] if flagged else []),
        in_specs=[
            pl.BlockSpec((1, BLOCKS, 2 * step, HD), lambda i, at=at: (at, 0, 0, 0))
            for at in [held] * rows + [0] * len(far)
        ]
        + [whole(value.shape) for value in grads]
        + [
            pl.BlockSpec(
                (1, 1, FLAG_ROWS, HD),
                lambda i, at=value.shape[2] // FLAG_ROWS - 1: (0, 0, at, 0),
            )
            for value in flag_sources
        ]
        + [ANY] * len(spare),
        out_specs=[whole(shape)] * kinds
        + ([whole((len(flag_sources), FLAG_ROWS, HD))] if flagged else []),
        cost_estimate=moved(kinds * 4 * BLOCKS * high * HD),
        compiler_params=LIGHT,
        name="relay",
    )(*near, *far, *grads, *flag_sources, *spare)


def nt(a, b):
    return lax.dot_general(a, b, (((1,), (1,)), ((), ())), preferred_element_type=F32)


def nn(a, b):
    return jnp.dot(a, b, preferred_element_type=F32)


def attend_kernel(plan, rows, tile, table_ref, *refs):
    loads, slabs_here, n_in, spare = plan
    inputs = refs[:n_in]
    rest = refs[n_in + spare :]
    done, local, grads_one, grads_two = rest[:4]
    qbuf, gbuf, kbuf, vbuf, kt, vt, dk_t, dv_t, s_buf, p_buf, ds_buf, ot = rest[4:]
    targets = {"k": kbuf, "v": vbuf, "q": qbuf, "g": gbuf}
    step = tile // BLOCKS

    def load(g, carry):
        for n, at, kind, slab, e in loads:
            to = pl.ds(pl.multiple_of(e * tile + g * step, step), step)
            targets[kind][slab, to] = inputs[n][0, g, pl.ds(at * step, step)]
        return carry

    lax.fori_loop(0, BLOCKS, load, 0)
    width = rows * tile
    team = slabs_here * rows
    places = kbuf.shape[0]

    def prepare(n, carry):
        kt[n] = kbuf[n].T
        vt[n] = vbuf[n].T
        dk_t[n] = jnp.zeros((HD, width), F32)
        dv_t[n] = jnp.zeros((HD, width), F32)
        return carry

    lax.fori_loop(0, places, prepare, 0)
    lane = lax.broadcasted_iota(jnp.int32, (1, width), 1)

    queries = [qbuf[a] for a in range(slabs_here)]
    grads_in = [gbuf[a] for a in range(slabs_here)]
    late = {}

    def spot(a, b):
        return table_ref[a * rows, 3 * rows + b]

    def by_query(a, b, e, seen, unseen):
        keep = jnp.zeros((1, width), jnp.int32)
        for f in range(rows):
            inside = (lane >= f * tile) & (lane < (f + 1) * tile)
            keep = jnp.where(inside, table_ref[a * rows + f, b * rows + e], keep)
        return jnp.where(keep > 0, seen, unseen)

    def scores(a, b, top):
        for e in range(rows):
            at = pl.ds(e * tile, tile)
            s = nt(kbuf[spot(a, b), at], queries[a])
            s_buf[a, b, at] = s
            best = jnp.max(s, axis=0, keepdims=True)
            top = jnp.maximum(top, by_query(a, b, e, best, -jnp.inf))
        return top

    def expo(a, b, top, total):
        for e in range(rows):
            at = pl.ds(e * tile, tile)
            p = jnp.exp2((s_buf[a, b, at] - by_query(a, b, e, top, jnp.inf)) * FACTOR)
            total = total + jnp.sum(p, axis=0, keepdims=True)
            p_buf[a, b, at] = p.astype(BF16)
        ot[a] += nn(vt[spot(a, b)], p_buf[a, b])
        return total

    def between(a, total):
        inv = 1.0 / total
        low_t = (ot[a] * inv).astype(BF16)
        grad_t = grads_in[a].T.astype(F32)
        offset = jnp.sum(grad_t * low_t.astype(F32), axis=0, keepdims=True)
        grad_over = (grad_t * inv).astype(BF16)
        query_over = (queries[a].T.astype(F32) * (inv * SCALE)).astype(BF16)
        out = low_t.T
        for f in range(rows):
            done[a * rows + f, 0] = out[f * tile : (f + 1) * tile]
        ot[a] = jnp.zeros((HD, width), F32)
        late[a] = (inv, offset, grad_over, query_over)

    def backward(a, b):
        _, offset, grad_over, query_over = late[a]
        place = spot(a, b)
        for e in range(rows):
            at = pl.ds(e * tile, tile)
            dp = nt(vbuf[place, at], grads_in[a])
            ds_buf[at] = p_buf[a, b, at] * (dp - offset).astype(BF16)
        dv_t[place] += nt(grad_over, p_buf[a, b])
        dk_t[place] += nt(query_over, ds_buf[...])
        ot[a] += nn(kt[place], ds_buf[...])

    def after(a):
        dq = (ot[a] * (late[a][0] * SCALE)).astype(BF16).T
        for f in range(rows):
            done[a * rows + f, 1] = dq[f * tile : (f + 1) * tile]

    tops = [jnp.full((1, width), -jnp.inf, F32) for _ in range(slabs_here)]
    totals = [jnp.zeros((1, width), F32) for _ in range(slabs_here)]
    for a in range(slabs_here):
        ot[a] = jnp.zeros((HD, width), F32)
    for turn in range(slabs_here + 2):
        here = [a for a in range(slabs_here) if 0 <= turn - a <= 2]

        def blocks(b, carry, turn=turn, here=here):
            tops, totals = list(carry[0]), list(carry[1])
            for a in here:
                if turn - a == 0:
                    tops[a] = scores(a, b, tops[a])
                elif turn - a == 1:
                    totals[a] = expo(a, b, tops[a], totals[a])
                else:
                    backward(a, b)
            return tuple(tops), tuple(totals)

        carry = (tuple(tops), tuple(totals))
        if turn in (0, 3):
            for b in range(3):
                carry = blocks(b, carry)
        else:
            carry = lax.fori_loop(0, 3, blocks, carry)
        tops, totals = carry
        for a in here:
            if turn - a == 1:
                between(a, totals[a])
            elif turn - a == 2:
                after(a)

    def give(e, carry):
        at = pl.ds(pl.multiple_of(e * tile, tile), tile)
        for n, sums in enumerate((dk_t, dv_t)):
            for a in range(slabs_here):
                local[a * rows + e, n] = sums[a, :, at].T
            for m, grads in enumerate((grads_one, grads_two)):
                grads[e, n] = sums[slabs_here + m, :, at].astype(BF16).T
        return carry

    lax.fori_loop(0, rows, give, 0)


def attend(rows, tile, slabs_here, table, loads, inputs, spare):
    places = slabs_here + 2
    team = slabs_here * rows
    width = rows * tile
    scores = 3 * slabs_here * width * width

    def head_spec(value, c):
        shape = (1,) + value.shape[1:]
        return pl.BlockSpec(shape, lambda i: (c, 0, 0, 0), pipeline_mode=pl.Buffered(1))

    def whole(shape):
        return pl.BlockSpec(shape, lambda i: (0,) * len(shape), pipeline_mode=pl.Buffered(1))

    shapes = [
        struct((team, 2, tile, HD), BF16),
        struct((team, 2, tile, HD), F32),
        struct((rows, 2, tile, HD), BF16),
        struct((rows, 2, tile, HD), BF16),
    ]
    plan = (loads, slabs_here, len(inputs), len(spare))
    return pl.pallas_call(
        functools.partial(attend_kernel, plan, rows, tile),
        grid=(1,),
        out_shape=shapes,
        in_specs=[SMEM] + [head_spec(value, c) for value, c in inputs] + [ANY] * len(spare),
        out_specs=[whole(shape.shape) for shape in shapes],
        scratch_shapes=[
            pltpu.VMEM((slabs_here, width, HD), BF16),
            pltpu.VMEM((slabs_here, width, HD), BF16),
            pltpu.VMEM((places, width, HD), BF16),
            pltpu.VMEM((places, width, HD), BF16),
            pltpu.VMEM((places, HD, width), BF16),
            pltpu.VMEM((places, HD, width), BF16),
            pltpu.VMEM((places, HD, width), F32),
            pltpu.VMEM((places, HD, width), F32),
            pltpu.VMEM((slabs_here, 3, width, width), F32),
            pltpu.VMEM((slabs_here, 3, width, width), BF16),
            pltpu.VMEM((width, width), BF16),
            pltpu.VMEM((slabs_here, HD, width), F32),
        ],
        cost_estimate=pl.CostEstimate(
            flops=12 * scores * HD, bytes_accessed=8 * 1024 * 1024, transcendentals=scores
        ),
        compiler_params=PARAMS,
        name="attend",
    )(table, *[value for value, _ in inputs], *spare)


def finish(rows, extras, done, local, grads, spare):
    team, _, tile, _ = done.shape
    step = tile // BLOCKS

    def kernel(done, local, *refs):
        terms, outs = refs[: len(grads)], refs[-team:]
        for d in range(team):
            out = outs[d].at[0]
            for n in range(2):
                out[n] = done[d, n]
                for g in range(BLOCKS):
                    at = pl.ds(g * step, step)
                    total = local[d, n, at]
                    for term, (_, packed), slab in zip(terms, grads, extras):
                        if d // rows != slab:
                            continue
                        if packed:
                            row = pl.ds((2 * (d % rows) + n) * step, step)
                            total = total + term[0, g, row].astype(F32)
                        else:
                            total = total + term[d % rows, n, at].astype(F32)
                    out[2 + n, at] = total.astype(BF16)

    def whole(shape):
        return pl.BlockSpec(shape, lambda i: (0,) * len(shape))

    def grad_spec(value, packed):
        if not packed:
            return whole(value.shape)
        return pl.BlockSpec((1, BLOCKS, 2 * rows * step, HD), lambda i: (0, 0, 1, 0))

    piece = (1, 4, tile, HD)
    return pl.pallas_call(
        kernel,
        grid=(1,),
        out_shape=[struct(piece, BF16)] * team,
        in_specs=[whole(done.shape), whole(local.shape)]
        + [grad_spec(*grad) for grad in grads]
        + [ANY] * len(spare),
        out_specs=[whole(piece)] * team,
        cost_estimate=moved(team * 24 * tile * HD),
        compiler_params=LIGHT,
        name="finish",
    )(done, local, *[value for value, _ in grads], *spare)


def unpack(c, places, pieces, outs, shape):
    tile = shape[1]
    step = tile // BLOCKS
    team = len(pieces)
    held = [] if outs is None else list(outs)

    def kernel(places_ref, *refs):
        for d in range(team):
            lanes = pl.ds(pl.multiple_of(places_ref[d] * HD, HD), HD)
            for n in range(4):
                refs[n - 4][0, :, lanes] = refs[d][0, n]

    return pl.pallas_call(
        kernel,
        grid=(BLOCKS,),
        out_shape=[struct(shape, BF16)] * 4,
        in_specs=[SMEM]
        + [pl.BlockSpec((1, 4, step, HD), lambda i: (0, 0, i, 0))] * team
        + [ANY] * len(held),
        out_specs=[pl.BlockSpec((1, step, team * HD), lambda i: (0, i, c))] * 4,
        input_output_aliases={1 + team + n: n for n in range(len(held))},
        cost_estimate=moved(16 * tile * team * HD),
        compiler_params=LIGHT,
        name="unpack",
    )(places, *pieces, *held)


def body(queries, keys, values, grad_out, window_tiles, window_count):
    rows_here, tile, lane_width = queries.shape
    wmax = window_tiles.shape[1]
    heads = lane_width // HD
    rows = lax.axis_size("sub")
    slabs = lax.axis_size("ctx")
    span = 2 if heads % (2 * rows) == 0 and slabs % 2 == 0 else 1
    team = span * rows
    per = heads // team
    size = slabs * rows
    slab = lax.axis_index("ctx")
    row = lax.axis_index("sub")
    odd = slab % span
    me = odd * rows + row

    def swap(value, d):
        if d == 0:
            return value
        return lax.ppermute(value, RING, [(i, i - i % team + (i % team ^ d)) for i in range(size)])

    def shift(value, way, flip=0):
        pairs = []
        for i in range(size):
            place = i % team // rows
            forward = (place == span - 1) if way == 0 else (place == 0)
            if span == 1:
                forward = way == 0
            j = i + team if forward else i - team
            if 0 <= j < size:
                pairs.append((i, j ^ flip))
        return lax.ppermute(value, RING, pairs)

    places = (window_tiles[0] // rows - slab + 1) * rows + window_tiles[0] % rows
    listed = jnp.arange(wmax) < window_count[0]
    flags = jnp.any(
        (places[None, :] == jnp.arange(3 * rows)[:, None]) & listed[None, :], axis=1
    ).astype(jnp.int32)

    members = jnp.arange(team, dtype=jnp.int32) ^ me
    sources = (keys, values, queries, grad_out)
    kinds = (0, 1, 2, 3)
    every = tuple(range(per))
    far = tuple(range(rows, team))
    step = tile // BLOCKS

    jobs = [(d, (0,), kinds, True) for d in (*far, 1, 0)]
    packed = pack(jobs, (0,), members, flags, sources, [])
    count = len(far)
    mates = {0: (packed[-1], swap(packed[-2], 1), 0)}
    sent = {(0, d): packed[n] for n, d in enumerate(far)}
    rest = every[1:]
    if rest:
        jobs = [(d, (c,), kinds, False) for c in rest for d in far]
        jobs += [(1, rest, kinds, False), (0, rest, kinds, False)]
        packed = pack(jobs, rest, members, flags, sources, [mates[0][1]], pltpu.HBM)
        sent.update(
            {(c, d): packed[m * count + n] for m, c in enumerate(rest) for n, d in enumerate(far)}
        )
        beside = swap(packed[-2], 1)
        mates.update({c: (packed[-1], beside, m) for m, c in enumerate(rest)})

    arrived = {key: swap(value, key[1]) for key, value in sent.items()}
    halos = {}
    ready = {}
    worked = {}
    home = {}

    def pass_on(c, spare):
        pieces = [arrived[c, d] for d in far]
        if c == 0:
            pieces = hbm(pieces)
        kept = pltpu.HBM if c < 2 else jax.ShapeDtypeStruct
        grads = [worked[c - 2][3], worked[c - 2][2]] if c >= 2 else []
        outs = relay(step, mates[c][2], mates[c][:2], pieces, grads, spare, c == 0, kept)
        ready[c] = outs[0]
        halos[c] = (shift(outs[0], 0), shift(outs[span - 1], 1))
        return outs[-1]

    def finished(c, spare):
        done, local, grads_one, grads_two = worked[c]
        if c + 2 < per:
            grads = [(halos[c + 2][1], True), (halos[c + 2][0], True)]
        else:
            grads = [(shift(grads_one, 1), False), (shift(grads_two, 0), False)]
        pieces = finish(rows, extras, done, local, grads, spare)
        home[c] = [swap(piece, d) for d, piece in enumerate(pieces)]
        return pieces[0]

    all_flags = pass_on(0, hbm([packed[0]]))
    if per > 1:
        pass_on(1, hbm([ready[0]]))
    table = all_flags[:, 0, : 3 * rows].astype(jnp.int32)
    table = table.reshape(team, 3, rows)
    table = jnp.where(row == 0, table, table[:, :, ::-1])
    if span == 2:
        turned = table[:, ::-1]
        table = jnp.concatenate(
            [
                jnp.where(odd == 0, table[:rows], turned[:rows]),
                jnp.where(odd == 0, turned[rows:], table[rows:]),
            ]
        )
    if span == 1:
        windows = ((1, 0, 2),)
        extras = (0, 0)
    else:
        windows = ((3, 0, 1), (2, 1, 0))
        extras = (0, 1)
    spots = jnp.repeat(jnp.asarray(windows, jnp.int32), rows, axis=0)
    table = jnp.concatenate([table.reshape(team, 3 * rows), spots], axis=1)

    for c in every:
        inputs = []
        loads = []

        def add(value, held, wanted, slab_at, tiles):
            for at, (e, kind) in enumerate((e, kind) for e in tiles for kind in wanted):
                loads.append((len(inputs), at, kind, slab_at, e))
            inputs.append((value, held))

        for e in range(rows):
            add(mates[c][e], mates[c][2], "kvqg", 0, [e])
        for n in range(len(far)):
            piece = arrived[c, far[n]]
            add(hbm([piece])[0] if c == 0 else piece, 0, "kvqg", 1, [n])
        for n in range(2):
            add(halos[c][n], 0, "kv", span + n, range(rows))
        spare = [ready[c + 1]] if c < per - 1 else []
        if c == 0:
            spare = hbm(spare)
        if c >= 2:
            spare.append(finished(c - 2, [worked[c - 1][0]]))
        if c >= 3:
            spare += home[c - 3][1:]
        worked[c] = attend(rows, tile, span, table, tuple(loads), inputs, spare)
        if c + 2 < per:
            pass_on(c + 2, [])
    for c in every[-2:]:
        early = [k for k in (c - 2, c - 1) if k in home and (k == c - 2 or c == per - 1)]
        gone = [home[k][d] for k in early for d in (range(1, team) if k == c - 2 else far[:1])]
        finished(c, [worked[per - 1][0]] + gone)
    outs = None
    for c in every:
        outs = unpack(c, members, home[c], outs, queries.shape)
    attended, grad_queries, grad_keys, grad_values = outs
    return (attended, grad_queries, grad_keys, grad_values)


def solution(mesh):
    spec = P(("grp", "ctx", "sub"), None, "head")
    return jax.shard_map(
        body,
        mesh=mesh,
        in_specs=(spec, spec, spec, spec, P(("grp", "ctx", "sub"), None), P(("grp", "ctx", "sub"))),
        out_specs=(spec, spec, spec, spec),
        check_vma=False,
    )
```

```python
import functools
import math

import jax
import jax.numpy as jnp
from jax import lax
from jax.experimental import pallas as pl
from jax.experimental.pallas import tpu as pltpu
from jax.sharding import PartitionSpec as P

HD = 128
FLAG_ROWS = 16
BLOCKS = 4
RING = ("ctx", "sub")
F32 = jnp.float32
BF16 = jnp.bfloat16
SCALE = 1.0 / math.sqrt(HD)
FACTOR = SCALE * math.log2(math.e)
ANY = pl.BlockSpec(memory_space=pl.ANY)
SMEM = pl.BlockSpec(memory_space=pltpu.SMEM)
PARAMS = pltpu.CompilerParams(vmem_limit_bytes=36 * 1024 * 1024)
LIGHT = pltpu.CompilerParams(vmem_limit_bytes=20 * 1024 * 1024)


def struct(shape, dtype):
    return jax.ShapeDtypeStruct(shape, dtype)


def hbm(values):
    return [pltpu.with_memory_space_constraint(value, pltpu.HBM) for value in values]


def moved(nbytes):
    return pl.CostEstimate(flops=0, bytes_accessed=nbytes, transcendentals=0)


def pack_kernel(jobs, step, first, places_ref, flags_ref, *refs):
    sources, outs = refs[:4], refs[-len(jobs) :]
    lane = lax.broadcasted_iota(jnp.int32, (FLAG_ROWS, HD), 1)
    flags = jnp.zeros((FLAG_ROWS, HD), F32)
    for w in range(flags_ref.shape[0]):
        flags = jnp.where(lane == w, flags_ref[w].astype(F32), flags)
    flags = flags.astype(BF16)
    team = places_ref.shape[0]
    for out, (d, heads, kinds, flagged) in zip(outs, jobs):
        for m, c in enumerate(heads):
            lanes = pl.ds(pl.multiple_of(((c - first) * team + places_ref[d]) * HD, HD), HD)
            for at, n in enumerate(kinds):
                out[m, 0, pl.ds(at * step, step)] = sources[n][0, :, lanes]
            if flagged:
                out[m, 0, pl.ds(len(kinds) * step, FLAG_ROWS)] = flags


def pack(jobs, heads, places, flags, sources, spare, kept=jax.ShapeDtypeStruct):
    _, tile, lane_width = sources[0].shape
    step = tile // BLOCKS
    team = places.shape[0]
    first = heads[0]
    count = len(heads)
    wide = count * team * HD if first % count == 0 else lane_width
    block = first // count if first % count == 0 else 0
    start = first if first % count == 0 else 0
    shapes = [
        (len(held), BLOCKS, len(kinds) * step + (FLAG_ROWS if flagged else 0), HD)
        for _, held, kinds, flagged in jobs
    ]
    return pl.pallas_call(
        functools.partial(pack_kernel, jobs, step, start),
        grid=(BLOCKS,),
        out_shape=[kept(shape, BF16) for shape in shapes],
        in_specs=[SMEM, SMEM]
        + [pl.BlockSpec((1, step, wide), lambda i: (0, i, block))] * 4
        + [ANY] * len(spare),
        out_specs=[
            pl.BlockSpec((shape[0], 1, shape[2], HD), lambda i: (0, i, 0, 0)) for shape in shapes
        ],
        cost_estimate=moved(sum(4 * HD * math.prod(shape[:3]) for shape in shapes)),
        compiler_params=LIGHT,
        name="pack",
    )(places, flags, *hbm(sources), *spare)


def relay_kernel(step, rows, near, far, grads, outs):
    for out, pieces, grad in zip(outs, (near, far), grads):
        for e, (piece, at) in enumerate(pieces):
            out[0, :, pl.ds(2 * step * e, 2 * step)] = piece[at, :, pl.ds(0, 2 * step)]
        if grad is not None:
            for e in range(rows):
                for n in range(2):
                    for g in range(BLOCKS):
                        at = pl.ds((2 * rows + 2 * e + n) * step, step)
                        out[0, g, at] = grad[e, n, pl.ds(g * step, step)]


def relay(step, held, near, far, grads, spare, flagged=False, kept=jax.ShapeDtypeStruct):
    rows = len(near)
    kinds = 2 if far else 1
    high = (4 if grads else 2) * rows * step
    flag_sources = [*near, *far] if flagged else []

    def kernel(*refs):
        refs = list(refs)
        near_refs = [(refs.pop(0), 0) for _ in range(rows)]
        far_refs = [(refs.pop(0), 0) for _ in far]
        grad_refs = [refs.pop(0) for _ in grads] or [None] * kinds
        flag_refs = [refs.pop(0) for _ in flag_sources]
        outs = refs[len(spare) :]
        relay_kernel(step, rows, near_refs, far_refs, grad_refs, outs[:kinds])
        for d, ref in enumerate(flag_refs):
            outs[kinds][d] = ref[0, 0]

    def whole(shape):
        return pl.BlockSpec(shape, lambda i: (0,) * len(shape))

    shape = (1, BLOCKS, high, HD)
    return pl.pallas_call(
        kernel,
        grid=(1,),
        out_shape=[kept(shape, BF16)] * kinds
        + ([struct((len(flag_sources), FLAG_ROWS, HD), BF16)] if flagged else []),
        in_specs=[
            pl.BlockSpec((1, BLOCKS, 2 * step, HD), lambda i, at=at: (at, 0, 0, 0))
            for at in [held] * rows + [0] * len(far)
        ]
        + [whole(value.shape) for value in grads]
        + [
            pl.BlockSpec(
                (1, 1, FLAG_ROWS, HD),
                lambda i, at=value.shape[2] // FLAG_ROWS - 1: (0, 0, at, 0),
            )
            for value in flag_sources
        ]
        + [ANY] * len(spare),
        out_specs=[whole(shape)] * kinds
        + ([whole((len(flag_sources), FLAG_ROWS, HD))] if flagged else []),
        cost_estimate=moved(kinds * 4 * BLOCKS * high * HD),
        compiler_params=LIGHT,
        name="relay",
    )(*near, *far, *grads, *flag_sources, *spare)


def nt(a, b):
    return lax.dot_general(a, b, (((1,), (1,)), ((), ())), preferred_element_type=F32)


def nn(a, b):
    return jnp.dot(a, b, preferred_element_type=F32)


def attend_kernel(plan, rows, tile, table_ref, *refs):
    loads, slabs_here, n_in, spare = plan
    inputs = refs[:n_in]
    rest = refs[n_in + spare :]
    done, local, grads_one, grads_two = rest[:4]
    qbuf, gbuf, kbuf, vbuf, kt, vt, dk_t, dv_t, s_buf, p_buf, ds_buf, ot = rest[4:]
    targets = {"k": kbuf, "v": vbuf, "q": qbuf, "g": gbuf}
    step = tile // BLOCKS

    def load(g, carry):
        for n, at, kind, slab, e in loads:
            to = pl.ds(pl.multiple_of(e * tile + g * step, step), step)
            targets[kind][slab, to] = inputs[n][0, g, pl.ds(at * step, step)]
        return carry

    lax.fori_loop(0, BLOCKS, load, 0)
    width = rows * tile
    team = slabs_here * rows
    places = kbuf.shape[0]

    def prepare(n, carry):
        kt[n] = kbuf[n].T
        vt[n] = vbuf[n].T
        dk_t[n] = jnp.zeros((HD, width), F32)
        dv_t[n] = jnp.zeros((HD, width), F32)
        return carry

    lax.fori_loop(0, places, prepare, 0)
    lane = lax.broadcasted_iota(jnp.int32, (1, width), 1)

    queries = [qbuf[a] for a in range(slabs_here)]
    grads_in = [gbuf[a] for a in range(slabs_here)]
    late = {}

    def spot(a, b):
        return table_ref[a * rows, 3 * rows + b]

    def by_query(a, b, e, seen, unseen):
        keep = jnp.zeros((1, width), jnp.int32)
        for f in range(rows):
            inside = (lane >= f * tile) & (lane < (f + 1) * tile)
            keep = jnp.where(inside, table_ref[a * rows + f, b * rows + e], keep)
        return jnp.where(keep > 0, seen, unseen)

    def scores(a, b, top):
        for e in range(rows):
            at = pl.ds(e * tile, tile)
            s = nt(kbuf[spot(a, b), at], queries[a])
            s_buf[a, b, at] = s
            best = jnp.max(s, axis=0, keepdims=True)
            top = jnp.maximum(top, by_query(a, b, e, best, -jnp.inf))
        return top

    def expo(a, b, top, total):
        for e in range(rows):
            at = pl.ds(e * tile, tile)
            p = jnp.exp2((s_buf[a, b, at] - by_query(a, b, e, top, jnp.inf)) * FACTOR)
            total = total + jnp.sum(p, axis=0, keepdims=True)
            p_buf[a, b, at] = p.astype(BF16)
        ot[a] += nn(vt[spot(a, b)], p_buf[a, b])
        return total

    def between(a, total):
        inv = 1.0 / total
        low_t = (ot[a] * inv).astype(BF16)
        grad_t = grads_in[a].T.astype(F32)
        offset = jnp.sum(grad_t * low_t.astype(F32), axis=0, keepdims=True)
        grad_over = (grad_t * inv).astype(BF16)
        query_over = (queries[a].T.astype(F32) * (inv * SCALE)).astype(BF16)
        out = low_t.T
        for f in range(rows):
            done[a * rows + f, 0] = out[f * tile : (f + 1) * tile]
        ot[a] = jnp.zeros((HD, width), F32)
        late[a] = (inv, offset, grad_over, query_over)

    def backward(a, b):
        _, offset, grad_over, query_over = late[a]
        place = spot(a, b)
        for e in range(rows):
            at = pl.ds(e * tile, tile)
            dp = nt(vbuf[place, at], grads_in[a])
            ds_buf[at] = p_buf[a, b, at] * (dp - offset).astype(BF16)
        dv_t[place] += nt(grad_over, p_buf[a, b])
        dk_t[place] += nt(query_over, ds_buf[...])
        ot[a] += nn(kt[place], ds_buf[...])

    def after(a):
        dq = (ot[a] * (late[a][0] * SCALE)).astype(BF16).T
        for f in range(rows):
            done[a * rows + f, 1] = dq[f * tile : (f + 1) * tile]

    tops = [jnp.full((1, width), -jnp.inf, F32) for _ in range(slabs_here)]
    totals = [jnp.zeros((1, width), F32) for _ in range(slabs_here)]
    for a in range(slabs_here):
        ot[a] = jnp.zeros((HD, width), F32)
    for turn in range(slabs_here + 2):
        here = [a for a in range(slabs_here) if 0 <= turn - a <= 2]

        def blocks(b, carry, turn=turn, here=here):
            tops, totals = list(carry[0]), list(carry[1])
            for a in here:
                if turn - a == 0:
                    tops[a] = scores(a, b, tops[a])
                elif turn - a == 1:
                    totals[a] = expo(a, b, tops[a], totals[a])
                else:
                    backward(a, b)
            return tuple(tops), tuple(totals)

        carry = (tuple(tops), tuple(totals))
        if turn in (0, 3):
            for b in range(3):
                carry = blocks(b, carry)
        else:
            carry = lax.fori_loop(0, 3, blocks, carry)
        tops, totals = carry
        for a in here:
            if turn - a == 1:
                between(a, totals[a])
            elif turn - a == 2:
                after(a)

    def give(e, carry):
        at = pl.ds(pl.multiple_of(e * tile, tile), tile)
        for n, sums in enumerate((dk_t, dv_t)):
            for a in range(slabs_here):
                local[a * rows + e, n] = sums[a, :, at].T
            for m, grads in enumerate((grads_one, grads_two)):
                grads[e, n] = sums[slabs_here + m, :, at].astype(BF16).T
        return carry

    lax.fori_loop(0, rows, give, 0)


def attend(rows, tile, slabs_here, table, loads, inputs, spare):
    places = slabs_here + 2
    team = slabs_here * rows
    width = rows * tile
    scores = 3 * slabs_here * width * width

    def head_spec(value, c):
        shape = (1,) + value.shape[1:]
        return pl.BlockSpec(shape, lambda i: (c, 0, 0, 0), pipeline_mode=pl.Buffered(1))

    def whole(shape):
        return pl.BlockSpec(shape, lambda i: (0,) * len(shape), pipeline_mode=pl.Buffered(1))

    shapes = [
        struct((team, 2, tile, HD), BF16),
        struct((team, 2, tile, HD), F32),
        struct((rows, 2, tile, HD), BF16),
        struct((rows, 2, tile, HD), BF16),
    ]
    plan = (loads, slabs_here, len(inputs), len(spare))
    return pl.pallas_call(
        functools.partial(attend_kernel, plan, rows, tile),
        grid=(1,),
        out_shape=shapes,
        in_specs=[SMEM] + [head_spec(value, c) for value, c in inputs] + [ANY] * len(spare),
        out_specs=[whole(shape.shape) for shape in shapes],
        scratch_shapes=[
            pltpu.VMEM((slabs_here, width, HD), BF16),
            pltpu.VMEM((slabs_here, width, HD), BF16),
            pltpu.VMEM((places, width, HD), BF16),
            pltpu.VMEM((places, width, HD), BF16),
            pltpu.VMEM((places, HD, width), BF16),
            pltpu.VMEM((places, HD, width), BF16),
            pltpu.VMEM((places, HD, width), F32),
            pltpu.VMEM((places, HD, width), F32),
            pltpu.VMEM((slabs_here, 3, width, width), F32),
            pltpu.VMEM((slabs_here, 3, width, width), BF16),
            pltpu.VMEM((width, width), BF16),
            pltpu.VMEM((slabs_here, HD, width), F32),
        ],
        cost_estimate=pl.CostEstimate(
            flops=12 * scores * HD, bytes_accessed=8 * 1024 * 1024, transcendentals=scores
        ),
        compiler_params=PARAMS,
        name="attend",
    )(table, *[value for value, _ in inputs], *spare)


def finish(rows, extras, dones, local, grads, spare):
    team, _, tile, _ = local.shape
    step = tile // BLOCKS
    ahead = 2 * len(dones)

    def kernel(*refs):
        ready, local = refs[: len(dones)], refs[len(dones)]
        terms, outs = refs[len(dones) + 1 : len(dones) + 1 + len(grads)], refs[-team:]
        for d in range(team):
            out = outs[d].at[0]
            for n in range(2):
                for m, done in enumerate(ready):
                    out[2 * m + n] = done[d, n]
                for g in range(BLOCKS):
                    at = pl.ds(g * step, step)
                    total = local[d, n, at]
                    for term, (_, packed), slab in zip(terms, grads, extras):
                        if d // rows != slab:
                            continue
                        if packed:
                            row = pl.ds((2 * (d % rows) + n) * step, step)
                            total = total + term[0, g, row].astype(F32)
                        else:
                            total = total + term[d % rows, n, at].astype(F32)
                    out[ahead + n, at] = total.astype(BF16)

    def whole(shape):
        return pl.BlockSpec(shape, lambda i: (0,) * len(shape))

    def grad_spec(value, packed):
        if not packed:
            return whole(value.shape)
        return pl.BlockSpec((1, BLOCKS, 2 * rows * step, HD), lambda i: (0, 0, 1, 0))

    piece = (1, ahead + 2, tile, HD)
    return pl.pallas_call(
        kernel,
        grid=(1,),
        out_shape=[struct(piece, BF16)] * team,
        in_specs=[whole(done.shape) for done in dones]
        + [whole(local.shape)]
        + [grad_spec(*grad) for grad in grads]
        + [ANY] * len(spare),
        out_specs=[whole(piece)] * team,
        cost_estimate=moved(team * (16 + 4 * ahead) * tile * HD),
        compiler_params=LIGHT,
        name="finish",
    )(*dones, local, *[value for value, _ in grads], *spare)


def unpack(c, places, pairs, outs, shape):
    tile = shape[1]
    step = tile // BLOCKS
    team = places.shape[0]
    held = [] if outs is None else list(outs)
    pieces = [*pairs[0], *pairs[1]]

    def kernel(places_ref, *refs):
        for d in range(team):
            lanes = pl.ds(pl.multiple_of(places_ref[d] * HD, HD), HD)
            for n in range(4):
                refs[n - 4][0, :, lanes] = refs[n // 2 * team + d][0, n % 2]

    return pl.pallas_call(
        kernel,
        grid=(BLOCKS,),
        out_shape=[struct(shape, BF16)] * 4,
        in_specs=[SMEM]
        + [pl.BlockSpec((1, 2, step, HD), lambda i, at=at: (0, at, i, 0)) for _, at in pieces]
        + [ANY] * len(held),
        out_specs=[pl.BlockSpec((1, step, team * HD), lambda i: (0, i, c))] * 4,
        input_output_aliases={1 + len(pieces) + n: n for n in range(len(held))},
        cost_estimate=moved(16 * tile * team * HD),
        compiler_params=LIGHT,
        name="unpack",
    )(places, *[value for value, _ in pieces], *held)


def body(queries, keys, values, grad_out, window_tiles, window_count):
    rows_here, tile, lane_width = queries.shape
    wmax = window_tiles.shape[1]
    heads = lane_width // HD
    rows = lax.axis_size("sub")
    slabs = lax.axis_size("ctx")
    span = 2 if heads % (2 * rows) == 0 and slabs % 2 == 0 else 1
    team = span * rows
    per = heads // team
    size = slabs * rows
    slab = lax.axis_index("ctx")
    row = lax.axis_index("sub")
    odd = slab % span
    me = odd * rows + row

    def swap(value, d):
        if d == 0:
            return value
        return lax.ppermute(value, RING, [(i, i - i % team + (i % team ^ d)) for i in range(size)])

    def shift(value, way, flip=0):
        pairs = []
        for i in range(size):
            place = i % team // rows
            forward = (place == span - 1) if way == 0 else (place == 0)
            if span == 1:
                forward = way == 0
            j = i + team if forward else i - team
            if 0 <= j < size:
                pairs.append((i, j ^ flip))
        return lax.ppermute(value, RING, pairs)

    places = (window_tiles[0] // rows - slab + 1) * rows + window_tiles[0] % rows
    listed = jnp.arange(wmax) < window_count[0]
    flags = jnp.any(
        (places[None, :] == jnp.arange(3 * rows)[:, None]) & listed[None, :], axis=1
    ).astype(jnp.int32)

    members = jnp.arange(team, dtype=jnp.int32) ^ me
    sources = (keys, values, queries, grad_out)
    kinds = (0, 1, 2, 3)
    every = tuple(range(per))
    far = tuple(range(rows, team))
    step = tile // BLOCKS

    jobs = [(d, (0,), kinds, True) for d in (*far, 1, 0)]
    packed = pack(jobs, (0,), members, flags, sources, [])
    count = len(far)
    mates = {0: (packed[-1], swap(packed[-2], 1), 0)}
    sent = {(0, d): packed[n] for n, d in enumerate(far)}
    rest = every[1:]
    if rest:
        jobs = [(d, (c,), kinds, False) for c in rest for d in far]
        jobs += [(1, rest, kinds, False), (0, rest, kinds, False)]
        packed = pack(jobs, rest, members, flags, sources, [mates[0][1]], pltpu.HBM)
        sent.update(
            {(c, d): packed[m * count + n] for m, c in enumerate(rest) for n, d in enumerate(far)}
        )
        beside = swap(packed[-2], 1)
        mates.update({c: (packed[-1], beside, m) for m, c in enumerate(rest)})

    arrived = {key: swap(value, key[1]) for key, value in sent.items()}
    halos = {}
    ready = {}
    worked = {}
    home = {}
    found = {}

    def pass_on(c, spare):
        pieces = [arrived[c, d] for d in far]
        if c == 0:
            pieces = hbm(pieces)
        kept = pltpu.HBM if c < 2 else jax.ShapeDtypeStruct
        grads = [worked[c - 2][3], worked[c - 2][2]] if c >= 2 else []
        outs = relay(step, mates[c][2], mates[c][:2], pieces, grads, spare, c == 0, kept)
        ready[c] = outs[0]
        halos[c] = (shift(outs[0], 0), shift(outs[span - 1], 1))
        return outs[-1]

    def finished(c, spare):
        _, local, grads_one, grads_two = worked[c]
        if c + 2 < per:
            grads = [(halos[c + 2][1], True), (halos[c + 2][0], True)]
        else:
            grads = [(shift(grads_one, 1), False), (shift(grads_two, 0), False)]
        heads_in = [0] if c == 0 else []
        heads_in += [c + 1] if c + 1 < per else []
        dones = [worked[k][0] for k in heads_in]
        pieces = finish(rows, extras, dones, local, grads, spare)
        for m, k in enumerate(heads_in):
            found[k] = (c, m)
        home[c] = [swap(piece, d) for d, piece in enumerate(pieces)]
        return pieces[0]

    all_flags = pass_on(0, hbm([packed[0]]))
    if per > 1:
        pass_on(1, hbm([ready[0]]))
    table = all_flags[:, 0, : 3 * rows].astype(jnp.int32)
    table = table.reshape(team, 3, rows)
    table = jnp.where(row == 0, table, table[:, :, ::-1])
    if span == 2:
        turned = table[:, ::-1]
        table = jnp.concatenate(
            [
                jnp.where(odd == 0, table[:rows], turned[:rows]),
                jnp.where(odd == 0, turned[rows:], table[rows:]),
            ]
        )
    if span == 1:
        windows = ((1, 0, 2),)
        extras = (0, 0)
    else:
        windows = ((3, 0, 1), (2, 1, 0))
        extras = (0, 1)
    spots = jnp.repeat(jnp.asarray(windows, jnp.int32), rows, axis=0)
    table = jnp.concatenate([table.reshape(team, 3 * rows), spots], axis=1)

    for c in every:
        inputs = []
        loads = []

        def add(value, held, wanted, slab_at, tiles):
            for at, (e, kind) in enumerate((e, kind) for e in tiles for kind in wanted):
                loads.append((len(inputs), at, kind, slab_at, e))
            inputs.append((value, held))

        for e in range(rows):
            add(mates[c][e], mates[c][2], "kvqg", 0, [e])
        for n in range(len(far)):
            piece = arrived[c, far[n]]
            add(hbm([piece])[0] if c == 0 else piece, 0, "kvqg", 1, [n])
        for n in range(2):
            add(halos[c][n], 0, "kv", span + n, range(rows))
        spare = [ready[c + 1]] if c < per - 1 else []
        if c == 0:
            spare = hbm(spare)
        if c >= 2:
            spare.append(finished(c - 2, []))
        if c >= 3:
            spare += home[c - 3][1:]
        worked[c] = attend(rows, tile, span, table, tuple(loads), inputs, spare)
        if c + 2 < per:
            pass_on(c + 2, [])
    for c in every[-2:]:
        early = [k for k in (c - 2, c - 1) if k in home and (k == c - 2 or c == per - 1)]
        gone = [home[k][d] for k in early for d in (range(1, team) if k == c - 2 else far[:1])]
        finished(c, gone)
    outs = None
    for c in every:
        held, at = found[c]
        last = home[c][0].shape[1] // 2 - 1
        pairs = ([(piece, at) for piece in home[held]], [(piece, last) for piece in home[c]])
        outs = unpack(c, members, pairs, outs, queries.shape)
    attended, grad_queries, grad_keys, grad_values = outs
    return (attended, grad_queries, grad_keys, grad_values)


def solution(mesh):
    spec = P(("grp", "ctx", "sub"), None, "head")
    return jax.shard_map(
        body,
        mesh=mesh,
        in_specs=(spec, spec, spec, spec, P(("grp", "ctx", "sub"), None), P(("grp", "ctx", "sub"))),
        out_specs=(spec, spec, spec, spec),
        check_vma=False,
    )
```

```python
import functools
import math

import jax
import jax.numpy as jnp
from jax import lax
from jax.experimental import pallas as pl
from jax.experimental.pallas import tpu as pltpu
from jax.sharding import PartitionSpec as P

HD = 128
FLAG_ROWS = 16
BLOCKS = 4
RING = ("ctx", "sub")
F32 = jnp.float32
BF16 = jnp.bfloat16
SCALE = 1.0 / math.sqrt(HD)
FACTOR = SCALE * math.log2(math.e)
ANY = pl.BlockSpec(memory_space=pl.ANY)
SMEM = pl.BlockSpec(memory_space=pltpu.SMEM)
PARAMS = pltpu.CompilerParams(vmem_limit_bytes=36 * 1024 * 1024)
LIGHT = pltpu.CompilerParams(vmem_limit_bytes=20 * 1024 * 1024)


def struct(shape, dtype):
    return jax.ShapeDtypeStruct(shape, dtype)


def hbm(values):
    return [pltpu.with_memory_space_constraint(value, pltpu.HBM) for value in values]


def moved(nbytes):
    return pl.CostEstimate(flops=0, bytes_accessed=nbytes, transcendentals=0)


def pack_kernel(jobs, step, first, places_ref, flags_ref, *refs):
    sources, outs = refs[:4], refs[-len(jobs) :]
    lane = lax.broadcasted_iota(jnp.int32, (FLAG_ROWS, HD), 1)
    flags = jnp.zeros((FLAG_ROWS, HD), F32)
    for w in range(flags_ref.shape[0]):
        flags = jnp.where(lane == w, flags_ref[w].astype(F32), flags)
    flags = flags.astype(BF16)
    team = places_ref.shape[0]
    for out, (d, heads, kinds, flagged) in zip(outs, jobs):
        for m, c in enumerate(heads):
            lanes = pl.ds(pl.multiple_of(((c - first) * team + places_ref[d]) * HD, HD), HD)
            for at, n in enumerate(kinds):
                out[m, 0, pl.ds(at * step, step)] = sources[n][0, :, lanes]
            if flagged:
                out[m, 0, pl.ds(len(kinds) * step, FLAG_ROWS)] = flags


def pack(jobs, heads, places, flags, sources, spare, kept=jax.ShapeDtypeStruct):
    _, tile, lane_width = sources[0].shape
    step = tile // BLOCKS
    team = places.shape[0]
    first = heads[0]
    count = len(heads)
    wide = count * team * HD if first % count == 0 else lane_width
    block = first // count if first % count == 0 else 0
    start = first if first % count == 0 else 0
    shapes = [
        (len(held), BLOCKS, len(kinds) * step + (FLAG_ROWS if flagged else 0), HD)
        for _, held, kinds, flagged in jobs
    ]
    return pl.pallas_call(
        functools.partial(pack_kernel, jobs, step, start),
        grid=(BLOCKS,),
        out_shape=[kept(shape, BF16) for shape in shapes],
        in_specs=[SMEM, SMEM]
        + [pl.BlockSpec((1, step, wide), lambda i: (0, i, block))] * 4
        + [ANY] * len(spare),
        out_specs=[
            pl.BlockSpec((shape[0], 1, shape[2], HD), lambda i: (0, i, 0, 0)) for shape in shapes
        ],
        cost_estimate=moved(sum(4 * HD * math.prod(shape[:3]) for shape in shapes)),
        compiler_params=LIGHT,
        name="pack",
    )(places, flags, *hbm(sources), *spare)


def relay_kernel(step, rows, near, far, grads, outs):
    for out, pieces, grad in zip(outs, (near, far), grads):
        for e, (piece, at) in enumerate(pieces):
            out[0, :, pl.ds(2 * step * e, 2 * step)] = piece[at, :, pl.ds(0, 2 * step)]
        if grad is not None:
            for e in range(rows):
                for n in range(2):
                    for g in range(BLOCKS):
                        at = pl.ds((2 * rows + 2 * e + n) * step, step)
                        out[0, g, at] = grad[e, n, pl.ds(g * step, step)]


def relay(step, held, near, far, grads, spare, flagged=False, kept=jax.ShapeDtypeStruct):
    rows = len(near)
    kinds = 2 if far else 1
    high = (4 if grads else 2) * rows * step
    flag_sources = [*near, *far] if flagged else []

    def kernel(*refs):
        refs = list(refs)
        near_refs = [(refs.pop(0), 0) for _ in range(rows)]
        far_refs = [(refs.pop(0), 0) for _ in far]
        grad_refs = [refs.pop(0) for _ in grads] or [None] * kinds
        flag_refs = [refs.pop(0) for _ in flag_sources]
        outs = refs[len(spare) :]
        relay_kernel(step, rows, near_refs, far_refs, grad_refs, outs[:kinds])
        for d, ref in enumerate(flag_refs):
            outs[kinds][d] = ref[0, 0]

    def whole(shape):
        return pl.BlockSpec(shape, lambda i: (0,) * len(shape))

    shape = (1, BLOCKS, high, HD)
    return pl.pallas_call(
        kernel,
        grid=(1,),
        out_shape=[kept(shape, BF16)] * kinds
        + ([struct((len(flag_sources), FLAG_ROWS, HD), BF16)] if flagged else []),
        in_specs=[
            pl.BlockSpec((1, BLOCKS, 2 * step, HD), lambda i, at=at: (at, 0, 0, 0))
            for at in [held] * rows + [0] * len(far)
        ]
        + [whole(value.shape) for value in grads]
        + [
            pl.BlockSpec(
                (1, 1, FLAG_ROWS, HD),
                lambda i, at=value.shape[2] // FLAG_ROWS - 1: (0, 0, at, 0),
            )
            for value in flag_sources
        ]
        + [ANY] * len(spare),
        out_specs=[whole(shape)] * kinds
        + ([whole((len(flag_sources), FLAG_ROWS, HD))] if flagged else []),
        cost_estimate=moved(kinds * 4 * BLOCKS * high * HD),
        compiler_params=LIGHT,
        name="relay",
    )(*near, *far, *grads, *flag_sources, *spare)


def nt(a, b):
    return lax.dot_general(a, b, (((1,), (1,)), ((), ())), preferred_element_type=F32)


def nn(a, b):
    return jnp.dot(a, b, preferred_element_type=F32)


def attend_kernel(plan, rows, tile, table_ref, *refs):
    loads, slabs_here, n_in, spare = plan
    inputs = refs[:n_in]
    rest = refs[n_in + spare :]
    done, local, grads_one, grads_two = rest[:4]
    qbuf, gbuf, kbuf, vbuf, kt, vt, dk_t, dv_t, s_buf, p_buf, ds_buf, ot = rest[4:]
    targets = {"k": kbuf, "v": vbuf, "q": qbuf, "g": gbuf}
    step = tile // BLOCKS

    def load(g, carry):
        for n, at, kind, slab, e in loads:
            to = pl.ds(pl.multiple_of(e * tile + g * step, step), step)
            targets[kind][slab, to] = inputs[n][0, g, pl.ds(at * step, step)]
        return carry

    lax.fori_loop(0, BLOCKS, load, 0)
    width = rows * tile
    team = slabs_here * rows
    places = kbuf.shape[0]

    def prepare(n, carry):
        kt[n] = kbuf[n].T
        vt[n] = vbuf[n].T
        dk_t[n] = jnp.zeros((HD, width), F32)
        dv_t[n] = jnp.zeros((HD, width), F32)
        return carry

    lax.fori_loop(0, places, prepare, 0)
    lane = lax.broadcasted_iota(jnp.int32, (1, width), 1)

    queries = [qbuf[a] for a in range(slabs_here)]
    grads_in = [gbuf[a] for a in range(slabs_here)]
    late = {}

    def spot(a, b):
        return table_ref[a * rows, 3 * rows + b]

    def by_query(a, b, e, seen, unseen):
        keep = jnp.zeros((1, width), jnp.int32)
        for f in range(rows):
            inside = (lane >= f * tile) & (lane < (f + 1) * tile)
            keep = jnp.where(inside, table_ref[a * rows + f, b * rows + e], keep)
        return jnp.where(keep > 0, seen, unseen)

    def scores(a, b, top):
        for e in range(rows):
            at = pl.ds(e * tile, tile)
            s = nt(kbuf[spot(a, b), at], queries[a])
            s_buf[a, b, at] = s
            best = jnp.max(s, axis=0, keepdims=True)
            top = jnp.maximum(top, by_query(a, b, e, best, -jnp.inf))
        return top

    def expo(a, b, top, total):
        for e in range(rows):
            at = pl.ds(e * tile, tile)
            p = jnp.exp2((s_buf[a, b, at] - by_query(a, b, e, top, jnp.inf)) * FACTOR)
            total = total + jnp.sum(p, axis=0, keepdims=True)
            p_buf[a, b, at] = p.astype(BF16)
        ot[a] += nn(vt[spot(a, b)], p_buf[a, b])
        return total

    def between(a, total):
        inv = 1.0 / total
        low_t = (ot[a] * inv).astype(BF16)
        grad_t = grads_in[a].T.astype(F32)
        offset = jnp.sum(grad_t * low_t.astype(F32), axis=0, keepdims=True)
        grad_over = (grad_t * inv).astype(BF16)
        query_over = (queries[a].T.astype(F32) * (inv * SCALE)).astype(BF16)
        out = low_t.T
        for f in range(rows):
            done[a * rows + f, 0] = out[f * tile : (f + 1) * tile]
        ot[a] = jnp.zeros((HD, width), F32)
        late[a] = (inv, offset, grad_over, query_over)

    def backward(a, b):
        _, offset, grad_over, query_over = late[a]
        place = spot(a, b)
        for e in range(rows):
            at = pl.ds(e * tile, tile)
            dp = nt(vbuf[place, at], grads_in[a])
            ds_buf[at] = p_buf[a, b, at] * (dp - offset).astype(BF16)
        dv_t[place] += nt(grad_over, p_buf[a, b])
        dk_t[place] += nt(query_over, ds_buf[...])
        ot[a] += nn(kt[place], ds_buf[...])

    def after(a):
        dq = (ot[a] * (late[a][0] * SCALE)).astype(BF16).T
        for f in range(rows):
            done[a * rows + f, 1] = dq[f * tile : (f + 1) * tile]

    tops = [jnp.full((1, width), -jnp.inf, F32) for _ in range(slabs_here)]
    totals = [jnp.zeros((1, width), F32) for _ in range(slabs_here)]
    for a in range(slabs_here):
        ot[a] = jnp.zeros((HD, width), F32)
    for turn in range(slabs_here + 2):
        here = [a for a in range(slabs_here) if 0 <= turn - a <= 2]

        def blocks(b, carry, turn=turn, here=here):
            tops, totals = list(carry[0]), list(carry[1])
            for a in here:
                if turn - a == 0:
                    tops[a] = scores(a, b, tops[a])
                elif turn - a == 1:
                    totals[a] = expo(a, b, tops[a], totals[a])
                else:
                    backward(a, b)
            return tuple(tops), tuple(totals)

        carry = (tuple(tops), tuple(totals))
        if turn in (2,):
            for b in range(3):
                carry = blocks(b, carry)
        else:
            carry = lax.fori_loop(0, 3, blocks, carry)
        tops, totals = carry
        for a in here:
            if turn - a == 1:
                between(a, totals[a])
            elif turn - a == 2:
                after(a)

    def give(e, carry):
        at = pl.ds(pl.multiple_of(e * tile, tile), tile)
        for n, sums in enumerate((dk_t, dv_t)):
            for a in range(slabs_here):
                local[a * rows + e, n] = sums[a, :, at].T
            for m, grads in enumerate((grads_one, grads_two)):
                grads[e, n] = sums[slabs_here + m, :, at].astype(BF16).T
        return carry

    lax.fori_loop(0, rows, give, 0)


def attend(rows, tile, slabs_here, table, loads, inputs, spare):
    places = slabs_here + 2
    team = slabs_here * rows
    width = rows * tile
    scores = 3 * slabs_here * width * width

    def head_spec(value, c):
        shape = (1,) + value.shape[1:]
        return pl.BlockSpec(shape, lambda i: (c, 0, 0, 0), pipeline_mode=pl.Buffered(1))

    def whole(shape):
        return pl.BlockSpec(shape, lambda i: (0,) * len(shape), pipeline_mode=pl.Buffered(1))

    shapes = [
        struct((team, 2, tile, HD), BF16),
        struct((team, 2, tile, HD), F32),
        struct((rows, 2, tile, HD), BF16),
        struct((rows, 2, tile, HD), BF16),
    ]
    plan = (loads, slabs_here, len(inputs), len(spare))
    return pl.pallas_call(
        functools.partial(attend_kernel, plan, rows, tile),
        grid=(1,),
        out_shape=shapes,
        in_specs=[SMEM] + [head_spec(value, c) for value, c in inputs] + [ANY] * len(spare),
        out_specs=[whole(shape.shape) for shape in shapes],
        scratch_shapes=[
            pltpu.VMEM((slabs_here, width, HD), BF16),
            pltpu.VMEM((slabs_here, width, HD), BF16),
            pltpu.VMEM((places, width, HD), BF16),
            pltpu.VMEM((places, width, HD), BF16),
            pltpu.VMEM((places, HD, width), BF16),
            pltpu.VMEM((places, HD, width), BF16),
            pltpu.VMEM((places, HD, width), F32),
            pltpu.VMEM((places, HD, width), F32),
            pltpu.VMEM((slabs_here, 3, width, width), F32),
            pltpu.VMEM((slabs_here, 3, width, width), BF16),
            pltpu.VMEM((width, width), BF16),
            pltpu.VMEM((slabs_here, HD, width), F32),
        ],
        cost_estimate=pl.CostEstimate(
            flops=12 * scores * HD, bytes_accessed=8 * 1024 * 1024, transcendentals=scores
        ),
        compiler_params=PARAMS,
        name="attend",
    )(table, *[value for value, _ in inputs], *spare)


def finish(rows, extras, dones, local, grads, spare):
    team, _, tile, _ = local.shape
    step = tile // BLOCKS
    ahead = 2 * len(dones)

    def kernel(*refs):
        ready, local = refs[: len(dones)], refs[len(dones)]
        terms, outs = refs[len(dones) + 1 : len(dones) + 1 + len(grads)], refs[-team:]
        for d in range(team):
            out = outs[d].at[0]
            for n in range(2):
                for m, done in enumerate(ready):
                    out[2 * m + n] = done[d, n]
                for g in range(BLOCKS):
                    at = pl.ds(g * step, step)
                    total = local[d, n, at]
                    for term, (_, packed), slab in zip(terms, grads, extras):
                        if d // rows != slab:
                            continue
                        if packed:
                            row = pl.ds((2 * (d % rows) + n) * step, step)
                            total = total + term[0, g, row].astype(F32)
                        else:
                            total = total + term[d % rows, n, at].astype(F32)
                    out[ahead + n, at] = total.astype(BF16)

    def whole(shape):
        return pl.BlockSpec(shape, lambda i: (0,) * len(shape))

    def grad_spec(value, packed):
        if not packed:
            return whole(value.shape)
        return pl.BlockSpec((1, BLOCKS, 2 * rows * step, HD), lambda i: (0, 0, 1, 0))

    piece = (1, ahead + 2, tile, HD)
    return pl.pallas_call(
        kernel,
        grid=(1,),
        out_shape=[struct(piece, BF16)] * team,
        in_specs=[whole(done.shape) for done in dones]
        + [whole(local.shape)]
        + [grad_spec(*grad) for grad in grads]
        + [ANY] * len(spare),
        out_specs=[whole(piece)] * team,
        cost_estimate=moved(team * (16 + 4 * ahead) * tile * HD),
        compiler_params=LIGHT,
        name="finish",
    )(*dones, local, *[value for value, _ in grads], *spare)


def unpack(c, places, pairs, outs, shape):
    tile = shape[1]
    step = tile // BLOCKS
    team = places.shape[0]
    held = [] if outs is None else list(outs)
    pieces = [*pairs[0], *pairs[1]]

    def kernel(places_ref, *refs):
        for d in range(team):
            lanes = pl.ds(pl.multiple_of(places_ref[d] * HD, HD), HD)
            for n in range(4):
                refs[n - 4][0, :, lanes] = refs[n // 2 * team + d][0, n % 2]

    return pl.pallas_call(
        kernel,
        grid=(BLOCKS,),
        out_shape=[struct(shape, BF16)] * 4,
        in_specs=[SMEM]
        + [pl.BlockSpec((1, 2, step, HD), lambda i, at=at: (0, at, i, 0)) for _, at in pieces]
        + [ANY] * len(held),
        out_specs=[pl.BlockSpec((1, step, team * HD), lambda i: (0, i, c))] * 4,
        input_output_aliases={1 + len(pieces) + n: n for n in range(len(held))},
        cost_estimate=moved(16 * tile * team * HD),
        compiler_params=LIGHT,
        name="unpack",
    )(places, *[value for value, _ in pieces], *held)


def body(queries, keys, values, grad_out, window_tiles, window_count):
    rows_here, tile, lane_width = queries.shape
    wmax = window_tiles.shape[1]
    heads = lane_width // HD
    rows = lax.axis_size("sub")
    slabs = lax.axis_size("ctx")
    span = 2 if heads % (2 * rows) == 0 and slabs % 2 == 0 else 1
    team = span * rows
    per = heads // team
    size = slabs * rows
    slab = lax.axis_index("ctx")
    row = lax.axis_index("sub")
    odd = slab % span
    me = odd * rows + row

    def swap(value, d):
        if d == 0:
            return value
        return lax.ppermute(value, RING, [(i, i - i % team + (i % team ^ d)) for i in range(size)])

    def shift(value, way, flip=0):
        pairs = []
        for i in range(size):
            place = i % team // rows
            forward = (place == span - 1) if way == 0 else (place == 0)
            if span == 1:
                forward = way == 0
            j = i + team if forward else i - team
            if 0 <= j < size:
                pairs.append((i, j ^ flip))
        return lax.ppermute(value, RING, pairs)

    places = (window_tiles[0] // rows - slab + 1) * rows + window_tiles[0] % rows
    listed = jnp.arange(wmax) < window_count[0]
    flags = jnp.any(
        (places[None, :] == jnp.arange(3 * rows)[:, None]) & listed[None, :], axis=1
    ).astype(jnp.int32)

    members = jnp.arange(team, dtype=jnp.int32) ^ me
    sources = (keys, values, queries, grad_out)
    kinds = (0, 1, 2, 3)
    every = tuple(range(per))
    far = tuple(range(rows, team))
    step = tile // BLOCKS

    jobs = [(d, (0,), kinds, True) for d in (*far, 1, 0)]
    packed = pack(jobs, (0,), members, flags, sources, [])
    count = len(far)
    mates = {0: (packed[-1], swap(packed[-2], 1), 0)}
    sent = {(0, d): packed[n] for n, d in enumerate(far)}
    rest = every[1:]
    if rest:
        jobs = [(d, (c,), kinds, False) for c in rest for d in far]
        jobs += [(1, rest, kinds, False), (0, rest, kinds, False)]
        packed = pack(jobs, rest, members, flags, sources, [mates[0][1]], pltpu.HBM)
        sent.update(
            {(c, d): packed[m * count + n] for m, c in enumerate(rest) for n, d in enumerate(far)}
        )
        beside = swap(packed[-2], 1)
        mates.update({c: (packed[-1], beside, m) for m, c in enumerate(rest)})

    arrived = {key: swap(value, key[1]) for key, value in sent.items()}
    halos = {}
    ready = {}
    worked = {}
    home = {}
    found = {}

    def pass_on(c, spare):
        pieces = [arrived[c, d] for d in far]
        if c == 0:
            pieces = hbm(pieces)
        kept = pltpu.HBM if c < 2 else jax.ShapeDtypeStruct
        grads = [worked[c - 2][3], worked[c - 2][2]] if c >= 2 else []
        outs = relay(step, mates[c][2], mates[c][:2], pieces, grads, spare, c == 0, kept)
        ready[c] = outs[0]
        halos[c] = (shift(outs[0], 0), shift(outs[span - 1], 1))
        return outs[-1]

    def finished(c, spare):
        _, local, grads_one, grads_two = worked[c]
        if c + 2 < per:
            grads = [(halos[c + 2][1], True), (halos[c + 2][0], True)]
        else:
            grads = [(shift(grads_one, 1), False), (shift(grads_two, 0), False)]
        heads_in = [0] if c == 0 else []
        heads_in += [c + 1] if c + 1 < per else []
        dones = [worked[k][0] for k in heads_in]
        pieces = finish(rows, extras, dones, local, grads, spare)
        for m, k in enumerate(heads_in):
            found[k] = (c, m)
        home[c] = [swap(piece, d) for d, piece in enumerate(pieces)]
        return pieces[0]

    all_flags = pass_on(0, hbm([packed[0]]))
    if per > 1:
        pass_on(1, hbm([ready[0]]))
    table = all_flags[:, 0, : 3 * rows].astype(jnp.int32)
    table = table.reshape(team, 3, rows)
    table = jnp.where(row == 0, table, table[:, :, ::-1])
    if span == 2:
        turned = table[:, ::-1]
        table = jnp.concatenate(
            [
                jnp.where(odd == 0, table[:rows], turned[:rows]),
                jnp.where(odd == 0, turned[rows:], table[rows:]),
            ]
        )
    if span == 1:
        windows = ((1, 0, 2),)
        extras = (0, 0)
    else:
        windows = ((3, 0, 1), (2, 1, 0))
        extras = (0, 1)
    spots = jnp.repeat(jnp.asarray(windows, jnp.int32), rows, axis=0)
    table = jnp.concatenate([table.reshape(team, 3 * rows), spots], axis=1)

    for c in every:
        inputs = []
        loads = []

        def add(value, held, wanted, slab_at, tiles):
            for at, (e, kind) in enumerate((e, kind) for e in tiles for kind in wanted):
                loads.append((len(inputs), at, kind, slab_at, e))
            inputs.append((value, held))

        for e in range(rows):
            add(mates[c][e], mates[c][2], "kvqg", 0, [e])
        for n in range(len(far)):
            piece = arrived[c, far[n]]
            add(hbm([piece])[0] if c == 0 else piece, 0, "kvqg", 1, [n])
        for n in range(2):
            add(halos[c][n], 0, "kv", span + n, range(rows))
        spare = [ready[c + 1]] if c < per - 1 else []
        if c == 0:
            spare = hbm(spare)
        if c >= 2:
            spare.append(finished(c - 2, []))
        if c >= 3:
            spare += home[c - 3][1:]
        worked[c] = attend(rows, tile, span, table, tuple(loads), inputs, spare)
        if c + 2 < per:
            pass_on(c + 2, [])
    for c in every[-2:]:
        early = [k for k in (c - 2, c - 1) if k in home and (k == c - 2 or c == per - 1)]
        gone = [home[k][d] for k in early for d in (range(1, team) if k == c - 2 else far[:1])]
        finished(c, gone)
    outs = None
    for c in every:
        held, at = found[c]
        last = home[c][0].shape[1] // 2 - 1
        pairs = ([(piece, at) for piece in home[held]], [(piece, last) for piece in home[c]])
        outs = unpack(c, members, pairs, outs, queries.shape)
    attended, grad_queries, grad_keys, grad_values = outs
    return (attended, grad_queries, grad_keys, grad_values)


def solution(mesh):
    spec = P(("grp", "ctx", "sub"), None, "head")
    return jax.shard_map(
        body,
        mesh=mesh,
        in_specs=(spec, spec, spec, spec, P(("grp", "ctx", "sub"), None), P(("grp", "ctx", "sub"))),
        out_specs=(spec, spec, spec, spec),
        check_vma=False,
    )
```
